32 devices in a mesh: row: 8 (over z, y), col: 4 (over x, core).
Axes of the slice: x: 2, y: 2, z: 4, core: 2. Of those that a mesh axis runs over, the one named last changes fastest.
Arguments:
- a_blocks: bfloat16 [512, 4, 128, 128], P('row', 'col'), may hold values from -4 to 4
- p_tiles: bfloat16 [512, 128, 128], P(('row', 'col')), may hold values from -0.5 to 0.5
- owner: int32 [512, 1], P('row'), may hold values from 0 to 7; in each aligned block of 64 rows (0 to 63, 64 to 127, ...) at most 16 rows name the same one
- agg_local: int32 [512], P('row'), may hold values from 0 to 1
- a_cols: int32 [512, 4], P('row', 'col'), may hold values from 0 to 511, as said below
Outputs:
- coarse: float32 [16, 16, 128, 128], P('row', 'col')
The draws below stay inside these ranges and needn't reach their ends.
Inputs may be any that keep to these rules, and one draw needn't show every extreme that they name: Column c of a_cols names a tile g with (g // 16) % 4 == c. Among the 64 tiles of one row slab at most 16 name the same owner, and in every draw some owner is named exactly 16 times by some slab.
All inputs are finite; a program needn't handle non-finite values.
Results may differ from the reference program's by a relative error of at most 0.0029.
Values may be sent and summed in bfloat16 or wider, within the bound.
No kernel may reach another device: no remote copies, remote signals or barrier semaphores. Data moves between devices by JAX's collectives and lax.ppermute only.
A program may use at most 192 MiB of HBM per device.

```python
import math
import jax
import jax.numpy as jnp
import numpy as np
from jax import lax

B = 128
FTD = 16
OWN = 2
FTR = 64
TILES = 512
CAP = 16
NAGG = 16
N_ROW = 8
N_COL = 4


def draw_a_cols(key, part):
    key = jax.random.fold_in(key, 7)
    first, second, third, fourth = jax.random.split(key, 4)
    home = (jnp.arange(TILES, dtype=jnp.int32) // FTR)[:, None]
    offset = jax.random.randint(fourth, (TILES, N_COL), -1, 2)
    near = jnp.clip(home + offset, 0, N_ROW - 1)
    far = jax.random.randint(first, (TILES, N_COL), 0, N_ROW)
    pick = jax.random.randint(third, (TILES, N_COL), 0, 8)
    slab = jnp.where(pick == 0, far, near)
    within = jax.random.randint(second, (TILES, N_COL), 0, FTD)
    column = jnp.arange(N_COL, dtype=jnp.int32)[None, :]
    return ((slab * N_COL + column) * FTD + within).astype(jnp.int32)


def touch_ends(array, key, least, largest):
    shape = array.shape
    index_at = [jax.random.randint(jax.random.fold_in(key, axis), (), 0, shape[axis]) for axis in range(len(shape))]
    array = array.at[tuple(index_at)].set(least)
    longest = shape.index(max(shape))
    index_at[longest] = (index_at[longest] + 1) % shape[longest]
    return array.at[tuple(index_at)].set(largest)


def level_of(key, dims, shards, low, high):
    def one(dim, shards_of):
        heights = jax.random.uniform(jax.random.fold_in(jax.random.fold_in(key, 6), dim), (shards_of,), jnp.float32, low / len(shards), high / len(shards))
        return jnp.repeat(jnp.exp(heights), dims[dim] // shards_of).reshape((-1,) + (1,) * (len(dims) - dim - 1))

    gain = one(*shards[0])
    for cut in shards[1:]:
        gain = gain * one(*cut)
    return gain


def shared_out(own_key, own, number, rows, number_of, top, most, lean):
    order = jax.random.permutation(own_key, number_of)
    crowded, usual = portions_of(number_of, rows * top, most, lean, True), portions_of(number_of, rows * top, most, lean, False)
    places = jnp.arange(number_of)

    def named(sizes, offset_by):
        used = int((sizes > 0).sum())
        fixed = max(1, used // 4)
        passed = fixed + (places - fixed + offset_by * (used - fixed)) % max(1, number_of - fixed)
        return jnp.zeros((number_of,), jnp.int32).at[order[jnp.where(places < fixed, places, passed)]].set(jnp.asarray(sizes, jnp.int32))

    sizes = jnp.where(number % 4 == 0, named(crowded, number // 4), named(usual, number - number // 4 - 1))
    mixed = jax.random.permutation(jax.random.fold_in(own, 3), number_of)
    source_of, receiver = mixed[0:number_of // 2 * 2:2], mixed[1:number_of // 2 * 2:2]
    margin = jnp.minimum(sizes[source_of] - 1, most - sizes[receiver]) // 2
    margin = jnp.where((source_of == order[0]) | (receiver == order[0]) | (sizes[receiver] == 0), 0, jnp.maximum(margin, 0))
    passed = jax.random.randint(jax.random.fold_in(own, 4), (number_of // 2,), 0, 1 << 20) % (margin + 1)
    sizes = sizes.at[source_of].add(-passed).at[receiver].add(passed)
    labels = jnp.searchsorted(jnp.cumsum(sizes), jnp.arange(rows * top), side="right").astype(jnp.int32)
    listing = labels.reshape(top, rows).T
    listing = listing[jax.random.permutation(jax.random.fold_in(own, 1), rows)]
    offset_by = jax.random.randint(jax.random.fold_in(own, 2), (rows, 1), 0, top)
    return jnp.take_along_axis(listing, (jnp.arange(top)[None, :] + offset_by) % top, axis=1)


def portions_of(count, total, most, slope, full):
    portions = [(1 << 20) // math.isqrt(grade ** slope) + 1 for grade in range(1, count + 1)]
    largest = most if full else min(most, max(-(-total // count), total * portions[0] // sum(portions)))
    least = 1 if total - largest >= count - 1 else 0
    holding, rest = [largest] + [least] * (count - 1), total - largest - least * (count - 1)
    while rest > 0:
        movable = [i for i in range(1, count) if holding[i] < largest] or [i for i in range(1, count) if holding[i] < most]
        mass, budget = sum([portions[i] for i in movable]), rest
        for i in movable:
            more = min(most - holding[i], max(1, budget * portions[i] // mass), rest)
            holding[i] = holding[i] + more
            rest = rest - more
    return np.array(holding)


def normal_values(stream_key, extent, spread, limit, cuts=(), kind=jnp.bfloat16):
    drawn = spread * jax.random.normal(stream_key, extent, jnp.float32)
    if cuts:
        drawn = drawn * level_of(stream_key, extent, cuts, -0.22, 0.18)
    return jnp.clip(drawn, -limit, limit).astype(kind)


def setup_inputs(seed: int = 0) -> dict:
    keys = jax.random.split(jax.random.key(seed), 6)
    a_blocks = normal_values(keys[0], (TILES, N_COL, B, B), 0.25, 4.0, ((0, 8), (1, 4)))
    p_tiles = normal_values(keys[1], (TILES, B, B), B ** -0.5, 0.5, ((0, 32),))
    owner_keys = jax.random.split(jax.random.fold_in(keys[2], 1), TILES // FTR)
    owner_turns = jax.random.permutation(jax.random.fold_in(keys[2], 3), TILES // FTR)
    owner = jax.vmap(lambda own, number: shared_out(jax.random.fold_in(keys[2], 2), own, number, FTR, N_ROW, 1, CAP, 1))(owner_keys, owner_turns).reshape((TILES, 1))
    agg_local = touch_ends(jax.random.randint(keys[3], (TILES,), 0, OWN), jax.random.fold_in(keys[3], 1), 0, OWN - 1).astype(jnp.int32)
    a_cols = draw_a_cols(jax.random.fold_in(keys[5], 71), 0)
    return {"a_blocks": a_blocks, "p_tiles": p_tiles, "owner": owner, "agg_local": agg_local, "a_cols": a_cols}


def reference(a_blocks, p_tiles, owner, agg_local, a_cols):
    aggregate = owner[:, 0] * OWN + agg_local
    groups = jnp.arange(TILES, dtype=jnp.int32).reshape(TILES // FTR, FTR)

    def accumulate(total, tiles):
        columns = a_cols[tiles]
        left = a_blocks[tiles].astype(jnp.float32)
        right = p_tiles[columns].astype(jnp.float32)
        product = jnp.einsum("tcij,tcjk->tcik", left, right).astype(jnp.bfloat16)
        row_side = p_tiles[tiles].astype(jnp.float32)
        contrib = jnp.einsum("tji,tcjk->tcik", row_side, product.astype(jnp.float32))
        where_to = aggregate[tiles][:, None] * NAGG + aggregate[columns]
        total = total.at[where_to.reshape(-1)].add(contrib.reshape(-1, B, B))
        return total, None

    start = jnp.zeros((NAGG * NAGG, B, B), jnp.float32)
    total, unused = lax.scan(accumulate, start, groups)
    return total.reshape(NAGG, NAGG, B, B)
```

```python
import functools
import math

import jax
import jax.numpy as jnp
from jax import lax
from jax.experimental import pallas as pl
from jax.experimental.pallas import tpu as pltpu
from jax.sharding import PartitionSpec as P

OWN = 2
UNROLL = 8
GROUPS = 4


def ring_order(count):
    return list(range(0, count, 2)) + list(range(1, count, 2))[::-1]


def swap(value, axis, bit):
    size = lax.axis_size(axis)
    return lax.ppermute(value, axis, [(i, i ^ bit) for i in range(size)])


def log2(size):
    power = size.bit_length() - 1
    assert size == 1 << power
    return power


class Sizes:
    def __init__(self, rows, cols, tiles, side):
        self.rows, self.cols, self.tiles, self.side = rows, cols, tiles, side
        self.slab = cols * tiles
        self.pairs = 2 * self.slab
        self.width = OWN * rows // cols
        self.per = OWN * self.width
        self.his = rows // 4
        self.buckets = 2 * self.his
        self.slots = self.pairs + self.buckets * UNROLL
        self.half = rows // 2
        self.early = (rows - 1, rows - 3)
        self.near = sum(self.early) * tiles
        cells = 2 * cols * self.per
        self.fields, shift = [], 0
        for size in (self.pairs, 2 * rows * tiles, self.slab, cells):
            self.fields.append((shift, size - 1))
            shift += log2(size)
        assert shift <= 31


def field(s, entry, k):
    shift, mask = s.fields[k]
    return (entry >> shift) & mask


def plan_kernel(s, cols_ref, aggs_ref, plan_ref, starts_ref, info, counts):
    row = lax.axis_index("row")
    col = lax.axis_index("col")

    def ring_place(index):
        return jnp.where((index & 1) == 0, index >> 1, s.rows - 1 - (index >> 1))

    here = ring_place(row)
    for b in range(s.buckets):
        counts[b] = 0

    def blank(k, carry):
        plan_ref[k] = -1
        return carry

    lax.fori_loop(0, s.slots + 1, blank, 0, unroll=8)

    def sort(i, carry):
        tile = i & (s.slab - 1)
        side = i >> log2(s.slab)
        other = cols_ref[i]
        other_row = other >> log2(s.slab)
        i_agg = aggs_ref[tile]
        j_agg = aggs_ref[((other_row ^ row) << log2(s.slab)) + (other & (s.slab - 1))]
        rel_col = (j_agg >> log2(s.width)) ^ col
        rel_row = (i_agg >> log2(OWN)) ^ row
        turn = ring_place(other_row) - here
        away = jnp.where(((col ^ side) & 1) == 0, turn, -turn) & (s.rows - 1)
        reach = jnp.abs(away - s.half)
        late = jnp.where(reach <= side, 1, 0)
        order = away - jnp.where(away > s.half, 1 + 2 * side, 0) + side * s.early[0]
        last = jnp.where(side == 0, 0, 2 + away - s.half)
        piece = jnp.where(late == 1, last, order)
        panel_at = (piece << log2(s.tiles)) + (other & (s.tiles - 1))
        rel_part = (tile >> log2(s.tiles)) ^ col
        part = (rel_part & 1) * (s.cols // 2) + (rel_part >> 1)
        rows_at = (part << log2(s.tiles)) + (tile & (s.tiles - 1))
        cell = (rel_row & 3) * (s.cols // 2) + (rel_col >> 1)
        cell = (cell << log2(OWN)) + (i_agg & (OWN - 1))
        cell = (cell << log2(s.width)) + (j_agg & (s.width - 1))
        bucket = (rel_row >> 2) * 2 + late
        mine = (rel_col & 1) == 0
        rank = counts[bucket]
        counts[bucket] = rank + jnp.where(mine, 1, 0)
        info[i * 2] = jnp.where(mine, rank * s.buckets + bucket, -1)
        entry = i
        for k, value in enumerate((panel_at, rows_at, cell)):
            entry = entry + (value << s.fields[k + 1][0])
        info[i * 2 + 1] = entry
        return carry

    lax.fori_loop(0, s.pairs, sort, 0, unroll=4)

    start = jnp.int32(0)
    for b in range(s.buckets):
        starts_ref[b] = start
        start = start + ((counts[b] + UNROLL - 1) & ~(UNROLL - 1))
    starts_ref[s.buckets] = start

    def place(i, carry):
        key = info[i * 2]
        slot = starts_ref[key & (s.buckets - 1)] + (key >> log2(s.buckets))
        plan_ref[jnp.where(key >= 0, slot, s.slots)] = info[i * 2 + 1]
        return carry

    lax.fori_loop(0, s.pairs, place, 0, unroll=4)


def room(*shapes):
    total = sum(math.prod(shape) * jnp.dtype(dtype).itemsize for shape, dtype in shapes)
    return total + (2 << 20)


def make_plan(s, cols, aggs):
    smem = pl.BlockSpec(memory_space=pltpu.SMEM)
    return pl.pallas_call(
        functools.partial(plan_kernel, s),
        in_specs=[smem, smem],
        out_specs=[smem, smem],
        out_shape=[
            jax.ShapeDtypeStruct((s.slots + 1,), jnp.int32),
            jax.ShapeDtypeStruct((s.buckets + 1,), jnp.int32),
        ],
        scratch_shapes=[
            pltpu.SMEM((s.pairs * 2,), jnp.int32),
            pltpu.SMEM((s.buckets,), jnp.int32),
        ],
        compiler_params=pltpu.CompilerParams(vmem_limit_bytes=room()),
        cost_estimate=pl.CostEstimate(flops=1 << 20, bytes_accessed=1 << 20, transcendentals=0),
    )(cols, aggs)


def product_kernel(s, plan_ref, starts_ref, *refs):
    slots_ref, rows_ref, a_buf, panel, rows_buf, sems = refs[-6:]
    copies = []
    for k in range(2):
        copies.append((refs[k], a_buf.at[pl.ds(k * s.slab, s.slab)]))
    for k in range(s.cols):
        copies.append((refs[2 + k], rows_buf.at[pl.ds(k * s.tiles, s.tiles)]))
    for k in range(sum(s.early)):
        source = refs[2] if k == 0 else refs[1 + s.cols + k]
        copies.append((source, panel.at[pl.ds(k * s.tiles, s.tiles)]))
    copies = [pltpu.make_async_copy(src, dst, sems.at[k]) for k, (src, dst) in enumerate(copies)]
    for copy in copies:
        copy.start()
    for copy in copies:
        copy.wait()

    def turn(k, carry):
        rows_ref[k] = rows_buf[k].T
        return carry

    lax.fori_loop(0, s.slab, turn, 0, unroll=4)

    for hi in range(s.his):
        begin = starts_ref[2 * hi] // UNROLL
        middle = starts_ref[2 * hi + 1] // UNROLL
        end = starts_ref[2 * hi + 2] // UNROLL

        def near(group, carry):
            for u in range(UNROLL):
                n = group * UNROLL + u
                entry = jnp.maximum(plan_ref[n], 0)
                slots_ref[n] = jnp.dot(
                    a_buf[field(s, entry, 0)],
                    panel[field(s, entry, 1)],
                    preferred_element_type=jnp.float32,
                ).astype(jnp.bfloat16)
            return carry

        def far(group, carry):
            for u in range(UNROLL):
                n = group * UNROLL + u
                slots_ref[n] = a_buf[field(s, jnp.maximum(plan_ref[n], 0), 0)]
            return carry

        lax.fori_loop(begin, middle, near, 0)
        lax.fori_loop(middle, end, far, 0)


def make_products(s, plan, starts, a_own, a_other, near, rows):
    smem = pl.BlockSpec(memory_space=pltpu.SMEM)
    vmem = pl.BlockSpec(memory_space=pltpu.VMEM)
    anywhere = pl.BlockSpec(memory_space=pl.ANY)
    shapes = [
        ((count, s.side, s.side), jnp.bfloat16)
        for count in (s.slots, s.slab, s.pairs, s.near, s.slab)
    ]
    hbm = pl.BlockSpec(memory_space=pltpu.HBM)
    a_own, own = (pltpu.with_memory_space_constraint(x, pltpu.HBM) for x in (a_own, rows[0]))
    operands = [a_own, a_other, own, *rows[1:], *near[1:]]
    return pl.pallas_call(
        functools.partial(product_kernel, s),
        in_specs=[smem, smem, hbm, anywhere, hbm] + [anywhere] * (len(operands) - 3),
        out_specs=[vmem, vmem],
        out_shape=[jax.ShapeDtypeStruct(*shape) for shape in shapes[:2]],
        scratch_shapes=[pltpu.VMEM(*shape) for shape in shapes[2:]]
        + [pltpu.SemaphoreType.DMA((len(operands) + 1,))],
        compiler_params=pltpu.CompilerParams(vmem_limit_bytes=room(*shapes)),
        cost_estimate=pl.CostEstimate(
            flops=s.pairs * s.side**3, bytes_accessed=16 << 20, transcendentals=0
        ),
    )(plan, starts, *operands)


def sum_kernel(
    s, plan_ref, starts_ref, slots_ref, rows_ref, far0, far1, far2, far3,
    send0, keep0, send1, keep1, send2, keep2, send3, keep3, total, far_buf, sems,
):
    hi = pl.program_id(0)
    copies = [
        pltpu.make_async_copy(ref, far_buf.at[pl.ds(k * s.tiles, s.tiles)], sems.at[k])
        for k, ref in enumerate((far0, far1, far2, far3))
    ]

    @pl.when(hi == 0)
    def _():
        for copy in copies:
            copy.start()

    cells = total.shape[0]

    def clear(k, carry):
        total[pl.ds(k * 8, 8)] = jnp.zeros((8,) + total.shape[1:], jnp.float32)
        return carry

    lax.fori_loop(0, cells // 8, clear, 0)

    def add(n, product):
        entry = plan_ref[n]
        known = jnp.maximum(entry, 0)
        term = jnp.dot(
            rows_ref[field(s, known, 2)], product, preferred_element_type=jnp.float32
        )
        total[field(s, known, 3)] += jnp.where(entry >= 0, term, 0.0)

    def near(group, carry):
        for u in range(UNROLL):
            n = group * UNROLL + u
            add(n, slots_ref[n])
        return carry

    def far(group, carry):
        for u in range(UNROLL):
            n = group * UNROLL + u
            piece = far_buf[field(s, jnp.maximum(plan_ref[n], 0), 1)]
            product = jnp.dot(slots_ref[n], piece, preferred_element_type=jnp.float32)
            add(n, product.astype(jnp.bfloat16))
        return carry

    begin = starts_ref[2 * hi] // UNROLL
    middle = starts_ref[2 * hi + 1] // UNROLL
    end = starts_ref[2 * hi + 2] // UNROLL
    lax.fori_loop(begin, middle, near, 0)

    @pl.when(hi == 0)
    def _():
        for copy in copies:
            copy.wait()

    lax.fori_loop(middle, end, far, 0)

    xh = s.cols // 4
    tall = s.side // GROUPS

    for z1 in range(2):
        for y in range(2):
            for x in range(xh):
                for x1 in range(2):
                    base = (((z1 * 2 + y) * xh + x) * 2 + x1) * s.per
                    part = [
                        total[pl.ds(base, s.per), k * tall:(k + 1) * tall, :]
                        for k in range(GROUPS)
                    ]
                    for k, (bit, send, keep, at) in enumerate((
                        (z1, send0, keep0, (y, 0, x1)),
                        (y, send1, keep1, (0, x1, z1)),
                        (x1, send2, keep2, (y, z1, 0)),
                        (z1, send3, keep3, (x1, 0, y)),
                    )):
                        if bit:
                            send[(*at, 0, x)] = part[k].astype(jnp.bfloat16)
                        else:
                            keep[(*at, 0, x)] = part[k]


def make_sums(s, plan, starts, slots, rows_t, far):
    smem = pl.BlockSpec(memory_space=pltpu.SMEM)
    vmem = pl.BlockSpec(memory_space=pltpu.VMEM)
    anywhere = pl.BlockSpec(memory_space=pl.ANY)
    last = (s.cols // 4, s.per, s.side // GROUPS, s.side)
    blocks = [
        ((2, 1, 2), lambda h: (0, h & 1, 0, h >> 1, 0, 0, 0, 0)),
        ((1, 2, 2), lambda h: (h & 1, 0, 0, h >> 1, 0, 0, 0, 0)),
        ((2, 2, 1), lambda h: (0, 0, h & 1, h >> 1, 0, 0, 0, 0)),
        ((2, 1, 2), lambda h: (0, h & 1, 0, h >> 1, 0, 0, 0, 0)),
    ]
    shapes = [
        ((s.slots + s.slab + 4 * s.tiles, s.side, s.side), jnp.bfloat16),
        ((2 * s.cols * s.per, s.side, s.side), jnp.float32),
    ]
    out_shape, out_specs = [], []
    for block, index in blocks:
        for dtype in (jnp.bfloat16, jnp.float32):
            out_shape.append(jax.ShapeDtypeStruct((2, 2, 2, s.his // 2) + last, dtype))
            out_specs.append(pl.BlockSpec(block + (1,) + last, index))
            shapes.append(((2,) + block + last, dtype))
    return pl.pallas_call(
        functools.partial(sum_kernel, s),
        grid=(s.his,),
        in_specs=[smem, smem, vmem, vmem] + [anywhere] * 4,
        out_specs=out_specs,
        out_shape=out_shape,
        scratch_shapes=[
            pltpu.VMEM((2 * s.cols * s.per, s.side, s.side), jnp.float32),
            pltpu.VMEM((4 * s.tiles, s.side, s.side), jnp.bfloat16),
            pltpu.SemaphoreType.DMA((4,)),
        ],
        compiler_params=pltpu.CompilerParams(vmem_limit_bytes=room(*shapes)),
        cost_estimate=pl.CostEstimate(
            flops=s.pairs * s.side**3, bytes_accessed=16 << 20, transcendentals=0
        ),
    )(plan, starts, slots, rows_t, *far)


def shards(a_blocks, p_tiles, owner, agg_local, a_cols):
    s = Sizes(
        lax.axis_size("row"), lax.axis_size("col"), p_tiles.shape[0], p_tiles.shape[1]
    )
    order = ring_order(s.rows)
    barrier = lax.optimization_barrier

    def ring(value, stream):
        moves = []
        for k in range(s.rows):
            for c in range(s.cols):
                step = 1 if (stream + c) % 2 == 0 else -1
                to = order[(k + step) % s.rows]
                moves.append((order[k] * s.cols + c, to * s.cols + c))
        return lax.ppermute(value, ("row", "col"), moves)

    first, second = ring(p_tiles, 0), ring(p_tiles, 1)
    rows = [p_tiles]
    bit = 2
    while bit < s.cols:
        rows += [swap(piece, "col", bit) for piece in rows]
        bit *= 2
    p_other = swap(p_tiles, "col", 1)
    cols = a_cols[:, 0]
    cols_other = swap(cols, "col", 1)
    aggs = owner[:, 0] * OWN + agg_local
    first, second, p_other, cols_other, aggs, *rows[1:] = barrier(
        (first, second, p_other, cols_other, aggs, *rows[1:])
    )
    own_near = {0: p_tiles, s.rows - 1: first, 1: second}
    other_near = {0: p_other}

    aggs = [aggs] + [swap(aggs, "row", mask) for mask in (1, 2, 3)]
    aggs = jnp.concatenate(aggs, 0)
    held = [1, s.rows - 1]
    for step in range(2, s.half):
        first, second = barrier((ring(first, 0), ring(second, 1)))
        if step == 2:
            came, aggs, a_own, *rest = barrier((first, aggs, a_blocks[:, 0], *rows[1:]))
            bit = 4
            while bit < s.rows:
                aggs = jnp.concatenate([aggs, swap(aggs, "row", bit)], 0)
                bit *= 2
            a_other = swap(a_own, "col", 1)
            rows += [p_other] + [swap(piece, "col", 1) for piece in rest]
        else:
            came, *rest = barrier((first, *(own_near[away] for away in held)))
            for away, piece in zip(held, rest):
                other_near[away] = swap(piece, "col", 1)
            held = []
        own_near[s.rows - step], own_near[step] = came, second
        held += [step, s.rows - step]

    far = ring(first, 0)
    last_other = [swap(own_near[away], "col", 1) for away in (s.half - 1, s.half + 1)]
    plan, starts = make_plan(s, jnp.concatenate([cols, cols_other], 0), aggs)
    near = [own_near[k] for k in sorted(own_near)]
    near += [other_near[k] for k in sorted(other_near)]
    slots, rows_t = make_products(s, plan, starts, a_blocks[:, 0], a_other, near, rows)
    far, slots, rows_t = barrier((far, slots, rows_t))
    far_other = swap(far, "col", 1)
    parts = make_sums(s, plan, starts, slots, rows_t, [far, last_other[0], far_other, last_other[1]])

    y, z1, z2, x1 = ("row", 1), ("row", 2), ("row", 4), ("col", 2)
    orders = [[z1, y, z2, x1], [y, z2, x1, z1], [x1, y, z1, z2], [z1, x1, z2, y]]
    sends, keeps, steps = list(parts[0::2]), list(parts[1::2]), [0] * GROUPS
    moving = [swap(sends[k], *orders[k][0]) for k in range(GROUPS)]
    for k in list(range(GROUPS)) * 4:
        got = moving[k]
        steps[k] += 1
        if steps[k] < 4:
            send = (keeps[k][1] + got[1].astype(jnp.float32)).astype(jnp.bfloat16)
            moving[k] = swap(send, *orders[k][steps[k]])
            keeps[k] = keeps[k][0] + got[0].astype(jnp.float32)
        else:
            keeps[k] = keeps[k] + got.astype(jnp.float32)
    total = jnp.concatenate(keeps, -2)
    tail = [("row", 1 << k) for k in range(3, log2(s.rows))][::-1]
    tail += [("col", 1 << k) for k in range(2, log2(s.cols))][::-1]
    total = total.reshape((2,) * len(tail) + total.shape[-3:])
    for axis in tail:
        got = swap(total[1].astype(jnp.bfloat16), *axis)
        total = total[0] + got.astype(jnp.float32)
    return total.reshape(OWN, s.width, s.side, s.side)


def solution(mesh):
    in_specs = (
        P("row", "col", None, None),
        P(("row", "col"), None, None),
        P("row", None),
        P("row"),
        P("row", "col"),
    )
    out_specs = P("row", "col", None, None)
    return jax.shard_map(shards, mesh=mesh, in_specs=in_specs, out_specs=out_specs, check_vma=False)
```

```python
import functools
import math

import jax
import jax.numpy as jnp
from jax import lax
from jax.experimental import pallas as pl
from jax.experimental.pallas import tpu as pltpu
from jax.sharding import PartitionSpec as P

OWN = 2
UNROLL = 8
GROUPS = 4


def ring_order(count):
    return list(range(0, count, 2)) + list(range(1, count, 2))[::-1]


def swap(value, axis, bit):
    size = lax.axis_size(axis)
    return lax.ppermute(value, axis, [(i, i ^ bit) for i in range(size)])


def log2(size):
    power = size.bit_length() - 1
    assert size == 1 << power
    return power


class Sizes:
    def __init__(self, rows, cols, tiles, side):
        self.rows, self.cols, self.tiles, self.side = rows, cols, tiles, side
        self.slab = cols * tiles
        self.pairs = 2 * self.slab
        self.width = OWN * rows // cols
        self.per = OWN * self.width
        self.his = rows // 4
        self.buckets = 2 * self.his
        self.slots = self.pairs + self.buckets * UNROLL
        self.half = rows // 2
        self.early = rows - 1
        self.near = 2 * self.early * tiles
        cells = 2 * cols * self.per
        self.fields, shift = [], 0
        for size in (self.pairs, 2 * rows * tiles, self.slab, cells):
            self.fields.append((shift, size - 1))
            shift += log2(size)
        assert shift <= 31


def field(s, entry, k):
    shift, mask = s.fields[k]
    return (entry >> shift) & mask


def plan_kernel(s, cols_ref, aggs_ref, plan_ref, starts_ref, info, counts):
    row = lax.axis_index("row")
    col = lax.axis_index("col")

    def ring_place(index):
        return jnp.where((index & 1) == 0, index >> 1, s.rows - 1 - (index >> 1))

    here = ring_place(row)
    for b in range(s.buckets):
        counts[b] = 0

    def blank(k, carry):
        plan_ref[k] = -1
        return carry

    lax.fori_loop(0, s.slots + 1, blank, 0, unroll=8)

    def sort(i, carry):
        tile = i & (s.slab - 1)
        side = i >> log2(s.slab)
        other = cols_ref[i]
        other_row = other >> log2(s.slab)
        i_agg = aggs_ref[tile]
        j_agg = aggs_ref[((other_row ^ row) << log2(s.slab)) + (other & (s.slab - 1))]
        rel_col = (j_agg >> log2(s.width)) ^ col
        rel_row = (i_agg >> log2(OWN)) ^ row
        turn = ring_place(other_row) - here
        away = jnp.where(((col ^ side) & 1) == 0, turn, -turn) & (s.rows - 1)
        late = jnp.where(away == s.half, 1, 0)
        order = away - jnp.where(away > s.half, 1, 0) + side * s.early
        piece = jnp.where(late == 1, side, order)
        panel_at = (piece << log2(s.tiles)) + (other & (s.tiles - 1))
        rel_part = (tile >> log2(s.tiles)) ^ col
        part = (rel_part & 1) * (s.cols // 2) + (rel_part >> 1)
        rows_at = (part << log2(s.tiles)) + (tile & (s.tiles - 1))
        cell = (rel_row & 3) * (s.cols // 2) + (rel_col >> 1)
        cell = (cell << log2(OWN)) + (i_agg & (OWN - 1))
        cell = (cell << log2(s.width)) + (j_agg & (s.width - 1))
        bucket = (rel_row >> 2) * 2 + late
        mine = (rel_col & 1) == 0
        rank = counts[bucket]
        counts[bucket] = rank + jnp.where(mine, 1, 0)
        info[i * 2] = jnp.where(mine, rank * s.buckets + bucket, -1)
        entry = i
        for k, value in enumerate((panel_at, rows_at, cell)):
            entry = entry + (value << s.fields[k + 1][0])
        info[i * 2 + 1] = entry
        return carry

    lax.fori_loop(0, s.pairs, sort, 0, unroll=4)

    start = jnp.int32(0)
    for b in range(s.buckets):
        starts_ref[b] = start
        start = start + ((counts[b] + UNROLL - 1) & ~(UNROLL - 1))
    starts_ref[s.buckets] = start

    def place(i, carry):
        key = info[i * 2]
        slot = starts_ref[key & (s.buckets - 1)] + (key >> log2(s.buckets))
        plan_ref[jnp.where(key >= 0, slot, s.slots)] = info[i * 2 + 1]
        return carry

    lax.fori_loop(0, s.pairs, place, 0, unroll=4)


def room(*shapes):
    total = sum(math.prod(shape) * jnp.dtype(dtype).itemsize for shape, dtype in shapes)
    return total + (2 << 20)


def make_plan(s, cols, aggs):
    smem = pl.BlockSpec(memory_space=pltpu.SMEM)
    return pl.pallas_call(
        functools.partial(plan_kernel, s),
        in_specs=[smem, smem],
        out_specs=[smem, smem],
        out_shape=[
            jax.ShapeDtypeStruct((s.slots + 1,), jnp.int32),
            jax.ShapeDtypeStruct((s.buckets + 1,), jnp.int32),
        ],
        scratch_shapes=[
            pltpu.SMEM((s.pairs * 2,), jnp.int32),
            pltpu.SMEM((s.buckets,), jnp.int32),
        ],
        compiler_params=pltpu.CompilerParams(vmem_limit_bytes=room()),
        cost_estimate=pl.CostEstimate(flops=1 << 20, bytes_accessed=16 << 20, transcendentals=0),
    )(cols, aggs)


def product_kernel(s, plan_ref, starts_ref, *refs):
    slots_ref, rows_ref, a_buf, panel, rows_buf, sems = refs[-6:]
    copies = []
    for k in range(2):
        copies.append((refs[k], a_buf.at[pl.ds(k * s.slab, s.slab)]))
    for k in range(s.cols):
        copies.append((refs[2 + k], rows_buf.at[pl.ds(k * s.tiles, s.tiles)]))
    for k in range(2 * s.early):
        source = refs[2] if k == 0 else refs[1 + s.cols + k]
        copies.append((source, panel.at[pl.ds(k * s.tiles, s.tiles)]))
    copies = [pltpu.make_async_copy(src, dst, sems.at[k]) for k, (src, dst) in enumerate(copies)]
    for copy in copies:
        copy.start()
    for copy in copies:
        copy.wait()

    def turn(k, carry):
        rows_ref[k] = rows_buf[k].T
        return carry

    lax.fori_loop(0, s.slab, turn, 0, unroll=4)

    for hi in range(s.his):
        begin = starts_ref[2 * hi] // UNROLL
        middle = starts_ref[2 * hi + 1] // UNROLL
        end = starts_ref[2 * hi + 2] // UNROLL

        def near(group, carry):
            for u in range(UNROLL):
                n = group * UNROLL + u
                entry = jnp.maximum(plan_ref[n], 0)
                slots_ref[n] = jnp.dot(
                    a_buf[field(s, entry, 0)],
                    panel[field(s, entry, 1)],
                    preferred_element_type=jnp.float32,
                ).astype(jnp.bfloat16)
            return carry

        def far(group, carry):
            for u in range(UNROLL):
                n = group * UNROLL + u
                slots_ref[n] = a_buf[field(s, jnp.maximum(plan_ref[n], 0), 0)]
            return carry

        lax.fori_loop(begin, middle, near, 0)
        lax.fori_loop(middle, end, far, 0)


def make_products(s, plan, starts, a_own, a_other, near, rows):
    smem = pl.BlockSpec(memory_space=pltpu.SMEM)
    vmem = pl.BlockSpec(memory_space=pltpu.VMEM)
    anywhere = pl.BlockSpec(memory_space=pl.ANY)
    shapes = [
        ((count, s.side, s.side), jnp.bfloat16)
        for count in (s.slots, s.slab, s.pairs, s.near, s.slab)
    ]
    hbm = pl.BlockSpec(memory_space=pltpu.HBM)
    a_own, own = (pltpu.with_memory_space_constraint(x, pltpu.HBM) for x in (a_own, rows[0]))
    operands = [a_own, a_other, own, *rows[1:], *near[1:]]
    return pl.pallas_call(
        functools.partial(product_kernel, s),
        in_specs=[smem, smem, hbm, anywhere, hbm] + [anywhere] * (len(operands) - 3),
        out_specs=[vmem, vmem],
        out_shape=[jax.ShapeDtypeStruct(*shape) for shape in shapes[:2]],
        scratch_shapes=[pltpu.VMEM(*shape) for shape in shapes[2:]]
        + [pltpu.SemaphoreType.DMA((len(operands) + 1,))],
        compiler_params=pltpu.CompilerParams(vmem_limit_bytes=room(*shapes)),
        cost_estimate=pl.CostEstimate(
            flops=s.pairs * s.side**3, bytes_accessed=1 << 20, transcendentals=0
        ),
    )(plan, starts, *operands)


def sum_kernel(
    s, plan_ref, starts_ref, slots_ref, rows_ref, far0, far1,
    send0, keep0, send1, keep1, send2, keep2, send3, keep3, total, far_buf, sems,
):
    hi = pl.program_id(0)
    copies = [
        pltpu.make_async_copy(ref, far_buf.at[pl.ds(k * s.tiles, s.tiles)], sems.at[k])
        for k, ref in enumerate((far0, far1))
    ]

    @pl.when(hi == 0)
    def _():
        for copy in copies:
            copy.start()

    cells = total.shape[0]

    def clear(k, carry):
        total[pl.ds(k * 8, 8)] = jnp.zeros((8,) + total.shape[1:], jnp.float32)
        return carry

    lax.fori_loop(0, cells // 8, clear, 0)

    def add(n, product):
        entry = plan_ref[n]
        known = jnp.maximum(entry, 0)
        term = jnp.dot(
            rows_ref[field(s, known, 2)], product, preferred_element_type=jnp.float32
        )
        total[field(s, known, 3)] += jnp.where(entry >= 0, term, 0.0)

    def near(group, carry):
        for u in range(UNROLL):
            n = group * UNROLL + u
            add(n, slots_ref[n])
        return carry

    def far(group, carry):
        for u in range(UNROLL):
            n = group * UNROLL + u
            piece = far_buf[field(s, jnp.maximum(plan_ref[n], 0), 1)]
            product = jnp.dot(slots_ref[n], piece, preferred_element_type=jnp.float32)
            add(n, product.astype(jnp.bfloat16))
        return carry

    begin = starts_ref[2 * hi] // UNROLL
    middle = starts_ref[2 * hi + 1] // UNROLL
    end = starts_ref[2 * hi + 2] // UNROLL
    lax.fori_loop(begin, middle, near, 0)

    @pl.when(hi == 0)
    def _():
        for copy in copies:
            copy.wait()

    lax.fori_loop(middle, end, far, 0)

    xh = s.cols // 4
    tall = s.side // GROUPS

    for z1 in range(2):
        for y in range(2):
            for x in range(xh):
                for x1 in range(2):
                    base = (((z1 * 2 + y) * xh + x) * 2 + x1) * s.per
                    part = [
                        total[pl.ds(base, s.per), k * tall:(k + 1) * tall, :]
                        for k in range(GROUPS)
                    ]
                    for k, (bit, send, keep, at) in enumerate((
                        (z1, send0, keep0, (y, 0, x1)),
                        (y, send1, keep1, (0, x1, z1)),
                        (x1, send2, keep2, (y, z1, 0)),
                        (z1, send3, keep3, (x1, 0, y)),
                    )):
                        if bit:
                            send[(*at, 0, x)] = part[k].astype(jnp.bfloat16)
                        else:
                            keep[(*at, 0, x)] = part[k]


def make_sums(s, plan, starts, slots, rows_t, far):
    smem = pl.BlockSpec(memory_space=pltpu.SMEM)
    vmem = pl.BlockSpec(memory_space=pltpu.VMEM)
    anywhere = pl.BlockSpec(memory_space=pl.ANY)
    last = (s.cols // 4, s.per, s.side // GROUPS, s.side)
    blocks = [
        ((2, 1, 2), lambda h: (0, h & 1, 0, h >> 1, 0, 0, 0, 0)),
        ((1, 2, 2), lambda h: (h & 1, 0, 0, h >> 1, 0, 0, 0, 0)),
        ((2, 2, 1), lambda h: (0, 0, h & 1, h >> 1, 0, 0, 0, 0)),
        ((2, 1, 2), lambda h: (0, h & 1, 0, h >> 1, 0, 0, 0, 0)),
    ]
    shapes = [
        ((s.slots + s.slab + 2 * s.tiles, s.side, s.side), jnp.bfloat16),
        ((2 * s.cols * s.per, s.side, s.side), jnp.float32),
    ]
    out_shape, out_specs = [], []
    for block, index in blocks:
        for dtype in (jnp.bfloat16, jnp.float32):
            out_shape.append(jax.ShapeDtypeStruct((2, 2, 2, s.his // 2) + last, dtype))
            out_specs.append(pl.BlockSpec(block + (1,) + last, index))
            shapes.append(((2,) + block + last, dtype))
    return pl.pallas_call(
        functools.partial(sum_kernel, s),
        grid=(s.his,),
        in_specs=[smem, smem, vmem, vmem, anywhere, anywhere],
        out_specs=out_specs,
        out_shape=out_shape,
        scratch_shapes=[
            pltpu.VMEM((2 * s.cols * s.per, s.side, s.side), jnp.float32),
            pltpu.VMEM((2 * s.tiles, s.side, s.side), jnp.bfloat16),
            pltpu.SemaphoreType.DMA((2,)),
        ],
        compiler_params=pltpu.CompilerParams(vmem_limit_bytes=room(*shapes)),
        cost_estimate=pl.CostEstimate(
            flops=s.pairs * s.side**3, bytes_accessed=16 << 20, transcendentals=0
        ),
    )(plan, starts, slots, rows_t, *far)


def shards(a_blocks, p_tiles, owner, agg_local, a_cols):
    s = Sizes(
        lax.axis_size("row"), lax.axis_size("col"), p_tiles.shape[0], p_tiles.shape[1]
    )
    order = ring_order(s.rows)
    barrier = lax.optimization_barrier

    def ring(value, stream):
        moves = []
        for k in range(s.rows):
            for c in range(s.cols):
                step = 1 if (stream + c) % 2 == 0 else -1
                to = order[(k + step) % s.rows]
                moves.append((order[k] * s.cols + c, to * s.cols + c))
        return lax.ppermute(value, ("row", "col"), moves)

    first = ring(p_tiles, 0)
    cols = a_cols[:, 0]
    cols_other = swap(cols, "col", 1)
    cols_other, mine = barrier((cols_other, p_tiles))
    second = ring(mine, 1)
    a_other, p_other = swap(a_blocks[:, 0], "col", 1), swap(p_tiles, "col", 1)

    aggs = owner[:, 0] * OWN + agg_local
    came, aggs, a_other, p_other = barrier((first, aggs, a_other, p_other))
    first = ring(first, 0)
    aggs = [aggs] + [swap(aggs, "row", mask) for mask in (1, 2, 3)]
    own_near, other_near = {0: p_tiles, s.rows - 1: came, 1: second}, {0: p_other}
    second = ring(second, 1)
    aggs, mine = barrier((jnp.concatenate(aggs, 0), p_tiles))
    bit = 4
    while bit < s.rows:
        aggs = jnp.concatenate([aggs, swap(aggs, "row", bit)], 0)
        bit *= 2
    rows = [mine]
    bit = 2
    while bit < s.cols:
        rows += [swap(piece, "col", bit) for piece in rows]
        bit *= 2
    plan, starts = make_plan(s, jnp.concatenate([cols, cols_other], 0), aggs)

    held = [1, s.rows - 1]
    for step in range(2, s.half - 1):
        came, *rest = barrier((second, *(own_near[away] for away in held), *rows[1:]))
        for away, piece in zip(held, rest):
            other_near[away] = swap(piece, "col", 1)
        if step == 2:
            rows += [p_other] + [swap(piece, "col", 1) for piece in rest[len(held):]]
        own_near[s.rows - step], own_near[step] = first, came
        first, second = ring(first, 0), ring(second, 1)
        held = [step, s.rows - step]

    others = sorted(set(other_near) - {0})
    tie = (first, second, plan, starts, *rows[s.cols // 2 + 1:])
    tie += (*(own_near[away] for away in held), *(other_near[away] for away in others))
    first, second, plan, starts, *rest = barrier(tie)
    rows[s.cols // 2 + 1:] = rest[:s.cols // 2 - 1]
    rest = rest[s.cols // 2 - 1:]
    for away, piece in zip(others, rest[len(held):]):
        other_near[away] = piece
    far = ring(first, 0)
    own_near[s.half + 1], own_near[s.half - 1] = first, second
    for away, piece in zip(held, rest):
        other_near[away] = swap(piece, "col", 1)
    for away in (s.half + 1, s.half - 1):
        other_near[away] = swap(own_near[away], "col", 1)
    near = [own_near[k] for k in sorted(own_near)]
    near += [other_near[k] for k in sorted(other_near)]
    slots, rows_t = make_products(s, plan, starts, a_blocks[:, 0], a_other, near, rows)
    far, slots, rows_t = barrier((far, slots, rows_t))
    far_other = swap(far, "col", 1)
    parts = make_sums(s, plan, starts, slots, rows_t, [far, far_other])

    y, z1, z2, x1 = ("row", 1), ("row", 2), ("row", 4), ("col", 2)
    orders = [[z1, y, z2, x1], [y, z2, x1, z1], [x1, y, z1, z2], [z1, x1, z2, y]]
    sends, keeps, steps = list(parts[0::2]), list(parts[1::2]), [0] * GROUPS
    moving = [swap(sends[k], *orders[k][0]) for k in range(GROUPS)]
    for k in list(range(GROUPS)) * 4:
        got = moving[k]
        steps[k] += 1
        if steps[k] < 4:
            send = (keeps[k][1] + got[1].astype(jnp.float32)).astype(jnp.bfloat16)
            moving[k] = swap(send, *orders[k][steps[k]])
            keeps[k] = keeps[k][0] + got[0].astype(jnp.float32)
        else:
            keeps[k] = keeps[k] + got.astype(jnp.float32)
    total = jnp.concatenate(keeps, -2)
    tail = [("row", 1 << k) for k in range(3, log2(s.rows))][::-1]
    tail += [("col", 1 << k) for k in range(2, log2(s.cols))][::-1]
    total = total.reshape((2,) * len(tail) + total.shape[-3:])
    for axis in tail:
        got = swap(total[1].astype(jnp.bfloat16), *axis)
        total = total[0] + got.astype(jnp.float32)
    return total.reshape(OWN, s.width, s.side, s.side)


def solution(mesh):
    in_specs = (
        P("row", "col", None, None),
        P(("row", "col"), None, None),
        P("row", None),
        P("row"),
        P("row", "col"),
    )
    out_specs = P("row", "col", None, None)
    return jax.shard_map(shards, mesh=mesh, in_specs=in_specs, out_specs=out_specs, check_vma=False)
```

```python
import functools
import itertools
import math

import jax
import jax.numpy as jnp
from jax import lax
from jax.experimental import pallas as pl
from jax.experimental.pallas import tpu as pltpu
from jax.sharding import PartitionSpec as P

OWN = 2
UNROLL = 8
ORDERS = (("1x2y", "x1y2"), ("xy12", "yx21"), ("y1x2", "2xy1"))
LINKS = {"x": ("col", 2), "y": ("row", 1), "1": ("row", 2), "2": ("row", 4)}


def ring_order(count):
    return list(range(0, count, 2)) + list(range(1, count, 2))[::-1]


def swap(value, axis, bit):
    size = lax.axis_size(axis)
    return lax.ppermute(value, axis, [(i, i ^ bit) for i in range(size)])


def exchange(value, links):
    rows, cols = lax.axis_size("row"), lax.axis_size("col")
    moves = []
    for r in range(rows):
        for c in range(cols):
            axis, bit = LINKS[links[c % 2]]
            to = (r ^ bit, c) if axis == "row" else (r, c ^ bit)
            moves.append((r * cols + c, to[0] * cols + to[1]))
    return lax.ppermute(value, ("row", "col"), moves)


def log2(size):
    power = size.bit_length() - 1
    assert size == 1 << power
    return power


class Sizes:
    def __init__(self, rows, cols, tiles, side):
        self.rows, self.cols, self.tiles, self.side = rows, cols, tiles, side
        self.slab = cols * tiles
        self.pairs = 2 * self.slab
        self.width = OWN * rows // cols
        self.per = OWN * self.width
        self.his = rows // 8
        self.blocks, self.tall = 4 * cols, self.per * side
        third = self.tall // 16 // 3 * 16
        self.splits = (0, third, 2 * third, self.tall)
        self.buckets = 2 * self.his
        self.slots = self.pairs + self.buckets * UNROLL
        self.half = rows // 2
        self.early = rows - 1
        self.near = 2 * self.early * tiles
        self.fields, shift = [], 0
        for size in (self.pairs, 2 * rows * tiles, self.blocks * self.per):
            self.fields.append((shift, size - 1))
            shift += log2(size)
        assert shift <= 31


def field(s, entry, k):
    shift, mask = s.fields[k]
    return (entry >> shift) & mask


def plan_kernel(s, cols_ref, aggs_ref, plan_ref, starts_ref, info, counts):
    row = lax.axis_index("row")
    col = lax.axis_index("col")

    def ring_place(index):
        return jnp.where((index & 1) == 0, index >> 1, s.rows - 1 - (index >> 1))

    here = ring_place(row)
    for b in range(s.buckets):
        counts[b] = 0

    def blank(k, carry):
        plan_ref[k] = -1
        return carry

    lax.fori_loop(0, s.slots + 1, blank, 0, unroll=8)

    def sort(i, carry):
        tile = i & (s.slab - 1)
        side = i >> log2(s.slab)
        other = cols_ref[i]
        other_row = other >> log2(s.slab)
        i_agg = aggs_ref[tile]
        j_agg = aggs_ref[((other_row ^ row) << log2(s.slab)) + (other & (s.slab - 1))]
        rel_col = (j_agg >> log2(s.width)) ^ col
        rel_row = (i_agg >> log2(OWN)) ^ row
        turn = ring_place(other_row) - here
        away = jnp.where(((col ^ side) & 1) == 0, turn, -turn) & (s.rows - 1)
        late = jnp.where(away == s.half, 1, 0)
        order = away - jnp.where(away > s.half, 1, 0) + side * s.early
        piece = jnp.where(late == 1, side, order)
        panel_at = (piece << log2(s.tiles)) + (other & (s.tiles - 1))
        cell = (rel_row & 7) * (s.cols // 2) + (rel_col >> 1)
        cell = (cell << log2(OWN)) + (i_agg & (OWN - 1))
        cell = (cell << log2(s.width)) + (j_agg & (s.width - 1))
        bucket = (rel_row >> 3) * 2 + late
        mine = (rel_col & 1) == 0
        rank = counts[bucket]
        counts[bucket] = rank + jnp.where(mine, 1, 0)
        info[i * 2] = jnp.where(mine, rank * s.buckets + bucket, -1)
        entry = i
        for k, value in enumerate((panel_at, cell)):
            entry = entry + (value << s.fields[k + 1][0])
        info[i * 2 + 1] = entry
        return carry

    lax.fori_loop(0, s.pairs, sort, 0, unroll=4)

    start = jnp.int32(0)
    for b in range(s.buckets):
        starts_ref[b] = start
        start = start + ((counts[b] + UNROLL - 1) & ~(UNROLL - 1))
    starts_ref[s.buckets] = start

    def place(i, carry):
        key = info[i * 2]
        slot = starts_ref[key & (s.buckets - 1)] + (key >> log2(s.buckets))
        plan_ref[jnp.where(key >= 0, slot, s.slots)] = info[i * 2 + 1]
        return carry

    lax.fori_loop(0, s.pairs, place, 0, unroll=4)


def room(*shapes):
    total = sum(math.prod(shape) * jnp.dtype(dtype).itemsize for shape, dtype in shapes)
    return total + (2 << 20)


def make_plan(s, cols, aggs):
    smem = pl.BlockSpec(memory_space=pltpu.SMEM)
    return pl.pallas_call(
        functools.partial(plan_kernel, s),
        in_specs=[smem, smem],
        out_specs=[smem, smem],
        out_shape=[
            jax.ShapeDtypeStruct((s.slots + 1,), jnp.int32),
            jax.ShapeDtypeStruct((s.buckets + 1,), jnp.int32),
        ],
        scratch_shapes=[
            pltpu.SMEM((s.pairs * 2,), jnp.int32),
            pltpu.SMEM((s.buckets,), jnp.int32),
        ],
        compiler_params=pltpu.CompilerParams(vmem_limit_bytes=room()),
        cost_estimate=pl.CostEstimate(flops=1 << 20, bytes_accessed=16 << 20, transcendentals=0),
    )(cols, aggs)


def product_kernel(s, plan_ref, starts_ref, *refs):
    slots_ref, rows_ref, a_buf, panel, rows_buf, sems = refs[-6:]
    copies = []
    for k in range(2):
        copies.append((refs[k], a_buf.at[pl.ds(k * s.slab, s.slab)]))
    for k in range(s.cols):
        copies.append((refs[2 + k], rows_buf.at[pl.ds(k * s.tiles, s.tiles)]))
    for k in range(2 * s.early):
        source = refs[2] if k == 0 else refs[1 + s.cols + k]
        copies.append((source, panel.at[pl.ds(k * s.tiles, s.tiles)]))
    copies = [pltpu.make_async_copy(src, dst, sems.at[k]) for k, (src, dst) in enumerate(copies)]
    for copy in copies:
        copy.start()
    for copy in copies:
        copy.wait()

    col = lax.axis_index("col")

    def turn(k, carry):
        part = k >> log2(s.tiles)
        rel = (part & (s.cols // 2 - 1)) * 2 + (part >> log2(s.cols // 2))
        rows_ref[((rel ^ col) << log2(s.tiles)) + (k & (s.tiles - 1))] = rows_buf[k].T
        return carry

    lax.fori_loop(0, s.slab, turn, 0, unroll=4)

    for hi in range(s.his):
        begin = starts_ref[2 * hi] // UNROLL
        middle = starts_ref[2 * hi + 1] // UNROLL
        end = starts_ref[2 * hi + 2] // UNROLL

        def near(group, carry):
            for u in range(UNROLL):
                n = group * UNROLL + u
                entry = jnp.maximum(plan_ref[n], 0)
                slots_ref[n] = jnp.dot(
                    a_buf[field(s, entry, 0)],
                    panel[field(s, entry, 1)],
                    preferred_element_type=jnp.float32,
                ).astype(jnp.bfloat16)
            return carry

        def far(group, carry):
            for u in range(UNROLL):
                n = group * UNROLL + u
                slots_ref[n] = a_buf[field(s, jnp.maximum(plan_ref[n], 0), 0)]
            return carry

        lax.fori_loop(begin, middle, near, 0)
        lax.fori_loop(middle, end, far, 0)


def make_products(s, plan, starts, a_own, a_other, near, rows):
    smem = pl.BlockSpec(memory_space=pltpu.SMEM)
    vmem = pl.BlockSpec(memory_space=pltpu.VMEM)
    anywhere = pl.BlockSpec(memory_space=pl.ANY)
    shapes = [
        ((count, s.side, s.side), jnp.bfloat16)
        for count in (s.slots, s.slab, s.pairs, s.near, s.slab)
    ]
    hbm = pl.BlockSpec(memory_space=pltpu.HBM)
    a_own, own = (pltpu.with_memory_space_constraint(x, pltpu.HBM) for x in (a_own, rows[0]))
    operands = [a_own, a_other, own, *rows[1:], *near[1:]]
    return pl.pallas_call(
        functools.partial(product_kernel, s),
        in_specs=[smem, smem, hbm, anywhere, hbm] + [anywhere] * (len(operands) - 3),
        out_specs=[vmem, vmem],
        out_shape=[jax.ShapeDtypeStruct(*shape) for shape in shapes[:2]],
        scratch_shapes=[pltpu.VMEM(*shape) for shape in shapes[2:]]
        + [pltpu.SemaphoreType.DMA((len(operands) + 1,))],
        compiler_params=pltpu.CompilerParams(vmem_limit_bytes=room(*shapes)),
        cost_estimate=pl.CostEstimate(
            flops=s.pairs * s.side**3, bytes_accessed=1 << 20, transcendentals=0
        ),
    )(plan, starts, *operands)


def sum_kernel(
    s, plan_ref, starts_ref, slots_ref, rows_ref, far0, far1,
    send0, keep0, send1, keep1, send2, keep2, total, far_buf, sems,
):
    hi = pl.program_id(0)
    copies = [
        pltpu.make_async_copy(ref, far_buf.at[pl.ds(k * s.tiles, s.tiles)], sems.at[k])
        for k, ref in enumerate((far0, far1))
    ]

    @pl.when(hi == 0)
    def _():
        for copy in copies:
            copy.start()

    def clear(k, carry):
        total[k] = jnp.zeros(total.shape[1:], jnp.float32)
        return carry

    lax.fori_loop(0, s.blocks, clear, 0)

    def add(n, product):
        entry = plan_ref[n]
        known = jnp.maximum(entry, 0)
        term = jnp.dot(
            rows_ref[known & (s.slab - 1)], product, preferred_element_type=jnp.float32
        )
        cell = field(s, known, 2)
        at = pl.ds(pl.multiple_of((cell & (s.per - 1)) * s.side, s.side), s.side)
        total[cell >> log2(s.per), at, :] += jnp.where(entry >= 0, term, 0.0)

    def near(group, carry):
        for u in range(UNROLL):
            n = group * UNROLL + u
            add(n, slots_ref[n])
        return carry

    def far(group, carry):
        for u in range(UNROLL):
            n = group * UNROLL + u
            piece = far_buf[field(s, jnp.maximum(plan_ref[n], 0), 1)]
            product = jnp.dot(slots_ref[n], piece, preferred_element_type=jnp.float32)
            add(n, product.astype(jnp.bfloat16))
        return carry

    begin = starts_ref[2 * hi] // UNROLL
    middle = starts_ref[2 * hi + 1] // UNROLL
    end = starts_ref[2 * hi + 2] // UNROLL
    lax.fori_loop(begin, middle, near, 0)

    @pl.when(hi == 0)
    def _():
        for copy in copies:
            copy.wait()

    lax.fori_loop(middle, end, far, 0)

    half = s.cols // 2
    weight = {"x": 1, "y": half, "1": 2 * half, "2": 4 * half}
    core = lax.axis_index("col") & 1
    outs = ((send0, keep0), (send1, keep1), (send2, keep2))
    for k, (send, keep) in enumerate(outs):
        for bits in itertools.product(range(2), repeat=4):
            base = [
                sum(weight[link] * bit for link, bit in zip(order, bits)) for order in ORDERS[k]
            ]
            base = jnp.where(core == 0, *base)
            for x in range(half // 2):
                part = total[base + 2 * x, s.splits[k]:s.splits[k + 1], :]
                if bits[0]:
                    send[(*bits[1:], 0, x)] = part.astype(jnp.bfloat16)
                else:
                    keep[(*bits[1:], 0, x)] = part


def make_sums(s, plan, starts, slots, rows_t, far):
    smem = pl.BlockSpec(memory_space=pltpu.SMEM)
    vmem = pl.BlockSpec(memory_space=pltpu.VMEM)
    anywhere = pl.BlockSpec(memory_space=pl.ANY)
    shapes = [
        ((s.slots + s.slab + 2 * s.tiles, s.side, s.side), jnp.bfloat16),
        ((s.blocks, s.tall, s.side), jnp.float32),
    ]
    out_shape, out_specs = [], []
    for k in range(len(ORDERS)):
        last = (s.cols // 4, s.splits[k + 1] - s.splits[k], s.side)
        for dtype in (jnp.bfloat16, jnp.float32):
            out_shape.append(jax.ShapeDtypeStruct((2, 2, 2, s.his) + last, dtype))
            out_specs.append(
                pl.BlockSpec((2, 2, 2, 1) + last, lambda h: (0, 0, 0, h, 0, 0, 0))
            )
            shapes.append(((2 if s.his > 1 else 1, 8) + last, dtype))
    return pl.pallas_call(
        functools.partial(sum_kernel, s),
        grid=(s.his,),
        in_specs=[smem, smem, vmem, vmem, anywhere, anywhere],
        out_specs=out_specs,
        out_shape=out_shape,
        scratch_shapes=[
            pltpu.VMEM((s.blocks, s.tall, s.side), jnp.float32),
            pltpu.VMEM((2 * s.tiles, s.side, s.side), jnp.bfloat16),
            pltpu.SemaphoreType.DMA((2,)),
        ],
        compiler_params=pltpu.CompilerParams(vmem_limit_bytes=room(*shapes)),
        cost_estimate=pl.CostEstimate(
            flops=s.pairs * s.side**3, bytes_accessed=16 << 20, transcendentals=0
        ),
    )(plan, starts, slots, rows_t, *far)


def shards(a_blocks, p_tiles, owner, agg_local, a_cols):
    s = Sizes(
        lax.axis_size("row"), lax.axis_size("col"), p_tiles.shape[0], p_tiles.shape[1]
    )
    order = ring_order(s.rows)
    barrier = lax.optimization_barrier

    def ring(value, stream):
        moves = []
        for k in range(s.rows):
            for c in range(s.cols):
                step = 1 if (stream + c) % 2 == 0 else -1
                to = order[(k + step) % s.rows]
                moves.append((order[k] * s.cols + c, to * s.cols + c))
        return lax.ppermute(value, ("row", "col"), moves)

    first = ring(p_tiles, 0)
    cols = a_cols[:, 0]
    cols_other = swap(cols, "col", 1)
    cols_other, mine = barrier((cols_other, p_tiles))
    second = ring(mine, 1)
    a_other, p_other = swap(a_blocks[:, 0], "col", 1), swap(p_tiles, "col", 1)

    aggs = owner[:, 0] * OWN + agg_local
    aggs, a_other, p_other, one, two, mine = barrier(
        (aggs, a_other, p_other, first, second, p_tiles)
    )
    own_near, other_near = {0: p_tiles, s.rows - 1: one, 1: two}, {0: p_other}
    first, second = ring(first, 0), ring(second, 1)
    aggs = [aggs] + [swap(aggs, "row", mask) for mask in (1, 2, 3)]
    second, aggs = barrier((second, jnp.concatenate(aggs, 0)))
    rows = [mine]
    bit = 2
    while bit < s.cols:
        rows += [swap(piece, "col", bit) for piece in rows]
        bit *= 2
    bit = 4
    while bit < s.rows:
        aggs = jnp.concatenate([aggs, swap(aggs, "row", bit)], 0)
        bit *= 2
    plan, starts = make_plan(s, jnp.concatenate([cols, cols_other], 0), aggs)

    held = [1, s.rows - 1]
    for step in range(2, s.half - 1):
        came, *rest = barrier((second, *(own_near[away] for away in held), *rows[1:]))
        for away, piece in zip(held, rest):
            other_near[away] = swap(piece, "col", 1)
        if step == 2:
            rows += [p_other] + [swap(piece, "col", 1) for piece in rest[len(held):]]
        own_near[s.rows - step], own_near[step] = first, came
        first, second = ring(first, 0), ring(second, 1)
        held = [step, s.rows - step]

    others = sorted(set(other_near) - {0})
    tie = (first, second, plan, starts)
    tie += (*(own_near[away] for away in held), *(other_near[away] for away in others))
    first, second, plan, starts, *rest = barrier(tie)
    for away, piece in zip(others, rest[len(held):]):
        other_near[away] = piece
    far = ring(first, 0)
    own_near[s.half + 1], own_near[s.half - 1] = first, second
    for away, piece in zip(held, rest):
        other_near[away] = swap(piece, "col", 1)
    for away in (s.half + 1, s.half - 1):
        other_near[away] = swap(own_near[away], "col", 1)
    near = [own_near[k] for k in sorted(own_near)]
    near += [other_near[k] for k in sorted(other_near)]
    slots, rows_t = make_products(s, plan, starts, a_blocks[:, 0], a_other, near, rows)
    far, slots, rows_t = barrier((far, slots, rows_t))
    far_other = swap(far, "col", 1)
    parts = make_sums(s, plan, starts, slots, rows_t, [far, far_other])

    sends, keeps = list(parts[0::2]), list(parts[1::2])
    groups = range(len(ORDERS))
    moving = [exchange(sends[k], [order[0] for order in ORDERS[k]]) for k in groups]
    for step in range(1, 5):
        for k in groups:
            got = moving[k]
            if step < 4:
                send = (keeps[k][1] + got[1].astype(jnp.float32)).astype(jnp.bfloat16)
                moving[k] = exchange(send, [order[step] for order in ORDERS[k]])
                keeps[k] = keeps[k][0] + got[0].astype(jnp.float32)
            else:
                keeps[k] = keeps[k] + got.astype(jnp.float32)
    total = jnp.concatenate(keeps, -2)
    tail = [("row", 1 << k) for k in range(3, log2(s.rows))][::-1]
    tail += [("col", 1 << k) for k in range(2, log2(s.cols))][::-1]
    total = total.reshape((2,) * len(tail) + total.shape[-2:])
    for axis in tail:
        got = swap(total[1].astype(jnp.bfloat16), *axis)
        total = total[0] + got.astype(jnp.float32)
    return total.reshape(OWN, s.width, s.side, s.side)


def solution(mesh):
    in_specs = (
        P("row", "col", None, None),
        P(("row", "col"), None, None),
        P("row", None),
        P("row"),
        P("row", "col"),
    )
    out_specs = P("row", "col", None, None)
    return jax.shard_map(shards, mesh=mesh, in_specs=in_specs, out_specs=out_specs, check_vma=False)
```

```python
import functools
import itertools
import math

import jax
import jax.numpy as jnp
from jax import lax
from jax.experimental import pallas as pl
from jax.experimental.pallas import tpu as pltpu
from jax.sharding import PartitionSpec as P

OWN = 2
UNROLL = 8
ORDERS = (("1x2y", "x1y2"), ("xy12", "yx21"), ("y1x2", "2xy1"))
LINKS = {"x": ("col", 2), "y": ("row", 1), "1": ("row", 2), "2": ("row", 4)}


def ring_order(count):
    return list(range(0, count, 2)) + list(range(1, count, 2))[::-1]


def swap(value, axis, bit):
    size = lax.axis_size(axis)
    return lax.ppermute(value, axis, [(i, i ^ bit) for i in range(size)])


def exchange(value, links):
    rows, cols = lax.axis_size("row"), lax.axis_size("col")
    moves = []
    for r in range(rows):
        for c in range(cols):
            axis, bit = LINKS[links[c % 2]]
            to = (r ^ bit, c) if axis == "row" else (r, c ^ bit)
            moves.append((r * cols + c, to[0] * cols + to[1]))
    return lax.ppermute(value, ("row", "col"), moves)


def log2(size):
    power = size.bit_length() - 1
    assert size == 1 << power
    return power


class Sizes:
    def __init__(self, rows, cols, tiles, side):
        self.rows, self.cols, self.tiles, self.side = rows, cols, tiles, side
        self.slab = cols * tiles
        self.pairs = 2 * self.slab
        self.width = OWN * rows // cols
        self.per = OWN * self.width
        self.his = rows // 8
        self.blocks, self.tall = 4 * cols, self.per * side
        third = self.tall // 16 // 3 * 16
        self.splits = (0, third, 2 * third, self.tall)
        self.buckets = 2 * self.his
        self.slots = self.pairs + self.buckets * UNROLL
        self.half = rows // 2
        self.early = rows - 1
        self.near = 2 * self.early * tiles
        self.fields, shift = [], 0
        for size in (self.pairs, 2 * rows * tiles, self.blocks * self.per):
            self.fields.append((shift, size - 1))
            shift += log2(size)
        assert shift <= 31


def field(s, entry, k):
    shift, mask = s.fields[k]
    return (entry >> shift) & mask


def plan_kernel(s, cols_ref, aggs_ref, plan_ref, starts_ref, info, counts):
    row = lax.axis_index("row")
    col = lax.axis_index("col")

    def ring_place(index):
        return jnp.where((index & 1) == 0, index >> 1, s.rows - 1 - (index >> 1))

    here = ring_place(row)
    for b in range(s.buckets):
        counts[b] = 0

    def blank(k, carry):
        plan_ref[k] = -1
        return carry

    lax.fori_loop(0, s.slots + 1, blank, 0, unroll=8)

    def sort(i, carry):
        tile = i & (s.slab - 1)
        side = i >> log2(s.slab)
        other = cols_ref[i]
        other_row = other >> log2(s.slab)
        i_agg = aggs_ref[tile]
        j_agg = aggs_ref[((other_row ^ row) << log2(s.slab)) + (other & (s.slab - 1))]
        rel_col = (j_agg >> log2(s.width)) ^ col
        rel_row = (i_agg >> log2(OWN)) ^ row
        turn = ring_place(other_row) - here
        away = jnp.where(((col ^ side) & 1) == 0, turn, -turn) & (s.rows - 1)
        late = jnp.where(away == s.half, 1, 0)
        order = away - jnp.where(away > s.half, 1, 0) + side * s.early
        piece = jnp.where(late == 1, side, order)
        panel_at = (piece << log2(s.tiles)) + (other & (s.tiles - 1))
        cell = (rel_row & 7) * (s.cols // 2) + (rel_col >> 1)
        cell = (cell << log2(OWN)) + (i_agg & (OWN - 1))
        cell = (cell << log2(s.width)) + (j_agg & (s.width - 1))
        bucket = (rel_row >> 3) * 2 + late
        mine = (rel_col & 1) == 0
        rank = counts[bucket]
        counts[bucket] = rank + jnp.where(mine, 1, 0)
        info[i * 2] = jnp.where(mine, rank * s.buckets + bucket, -1)
        entry = i
        for k, value in enumerate((panel_at, cell)):
            entry = entry + (value << s.fields[k + 1][0])
        info[i * 2 + 1] = entry
        return carry

    lax.fori_loop(0, s.pairs, sort, 0, unroll=4)

    start = jnp.int32(0)
    for b in range(s.buckets):
        starts_ref[b] = start
        start = start + ((counts[b] + UNROLL - 1) & ~(UNROLL - 1))
    starts_ref[s.buckets] = start

    def place(i, carry):
        key = info[i * 2]
        slot = starts_ref[key & (s.buckets - 1)] + (key >> log2(s.buckets))
        plan_ref[jnp.where(key >= 0, slot, s.slots)] = info[i * 2 + 1]
        return carry

    lax.fori_loop(0, s.pairs, place, 0, unroll=4)


def room(*shapes):
    total = sum(math.prod(shape) * jnp.dtype(dtype).itemsize for shape, dtype in shapes)
    return total + (2 << 20)


def make_plan(s, cols, aggs):
    smem = pl.BlockSpec(memory_space=pltpu.SMEM)
    return pl.pallas_call(
        functools.partial(plan_kernel, s),
        in_specs=[smem, smem],
        out_specs=[smem, smem],
        out_shape=[
            jax.ShapeDtypeStruct((s.slots + 1,), jnp.int32),
            jax.ShapeDtypeStruct((s.buckets + 1,), jnp.int32),
        ],
        scratch_shapes=[
            pltpu.SMEM((s.pairs * 2,), jnp.int32),
            pltpu.SMEM((s.buckets,), jnp.int32),
        ],
        compiler_params=pltpu.CompilerParams(vmem_limit_bytes=room()),
        cost_estimate=pl.CostEstimate(flops=1 << 20, bytes_accessed=16 << 20, transcendentals=0),
    )(cols, aggs)


def product_kernel(s, plan_ref, starts_ref, *refs):
    slots_ref, rows_ref, a_buf, panel, rows_buf, sems = refs[-6:]
    copies = []
    for k in range(2):
        copies.append((refs[k], a_buf.at[pl.ds(k * s.slab, s.slab)]))
    for k in range(s.cols):
        copies.append((refs[2 + k], rows_buf.at[pl.ds(k * s.tiles, s.tiles)]))
    for k in range(2 * s.early):
        source = refs[2] if k == 0 else refs[1 + s.cols + k]
        copies.append((source, panel.at[pl.ds(k * s.tiles, s.tiles)]))
    copies = [pltpu.make_async_copy(src, dst, sems.at[k]) for k, (src, dst) in enumerate(copies)]
    for copy in copies:
        copy.start()
    for copy in copies:
        copy.wait()

    col = lax.axis_index("col")

    def turn(k, carry):
        part = k >> log2(s.tiles)
        rel = (part & (s.cols // 2 - 1)) * 2 + (part >> log2(s.cols // 2))
        rows_ref[((rel ^ col) << log2(s.tiles)) + (k & (s.tiles - 1))] = rows_buf[k].T
        return carry

    lax.fori_loop(0, s.slab, turn, 0, unroll=4)

    for hi in range(s.his):
        begin = starts_ref[2 * hi] // UNROLL
        middle = starts_ref[2 * hi + 1] // UNROLL
        end = starts_ref[2 * hi + 2] // UNROLL

        def near(group, carry):
            for u in range(UNROLL):
                n = group * UNROLL + u
                entry = jnp.maximum(plan_ref[n], 0)
                slots_ref[n] = jnp.dot(
                    a_buf[field(s, entry, 0)],
                    panel[field(s, entry, 1)],
                    preferred_element_type=jnp.float32,
                ).astype(jnp.bfloat16)
            return carry

        def far(group, carry):
            for u in range(UNROLL):
                n = group * UNROLL + u
                slots_ref[n] = a_buf[field(s, jnp.maximum(plan_ref[n], 0), 0)]
            return carry

        lax.fori_loop(begin, middle, near, 0)
        lax.fori_loop(middle, end, far, 0)


def make_products(s, plan, starts, a_own, a_other, near, rows):
    smem = pl.BlockSpec(memory_space=pltpu.SMEM)
    vmem = pl.BlockSpec(memory_space=pltpu.VMEM)
    anywhere = pl.BlockSpec(memory_space=pl.ANY)
    shapes = [
        ((count, s.side, s.side), jnp.bfloat16)
        for count in (s.slots, s.slab, s.pairs, s.near, s.slab)
    ]
    hbm = pl.BlockSpec(memory_space=pltpu.HBM)
    a_own, own = (pltpu.with_memory_space_constraint(x, pltpu.HBM) for x in (a_own, rows[0]))
    operands = [a_own, a_other, own, *rows[1:], *near[1:]]
    return pl.pallas_call(
        functools.partial(product_kernel, s),
        in_specs=[smem, smem, hbm, anywhere, hbm] + [anywhere] * (len(operands) - 3),
        out_specs=[vmem, vmem],
        out_shape=[jax.ShapeDtypeStruct(*shape) for shape in shapes[:2]],
        scratch_shapes=[pltpu.VMEM(*shape) for shape in shapes[2:]]
        + [pltpu.SemaphoreType.DMA((len(operands) + 1,))],
        compiler_params=pltpu.CompilerParams(vmem_limit_bytes=room(*shapes)),
        cost_estimate=pl.CostEstimate(
            flops=s.pairs * s.side**3, bytes_accessed=1 << 20, transcendentals=0
        ),
    )(plan, starts, *operands)


def sum_kernel(
    s, plan_ref, starts_ref, slots_ref, rows_ref, far0, far1,
    send0, keep0, send1, keep1, send2, keep2, total, far_buf, sems,
):
    hi = pl.program_id(0)
    copies = [
        pltpu.make_async_copy(ref, far_buf.at[pl.ds(k * s.tiles, s.tiles)], sems.at[k])
        for k, ref in enumerate((far0, far1))
    ]

    @pl.when(hi == 0)
    def _():
        for copy in copies:
            copy.start()

    def clear(k, carry):
        total[k] = jnp.zeros(total.shape[1:], jnp.float32)
        return carry

    lax.fori_loop(0, s.blocks, clear, 0)

    def add(n, product):
        entry = plan_ref[n]
        known = jnp.maximum(entry, 0)
        term = jnp.dot(
            rows_ref[known & (s.slab - 1)], product, preferred_element_type=jnp.float32
        )
        cell = field(s, known, 2)
        at = pl.ds(pl.multiple_of((cell & (s.per - 1)) * s.side, s.side), s.side)
        total[cell >> log2(s.per), at, :] += jnp.where(entry >= 0, term, 0.0)

    def near(group, carry):
        for u in range(UNROLL):
            n = group * UNROLL + u
            add(n, slots_ref[n])
        return carry

    def far(group, carry):
        for u in range(UNROLL):
            n = group * UNROLL + u
            piece = far_buf[field(s, jnp.maximum(plan_ref[n], 0), 1)]
            product = jnp.dot(slots_ref[n], piece, preferred_element_type=jnp.float32)
            add(n, product.astype(jnp.bfloat16))
        return carry

    begin = starts_ref[2 * hi] // UNROLL
    middle = starts_ref[2 * hi + 1] // UNROLL
    end = starts_ref[2 * hi + 2] // UNROLL
    lax.fori_loop(begin, middle, near, 0)

    @pl.when(hi == 0)
    def _():
        for copy in copies:
            copy.wait()

    lax.fori_loop(middle, end, far, 0)

    half = s.cols // 2
    weight = {"x": 1, "y": half, "1": 2 * half, "2": 4 * half}
    core = lax.axis_index("col") & 1
    outs = ((send0, keep0), (send1, keep1), (send2, keep2))
    for k, (send, keep) in enumerate(outs):
        for bits in itertools.product(range(2), repeat=4):
            base = [
                sum(weight[link] * bit for link, bit in zip(order, bits)) for order in ORDERS[k]
            ]
            base = jnp.where(core == 0, *base)
            for x in range(half // 2):
                part = total[base + 2 * x, s.splits[k]:s.splits[k + 1], :]
                if bits[0]:
                    send[(*bits[1:], 0, x)] = part.astype(jnp.bfloat16)
                else:
                    keep[(*bits[1:], 0, x)] = part


def make_sums(s, plan, starts, slots, rows_t, far):
    smem = pl.BlockSpec(memory_space=pltpu.SMEM)
    vmem = pl.BlockSpec(memory_space=pltpu.VMEM)
    anywhere = pl.BlockSpec(memory_space=pl.ANY)
    shapes = [
        ((s.slots + s.slab + 2 * s.tiles, s.side, s.side), jnp.bfloat16),
        ((s.blocks, s.tall, s.side), jnp.float32),
    ]
    out_shape, out_specs = [], []
    for k in range(len(ORDERS)):
        last = (s.cols // 4, s.splits[k + 1] - s.splits[k], s.side)
        for dtype in (jnp.bfloat16, jnp.float32):
            out_shape.append(jax.ShapeDtypeStruct((2, 2, 2, s.his) + last, dtype))
            out_specs.append(
                pl.BlockSpec((2, 2, 2, 1) + last, lambda h: (0, 0, 0, h, 0, 0, 0))
            )
            shapes.append(((2 if s.his > 1 else 1, 8) + last, dtype))
    return pl.pallas_call(
        functools.partial(sum_kernel, s),
        grid=(s.his,),
        in_specs=[smem, smem, vmem, vmem, anywhere, anywhere],
        out_specs=out_specs,
        out_shape=out_shape,
        scratch_shapes=[
            pltpu.VMEM((s.blocks, s.tall, s.side), jnp.float32),
            pltpu.VMEM((2 * s.tiles, s.side, s.side), jnp.bfloat16),
            pltpu.SemaphoreType.DMA((2,)),
        ],
        compiler_params=pltpu.CompilerParams(vmem_limit_bytes=room(*shapes)),
        cost_estimate=pl.CostEstimate(
            flops=s.pairs * s.side**3, bytes_accessed=16 << 20, transcendentals=0
        ),
    )(plan, starts, slots, rows_t, *far)


def shards(a_blocks, p_tiles, owner, agg_local, a_cols):
    s = Sizes(
        lax.axis_size("row"), lax.axis_size("col"), p_tiles.shape[0], p_tiles.shape[1]
    )
    order = ring_order(s.rows)
    barrier = lax.optimization_barrier

    def ring(value, stream):
        moves = []
        for k in range(s.rows):
            for c in range(s.cols):
                step = 1 if (stream + c) % 2 == 0 else -1
                to = order[(k + step) % s.rows]
                moves.append((order[k] * s.cols + c, to * s.cols + c))
        return lax.ppermute(value, ("row", "col"), moves)

    first = ring(p_tiles, 0)
    cols = a_cols[:, 0]
    cols_other = swap(cols, "col", 1)
    cols_other, mine = barrier((cols_other, p_tiles))
    second = ring(mine, 1)
    a_other, p_other = swap(a_blocks[:, 0], "col", 1), swap(p_tiles, "col", 1)

    aggs = owner[:, 0] * OWN + agg_local
    came, aggs, a_other, p_other = barrier((first, aggs, a_other, p_other))
    first = ring(first, 0)
    aggs = [aggs] + [swap(aggs, "row", mask) for mask in (1, 2, 3)]
    own_near, other_near = {0: p_tiles, s.rows - 1: came, 1: second}, {0: p_other}
    second = ring(second, 1)
    aggs, mine = barrier((jnp.concatenate(aggs, 0), p_tiles))
    bit = 4
    while bit < s.rows:
        aggs = jnp.concatenate([aggs, swap(aggs, "row", bit)], 0)
        bit *= 2
    rows = [mine]
    bit = 2
    while bit < s.cols:
        rows += [swap(piece, "col", bit) for piece in rows]
        bit *= 2
    plan, starts = make_plan(s, jnp.concatenate([cols, cols_other], 0), aggs)

    held = [1, s.rows - 1]
    for step in range(2, s.half - 1):
        came, *rest = barrier((second, *(own_near[away] for away in held), *rows[1:]))
        for away, piece in zip(held, rest):
            other_near[away] = swap(piece, "col", 1)
        if step == 2:
            rows += [p_other] + [swap(piece, "col", 1) for piece in rest[len(held):]]
        own_near[s.rows - step], own_near[step] = first, came
        first, second = ring(first, 0), ring(second, 1)
        held = [step, s.rows - step]

    others = sorted(set(other_near) - {0})
    tie = (first, second, plan, starts, *rows[s.cols // 2 + 1:])
    tie += (*(own_near[away] for away in held), *(other_near[away] for away in others))
    first, second, plan, starts, *rest = barrier(tie)
    rows[s.cols // 2 + 1:] = rest[:s.cols // 2 - 1]
    rest = rest[s.cols // 2 - 1:]
    for away, piece in zip(others, rest[len(held):]):
        other_near[away] = piece
    far = ring(first, 0)
    own_near[s.half + 1], own_near[s.half - 1] = first, second
    for away, piece in zip(held, rest):
        other_near[away] = swap(piece, "col", 1)
    for away in (s.half + 1, s.half - 1):
        other_near[away] = swap(own_near[away], "col", 1)
    near = [own_near[k] for k in sorted(own_near)]
    near += [other_near[k] for k in sorted(other_near)]
    slots, rows_t = make_products(s, plan, starts, a_blocks[:, 0], a_other, near, rows)
    far, slots, rows_t = barrier((far, slots, rows_t))
    far_other = swap(far, "col", 1)
    parts = make_sums(s, plan, starts, slots, rows_t, [far, far_other])

    sends, keeps = list(parts[0::2]), list(parts[1::2])
    groups = range(len(ORDERS))
    moving = [exchange(sends[k], [order[0] for order in ORDERS[k]]) for k in groups]
    for step in range(1, 5):
        for k in groups:
            got = moving[k]
            if step < 4:
                send = (keeps[k][1] + got[1].astype(jnp.float32)).astype(jnp.bfloat16)
                moving[k] = exchange(send, [order[step] for order in ORDERS[k]])
                keeps[k] = keeps[k][0] + got[0].astype(jnp.float32)
            else:
                keeps[k] = keeps[k] + got.astype(jnp.float32)
    total = jnp.concatenate(keeps, -2)
    tail = [("row", 1 << k) for k in range(3, log2(s.rows))][::-1]
    tail += [("col", 1 << k) for k in range(2, log2(s.cols))][::-1]
    total = total.reshape((2,) * len(tail) + total.shape[-2:])
    for axis in tail:
        got = swap(total[1].astype(jnp.bfloat16), *axis)
        total = total[0] + got.astype(jnp.float32)
    return total.reshape(OWN, s.width, s.side, s.side)


def solution(mesh):
    in_specs = (
        P("row", "col", None, None),
        P(("row", "col"), None, None),
        P("row", None),
        P("row"),
        P("row", "col"),
    )
    out_specs = P("row", "col", None, None)
    return jax.shard_map(shards, mesh=mesh, in_specs=in_specs, out_specs=out_specs, check_vma=False)
```

```python
import functools
import itertools
import math

import jax
import jax.numpy as jnp
from jax import lax
from jax.experimental import pallas as pl
from jax.experimental.pallas import tpu as pltpu
from jax.sharding import PartitionSpec as P

OWN = 2
UNROLL = 8
LOOK_BITS = 12
ORDERS = (("1x2y", "x1y2"), ("xy12", "yx21"), ("y1x2", "2xy1"))
LINKS = {"x": ("col", 2), "y": ("row", 1), "1": ("row", 2), "2": ("row", 4)}


def ring_order(count):
    return list(range(0, count, 2)) + list(range(1, count, 2))[::-1]


def swap(value, axis, bit):
    size = lax.axis_size(axis)
    return lax.ppermute(value, axis, [(i, i ^ bit) for i in range(size)])


def exchange(value, links):
    rows, cols = lax.axis_size("row"), lax.axis_size("col")
    moves = []
    for r in range(rows):
        for c in range(cols):
            axis, bit = LINKS[links[c % 2]]
            to = (r ^ bit, c) if axis == "row" else (r, c ^ bit)
            moves.append((r * cols + c, to[0] * cols + to[1]))
    return lax.ppermute(value, ("row", "col"), moves)


def log2(size):
    power = size.bit_length() - 1
    assert size == 1 << power
    return power


class Sizes:
    def __init__(self, rows, cols, tiles, side):
        self.rows, self.cols, self.tiles, self.side = rows, cols, tiles, side
        self.slab = cols * tiles
        self.pairs = 2 * self.slab
        self.width = OWN * rows // cols
        self.per = OWN * self.width
        self.his = rows // 8
        self.blocks, self.tall = 4 * cols, self.per * side
        third = self.tall // 16 // 3 * 16
        self.splits = (0, third, 2 * third, self.tall)
        self.buckets = 2 * self.his
        self.slots = self.pairs + self.buckets * UNROLL
        self.half = rows // 2
        self.early = rows - 1
        self.near = 2 * self.early * tiles
        self.fields, shift = [], 0
        for size in (self.pairs, 2 * rows * tiles, self.blocks * self.per):
            self.fields.append((shift, size - 1))
            shift += log2(size)
        assert shift <= 31


def field(s, entry, k):
    shift, mask = s.fields[k]
    return (entry >> shift) & mask


def column_part(s, j_agg, col):
    rel_col = (j_agg >> log2(s.width)) ^ col
    part = ((rel_col >> 1) << log2(s.per)) + (j_agg & (s.width - 1))
    return (rel_col & 1) == 0, part << s.fields[2][0]


def plan_kernel(s, cols_ref, aggs_ref, near_ref, late_ref, meta_ref, info, counts):
    row = lax.axis_index("row")
    col = lax.axis_index("col")

    def ring_place(index):
        return jnp.where((index & 1) == 0, index >> 1, s.rows - 1 - (index >> 1))

    here = ring_place(row)
    for b in range(s.buckets):
        counts[b] = 0

    def sort(i, carry):
        n_near, n_late = carry
        tile = i & (s.slab - 1)
        side = i >> log2(s.slab)
        other = cols_ref[i]
        i_agg = aggs_ref[tile]
        rel_row = (i_agg >> log2(OWN)) ^ row
        turn = ring_place(other >> log2(s.slab)) - here
        mine = jnp.where((col & 1) == 0, turn, -turn) & (s.rows - 1)
        away = jnp.where(((col ^ side) & 1) == 0, turn, -turn) & (s.rows - 1)
        late = jnp.where(away == s.half, 1, 0)
        order = away - jnp.where(away > s.half, 1, 0) + side * s.early
        piece = jnp.where(late == 1, side, order)
        panel_at = (piece << log2(s.tiles)) + (other & (s.tiles - 1))
        cell = ((rel_row & 7) << (log2(s.cols // 2) + log2(s.per))) + (
            (i_agg & (OWN - 1)) << log2(s.width)
        )
        entry = i + (panel_at << s.fields[1][0]) + (cell << s.fields[2][0])
        slab_at = mine - jnp.where(mine > s.half, 1, 0)
        look = jnp.where(late == 1, 0, slab_at << log2(s.slab)) + (other & (s.slab - 1))
        look = look + ((rel_row >> 3) << LOOK_BITS)
        bucket = (rel_row >> 3) * 2 + late
        counts[bucket] = counts[bucket] + 1
        near_ref[n_near * 2] = entry
        near_ref[n_near * 2 + 1] = look
        info[n_late * 2] = entry
        info[n_late * 2 + 1] = look
        return n_near + 1 - late, n_late + late

    zero = jnp.int32(0)
    n_near, n_late = lax.fori_loop(0, s.pairs, sort, (zero, zero), unroll=4)
    for u in range(4):
        near_ref[(n_near + u) * 2] = 0
        near_ref[(n_near + u) * 2 + 1] = 0

    start = zero
    for b in range(s.buckets):
        meta_ref[b] = start
        start = start + ((counts[b] + UNROLL - 1) & ~(UNROLL - 1))
    meta_ref[s.buckets] = start
    meta_ref[s.buckets + 1] = n_near
    for hi in range(s.his):
        meta_ref[s.buckets + 2 + hi] = counts[2 * hi + 1]
        for u in range(UNROLL):
            at = meta_ref[2 * hi + 1] + counts[2 * hi + 1] + u
            late_ref[jnp.where(at < meta_ref[2 * hi + 2], at, s.slots) * 2] = 0
        counts[2 * hi + 1] = 0

    def place(n, carry):
        look = info[n * 2 + 1]
        bucket = (look >> LOOK_BITS) * 2 + 1
        rank = counts[bucket]
        counts[bucket] = rank + 1
        slot = meta_ref[bucket] + rank
        late_ref[slot * 2] = info[n * 2]
        late_ref[slot * 2 + 1] = look & ((1 << LOOK_BITS) - 1)
        return carry

    lax.fori_loop(0, n_late, place, 0)


def room(*shapes):
    total = sum(math.prod(shape) * jnp.dtype(dtype).itemsize for shape, dtype in shapes)
    return total + (2 << 20)


def make_plan(s, cols, aggs):
    smem = pl.BlockSpec(memory_space=pltpu.SMEM)
    counts = (s.pairs * 2 + 8, (s.slots + 1) * 2, s.buckets + 2 + s.his)
    return pl.pallas_call(
        functools.partial(plan_kernel, s),
        in_specs=[smem, smem],
        out_specs=[smem, smem, smem],
        out_shape=[jax.ShapeDtypeStruct((count,), jnp.int32) for count in counts],
        scratch_shapes=[
            pltpu.SMEM((s.pairs * 2,), jnp.int32),
            pltpu.SMEM((s.buckets,), jnp.int32),
        ],
        compiler_params=pltpu.CompilerParams(vmem_limit_bytes=room()),
        cost_estimate=pl.CostEstimate(flops=1 << 20, bytes_accessed=16 << 20, transcendentals=0),
    )(cols, aggs)


def product_kernel(s, near_ref, late_ref, meta_ref, aggs_ref, *refs):
    slots_ref, rows_ref, plan_ref, counts, a_buf, rows_buf, panel, sems = refs[-8:]
    high = s.tiles * s.side
    copies = []
    for k in range(2):
        copies.append((refs[k], a_buf.at[pl.ds(k * s.slab, s.slab)]))
    for k in range(s.cols):
        copies.append((refs[2 + k], rows_buf.at[pl.ds(k * high, high)]))
    for k in range(2 * s.early):
        source = refs[2] if k == 0 else refs[1 + s.cols + k]
        copies.append((source.at[pl.ds(0, high)], panel.at[pl.ds(k * high, high)]))
    copies = [pltpu.make_async_copy(src, dst, sems.at[k]) for k, (src, dst) in enumerate(copies)]
    for copy in copies:
        copy.start()

    col = lax.axis_index("col")
    for hi in range(s.his):
        counts[hi] = 0
    n_near = meta_ref[s.buckets + 1]

    def pick(step, carry):
        for n in range(4):
            n = step * 4 + n
            look = near_ref[n * 2 + 1]
            hi = look >> LOOK_BITS
            mine, part = column_part(s, aggs_ref[look & ((1 << LOOK_BITS) - 1)], col)
            mine = mine & (n < n_near)
            rank = counts[hi]
            counts[hi] = rank + jnp.where(mine, 1, 0)
            plan_ref[jnp.where(mine, meta_ref[2 * hi] + rank, s.slots)] = near_ref[n * 2] + part
        return carry

    lax.fori_loop(0, pl.cdiv(n_near, 4), pick, 0)
    for hi in range(s.his):
        for u in range(UNROLL):
            at = meta_ref[2 * hi] + counts[hi] + u
            plan_ref[jnp.where(at < meta_ref[2 * hi + 1], at, s.slots)] = -1
    for copy in copies:
        copy.wait()

    def turn(k, carry):
        part = k >> log2(s.tiles)
        rel = (part & (s.cols // 2 - 1)) * 2 + (part >> log2(s.cols // 2))
        at = pl.ds(pl.multiple_of(k * s.side, s.side), s.side)
        rows_ref[((rel ^ col) << log2(s.tiles)) + (k & (s.tiles - 1))] = rows_buf[at, :].T
        return carry

    lax.fori_loop(0, s.slab, turn, 0, unroll=4)

    for hi in range(s.his):
        begin = meta_ref[2 * hi] // UNROLL
        middle = pl.cdiv(meta_ref[2 * hi] + counts[hi], UNROLL)

        def near(group, carry):
            for u in range(UNROLL):
                n = group * UNROLL + u
                entry = jnp.maximum(plan_ref[n], 0)
                at = pl.multiple_of(field(s, entry, 1) * s.side, s.side)
                slots_ref[n] = jnp.dot(
                    a_buf[field(s, entry, 0)],
                    panel[pl.ds(at, s.side), :],
                    preferred_element_type=jnp.float32,
                ).astype(jnp.bfloat16)
            return carry

        def far(group, carry):
            for u in range(UNROLL):
                n = group * UNROLL + u
                slots_ref[n] = a_buf[field(s, late_ref[n * 2], 0)]
            return carry

        lax.fori_loop(begin, middle, near, 0)
        lax.fori_loop(meta_ref[2 * hi + 1] // UNROLL, meta_ref[2 * hi + 2] // UNROLL, far, 0)


def make_products(s, plan, aggs, a_own, a_other, near, rows):
    smem = pl.BlockSpec(memory_space=pltpu.SMEM)
    vmem = pl.BlockSpec(memory_space=pltpu.VMEM)
    hbm = pl.BlockSpec(memory_space=pltpu.HBM)
    anywhere = pl.BlockSpec(memory_space=pl.ANY)
    block = (s.side, s.side)
    shapes = [((count,) + block, jnp.bfloat16) for count in (s.slots, s.slab, s.pairs)]
    shapes += [((count * s.side, s.side), jnp.bfloat16) for count in (s.slab, s.near)]
    a_own, own = (pltpu.with_memory_space_constraint(x, pltpu.HBM) for x in (a_own, rows[0]))
    operands = [a_own, a_other, own, *rows[1:], *near[1:]]
    return pl.pallas_call(
        functools.partial(product_kernel, s),
        in_specs=[smem] * 4 + [hbm, anywhere, hbm] + [anywhere] * (len(operands) - 3),
        out_specs=[vmem, vmem, smem, smem],
        out_shape=[jax.ShapeDtypeStruct(*shape) for shape in shapes[:2]]
        + [jax.ShapeDtypeStruct((count,), jnp.int32) for count in (s.slots + 1, s.his)],
        scratch_shapes=[pltpu.VMEM(*shape) for shape in shapes[2:]]
        + [pltpu.SemaphoreType.DMA((len(operands) + 1,))],
        compiler_params=pltpu.CompilerParams(vmem_limit_bytes=room(*shapes)),
        cost_estimate=pl.CostEstimate(
            flops=s.pairs * s.side**3, bytes_accessed=1 << 20, transcendentals=0
        ),
    )(*plan, aggs, *operands)


def sum_kernel(
    s, plan_ref, counts, late_ref, meta_ref, aggs_ref, slots_ref, rows_ref, far0, far1,
    send0, keep0, send1, keep1, send2, keep2, total, far_buf, picked, sems,
):
    hi = pl.program_id(0)
    high = s.tiles * s.side
    copies = [
        pltpu.make_async_copy(
            ref.at[pl.ds(0, high)], far_buf.at[pl.ds(k * high, high)], sems.at[k]
        )
        for k, ref in enumerate((far0, far1))
    ]

    @pl.when(hi == 0)
    def _():
        for copy in copies:
            copy.start()

    def clear(k, carry):
        total[k] = jnp.zeros(total.shape[1:], jnp.float32)
        return carry

    lax.fori_loop(0, s.blocks, clear, 0)

    def add(entry, product):
        known = jnp.maximum(entry, 0)
        term = jnp.dot(
            rows_ref[known & (s.slab - 1)], product, preferred_element_type=jnp.float32
        )
        cell = field(s, known, 2)
        at = pl.ds(pl.multiple_of((cell & (s.per - 1)) * s.side, s.side), s.side)
        total[cell >> log2(s.per), at, :] += jnp.where(entry >= 0, term, 0.0)

    def near(group, carry):
        for u in range(UNROLL):
            n = group * UNROLL + u
            add(plan_ref[n], slots_ref[n])
        return carry

    begin = meta_ref[2 * hi]
    lax.fori_loop(begin // UNROLL, pl.cdiv(begin + counts[hi], UNROLL), near, 0)

    col = lax.axis_index("col")
    first = meta_ref[2 * hi + 1]

    def pick(n, n_mine):
        slot = first + n
        mine, part = column_part(s, aggs_ref[late_ref[slot * 2 + 1]], col)
        picked[n_mine * 2] = slot
        picked[n_mine * 2 + 1] = late_ref[slot * 2] + part
        return n_mine + jnp.where(mine, 1, 0)

    n_mine = lax.fori_loop(0, meta_ref[s.buckets + 2 + hi], pick, jnp.int32(0))
    for u in range(UNROLL):
        picked[(n_mine + u) * 2] = 0
        picked[(n_mine + u) * 2 + 1] = -1

    @pl.when(hi == 0)
    def _():
        for copy in copies:
            copy.wait()

    def far(group, carry):
        for u in range(UNROLL):
            n = group * UNROLL + u
            slot, entry = picked[n * 2], picked[n * 2 + 1]
            at = field(s, jnp.maximum(entry, 0), 1) * s.side
            piece = far_buf[pl.ds(pl.multiple_of(at, s.side), s.side), :]
            product = jnp.dot(slots_ref[slot], piece, preferred_element_type=jnp.float32)
            add(entry, product.astype(jnp.bfloat16))
        return carry

    lax.fori_loop(0, pl.cdiv(n_mine, UNROLL), far, 0)

    half = s.cols // 2
    weight = {"x": 1, "y": half, "1": 2 * half, "2": 4 * half}
    core = lax.axis_index("col") & 1
    outs = ((send0, keep0), (send1, keep1), (send2, keep2))
    for k, (send, keep) in enumerate(outs):
        for bits in itertools.product(range(2), repeat=4):
            base = [
                sum(weight[link] * bit for link, bit in zip(order, bits)) for order in ORDERS[k]
            ]
            base = jnp.where(core == 0, *base)
            for x in range(half // 2):
                part = total[base + 2 * x, s.splits[k]:s.splits[k + 1], :]
                if bits[0]:
                    send[(*bits[1:], 0, x)] = part.astype(jnp.bfloat16)
                else:
                    keep[(*bits[1:], 0, x)] = part


def make_sums(s, lists, slots, rows_t, far):
    smem = pl.BlockSpec(memory_space=pltpu.SMEM)
    vmem = pl.BlockSpec(memory_space=pltpu.VMEM)
    anywhere = pl.BlockSpec(memory_space=pl.ANY)
    shapes = [
        ((s.slots + s.slab + 2 * s.tiles, s.side, s.side), jnp.bfloat16),
        ((s.blocks, s.tall, s.side), jnp.float32),
    ]
    out_shape, out_specs = [], []
    for k in range(len(ORDERS)):
        last = (s.cols // 4, s.splits[k + 1] - s.splits[k], s.side)
        for dtype in (jnp.bfloat16, jnp.float32):
            out_shape.append(jax.ShapeDtypeStruct((2, 2, 2, s.his) + last, dtype))
            out_specs.append(
                pl.BlockSpec((2, 2, 2, 1) + last, lambda h: (0, 0, 0, h, 0, 0, 0))
            )
            shapes.append(((2 if s.his > 1 else 1, 8) + last, dtype))
    return pl.pallas_call(
        functools.partial(sum_kernel, s),
        grid=(s.his,),
        in_specs=[smem] * 5 + [vmem, vmem, anywhere, anywhere],
        out_specs=out_specs,
        out_shape=out_shape,
        scratch_shapes=[
            pltpu.VMEM((s.blocks, s.tall, s.side), jnp.float32),
            pltpu.VMEM((2 * s.tiles * s.side, s.side), jnp.bfloat16),
            pltpu.SMEM(((s.pairs + UNROLL) * 2,), jnp.int32),
            pltpu.SemaphoreType.DMA((2,)),
        ],
        compiler_params=pltpu.CompilerParams(vmem_limit_bytes=room(*shapes)),
        cost_estimate=pl.CostEstimate(
            flops=s.pairs * s.side**3, bytes_accessed=16 << 20, transcendentals=0
        ),
    )(*lists, slots, rows_t, *far)


def shards(a_blocks, p_tiles, owner, agg_local, a_cols):
    s = Sizes(
        lax.axis_size("row"), lax.axis_size("col"), p_tiles.shape[0], p_tiles.shape[1]
    )
    order = ring_order(s.rows)
    barrier = lax.optimization_barrier

    def ring(value, stream):
        moves = []
        for k in range(s.rows):
            for c in range(s.cols):
                step = 1 if (stream + c) % 2 == 0 else -1
                to = order[(k + step) % s.rows]
                moves.append((order[k] * s.cols + c, to * s.cols + c))
        return lax.ppermute(value, ("row", "col"), moves)

    high = s.tiles * s.side
    aggs = owner[:, 0] * OWN + agg_local
    label = jnp.pad(aggs.astype(jnp.bfloat16)[None], ((0, 15), (0, s.side - s.slab)))
    mine = p_tiles.reshape(high, s.side)
    labelled = jnp.concatenate([mine, label], 0)

    def labels(piece):
        return piece[high, :s.slab].astype(jnp.int32)

    first = ring(labelled, 0)
    cols = a_cols[:, 0]
    cols_other = swap(cols, "col", 1)
    cols_other, labelled = barrier((cols_other, labelled))
    second = ring(labelled, 1)
    a_other, p_other = swap(a_blocks[:, 0], "col", 1), swap(mine, "col", 1)
    plan = make_plan(s, jnp.concatenate([cols, cols_other], 0), aggs)

    came, a_other, p_other, mine = barrier((first, a_other, p_other, mine))
    first = ring(first, 0)
    own_near, other_near = {0: labelled, s.rows - 1: came, 1: second}, {0: p_other}
    second = ring(second, 1)
    rows = [mine]
    bit = 2
    while bit < s.cols:
        rows += [swap(piece, "col", bit) for piece in rows]
        bit *= 2

    held = [1, s.rows - 1]
    for step in range(2, s.half - 1):
        came, *rest = barrier((second, *(own_near[away] for away in held), *rows[1:]))
        for away, piece in zip(held, rest):
            other_near[away] = swap(piece, "col", 1)
        if step == 2:
            rows += [p_other] + [swap(piece, "col", 1) for piece in rest[len(held):]]
        own_near[s.rows - step], own_near[step] = first, came
        first, second = ring(first, 0), ring(second, 1)
        held = [step, s.rows - step]

    others = sorted(set(other_near) - {0})
    tie = (first, second, *plan)
    tie += (*(own_near[away] for away in held), *(other_near[away] for away in others))
    first, second, *rest = barrier(tie)
    plan, rest = rest[:len(plan)], rest[len(plan):]
    for away, piece in zip(others, rest[len(held):]):
        other_near[away] = piece
    far = ring(first, 0)
    own_near[s.half + 1], own_near[s.half - 1] = first, second
    for away, piece in zip(held, rest):
        other_near[away] = swap(piece, "col", 1)
    for away in (s.half + 1, s.half - 1):
        other_near[away] = swap(own_near[away], "col", 1)
    near = [own_near[k] for k in sorted(own_near)]
    near_aggs = jnp.concatenate([labels(piece) for piece in near], 0)
    near += [other_near[k] for k in sorted(other_near)]
    slots, rows_t, picks, counts = make_products(
        s, plan, near_aggs, a_blocks[:, 0], a_other, near, rows
    )
    far, slots, rows_t = barrier((far, slots, rows_t))
    far_other = swap(far, "col", 1)
    lists = (picks, counts, plan[1], plan[2], labels(far))
    parts = make_sums(s, lists, slots, rows_t, [far, far_other])

    sends, keeps = list(parts[0::2]), list(parts[1::2])
    groups = range(len(ORDERS))
    moving = [exchange(sends[k], [order[0] for order in ORDERS[k]]) for k in groups]
    for step in range(1, 5):
        for k in groups:
            got = moving[k]
            if step < 4:
                send = (keeps[k][1] + got[1].astype(jnp.float32)).astype(jnp.bfloat16)
                moving[k] = exchange(send, [order[step] for order in ORDERS[k]])
                keeps[k] = keeps[k][0] + got[0].astype(jnp.float32)
            else:
                keeps[k] = keeps[k] + got.astype(jnp.float32)
    total = jnp.concatenate(keeps, -2)
    tail = [("row", 1 << k) for k in range(3, log2(s.rows))][::-1]
    tail += [("col", 1 << k) for k in range(2, log2(s.cols))][::-1]
    total = total.reshape((2,) * len(tail) + total.shape[-2:])
    for axis in tail:
        got = swap(total[1].astype(jnp.bfloat16), *axis)
        total = total[0] + got.astype(jnp.float32)
    return total.reshape(OWN, s.width, s.side, s.side)


def solution(mesh):
    in_specs = (
        P("row", "col", None, None),
        P(("row", "col"), None, None),
        P("row", None),
        P("row"),
        P("row", "col"),
    )
    out_specs = P("row", "col", None, None)
    return jax.shard_map(shards, mesh=mesh, in_specs=in_specs, out_specs=out_specs, check_vma=False)
```

```python
import functools
import itertools
import math

import jax
import jax.numpy as jnp
from jax import lax
from jax.experimental import pallas as pl
from jax.experimental.pallas import tpu as pltpu
from jax.sharding import PartitionSpec as P

OWN = 2
UNROLL = 8
LOOK_BITS = 12
LABEL = 16
ORDERS = (("1x2y", "x1y2"), ("xy12", "yx21"), ("y1x2", "2xy1"))
LINKS = {"x": ("col", 2), "y": ("row", 1), "1": ("row", 2), "2": ("row", 4)}


def ring_order(count):
    return list(range(0, count, 2)) + list(range(1, count, 2))[::-1]


def swap(value, axis, bit):
    size = lax.axis_size(axis)
    return lax.ppermute(value, axis, [(i, i ^ bit) for i in range(size)])


def exchange(value, links):
    rows, cols = lax.axis_size("row"), lax.axis_size("col")
    moves = []
    for r in range(rows):
        for c in range(cols):
            axis, bit = LINKS[links[c % 2]]
            to = (r ^ bit, c) if axis == "row" else (r, c ^ bit)
            moves.append((r * cols + c, to[0] * cols + to[1]))
    return lax.ppermute(value, ("row", "col"), moves)


def log2(size):
    power = size.bit_length() - 1
    assert size == 1 << power
    return power


class Sizes:
    def __init__(self, rows, cols, tiles, side):
        self.rows, self.cols, self.tiles, self.side = rows, cols, tiles, side
        self.slab = cols * tiles
        self.pairs = 2 * self.slab
        self.width = OWN * rows // cols
        self.per = OWN * self.width
        self.his = rows // 8
        self.blocks, self.tall = 4 * cols, self.per * side
        third = self.tall // 16 // 3 * 16
        self.splits = (0, third, 2 * third, self.tall)
        self.buckets = 2 * self.his
        self.slots = self.pairs + self.buckets * UNROLL
        self.half = rows // 2
        self.early = rows - 1
        self.near = 2 * self.early * tiles
        self.fields, shift = [], 0
        for size in (self.pairs, 2 * rows * tiles, self.blocks * self.per):
            self.fields.append((shift, size - 1))
            shift += log2(size)
        assert shift <= 31


def field(s, entry, k):
    shift, mask = s.fields[k]
    return (entry >> shift) & mask


def column_part(s, j_agg, col):
    rel_col = (j_agg >> log2(s.width)) ^ col
    part = ((rel_col >> 1) << log2(s.per)) + (j_agg & (s.width - 1))
    return (rel_col & 1) == 0, part << s.fields[2][0]


def plan_kernel(s, cols_ref, aggs_ref, near_ref, late_ref, meta_ref, info, counts):
    row = lax.axis_index("row")
    col = lax.axis_index("col")

    def ring_place(index):
        return jnp.where((index & 1) == 0, index >> 1, s.rows - 1 - (index >> 1))

    here = ring_place(row)
    for b in range(s.buckets):
        counts[b] = 0

    def sort(i, carry):
        n_near, n_late = carry
        tile = i & (s.slab - 1)
        side = i >> log2(s.slab)
        other = cols_ref[i]
        i_agg = aggs_ref[tile]
        rel_row = (i_agg >> log2(OWN)) ^ row
        turn = ring_place(other >> log2(s.slab)) - here
        mine = jnp.where((col & 1) == 0, turn, -turn) & (s.rows - 1)
        away = jnp.where(((col ^ side) & 1) == 0, turn, -turn) & (s.rows - 1)
        late = jnp.where(away == s.half, 1, 0)
        order = away - jnp.where(away > s.half, 1, 0) + side * s.early
        piece = jnp.where(late == 1, side, order)
        panel_at = (piece << log2(s.tiles)) + (other & (s.tiles - 1))
        cell = ((rel_row & 7) << (log2(s.cols // 2) + log2(s.per))) + (
            (i_agg & (OWN - 1)) << log2(s.width)
        )
        entry = i + (panel_at << s.fields[1][0]) + (cell << s.fields[2][0])
        slab_at = mine - jnp.where(mine > s.half, 1, 0)
        look = jnp.where(late == 1, 0, slab_at << log2(s.slab)) + (other & (s.slab - 1))
        look = look + ((rel_row >> 3) << LOOK_BITS)
        bucket = (rel_row >> 3) * 2 + late
        counts[bucket] = counts[bucket] + 1
        near_ref[n_near * 2] = entry
        near_ref[n_near * 2 + 1] = look
        info[n_late * 2] = entry
        info[n_late * 2 + 1] = look
        return n_near + 1 - late, n_late + late

    zero = jnp.int32(0)
    n_near, n_late = lax.fori_loop(0, s.pairs, sort, (zero, zero), unroll=4)
    for u in range(4):
        near_ref[(n_near + u) * 2] = 0
        near_ref[(n_near + u) * 2 + 1] = 0

    start = zero
    for b in range(s.buckets):
        meta_ref[b] = start
        start = start + ((counts[b] + UNROLL - 1) & ~(UNROLL - 1))
    meta_ref[s.buckets] = start
    meta_ref[s.buckets + 1] = n_near
    for hi in range(s.his):
        meta_ref[s.buckets + 2 + hi] = counts[2 * hi + 1]
        for u in range(UNROLL):
            at = meta_ref[2 * hi + 1] + counts[2 * hi + 1] + u
            late_ref[jnp.where(at < meta_ref[2 * hi + 2], at, s.slots) * 2] = 0
        counts[2 * hi + 1] = 0

    def place(n, carry):
        look = info[n * 2 + 1]
        bucket = (look >> LOOK_BITS) * 2 + 1
        rank = counts[bucket]
        counts[bucket] = rank + 1
        slot = meta_ref[bucket] + rank
        late_ref[slot * 2] = info[n * 2]
        late_ref[slot * 2 + 1] = look & ((1 << LOOK_BITS) - 1)
        return carry

    lax.fori_loop(0, n_late, place, 0)


def room(*shapes):
    total = sum(math.prod(shape) * jnp.dtype(dtype).itemsize for shape, dtype in shapes)
    return total + (2 << 20)


def make_plan(s, cols, aggs):
    smem = pl.BlockSpec(memory_space=pltpu.SMEM)
    counts = (s.pairs * 2 + 8, (s.slots + 1) * 2, s.buckets + 2 + s.his)
    return pl.pallas_call(
        functools.partial(plan_kernel, s),
        in_specs=[smem, smem],
        out_specs=[smem, smem, smem],
        out_shape=[jax.ShapeDtypeStruct((count,), jnp.int32) for count in counts],
        scratch_shapes=[
            pltpu.SMEM((s.pairs * 2,), jnp.int32),
            pltpu.SMEM((s.buckets,), jnp.int32),
        ],
        compiler_params=pltpu.CompilerParams(vmem_limit_bytes=room()),
        cost_estimate=pl.CostEstimate(flops=1 << 20, bytes_accessed=16 << 20, transcendentals=0),
    )(cols, aggs)


def product_kernel(s, near_ref, late_ref, meta_ref, *refs):
    slots_ref, rows_ref, plan_ref, counts = refs[-12:-8]
    a_buf, rows_buf, panel, label_buf, label_ints, labels, sems, label_sems = refs[-8:]
    high = s.tiles * s.side
    label_copies = [
        pltpu.make_async_copy(
            refs[2 + s.cols + k].at[pl.ds(high, LABEL)],
            label_buf.at[pl.ds(k * LABEL, LABEL)],
            label_sems.at[k],
        )
        for k in range(s.early)
    ]
    for copy in label_copies:
        copy.start()
    copies = []
    for k in range(2):
        copies.append((refs[k], a_buf.at[pl.ds(k * s.slab, s.slab)]))
    for k in range(s.cols):
        copies.append((refs[2 + k], rows_buf.at[pl.ds(k * high, high)]))
    for k in range(2 * s.early):
        source = refs[2 + s.cols + k]
        copies.append((source.at[pl.ds(0, high)], panel.at[pl.ds(k * high, high)]))
    copies = [pltpu.make_async_copy(src, dst, sems.at[k]) for k, (src, dst) in enumerate(copies)]
    for copy in copies:
        copy.start()

    col = lax.axis_index("col")
    for hi in range(s.his):
        counts[hi] = 0
    n_near = meta_ref[s.buckets + 1]
    for copy in label_copies:
        copy.wait()
    label_ints[...] = label_buf[...].astype(jnp.float32).astype(jnp.int32)
    copy = pltpu.make_async_copy(label_ints, labels, label_sems.at[s.early])
    copy.start()
    copy.wait()

    def pick(step, carry):
        for n in range(4):
            n = step * 4 + n
            look = near_ref[n * 2 + 1]
            hi = look >> LOOK_BITS
            slab = (look & ((1 << LOOK_BITS) - 1)) >> log2(s.slab)
            j_agg = labels[slab * LABEL, look & (s.slab - 1)]
            mine, part = column_part(s, j_agg, col)
            mine = mine & (n < n_near)
            rank = counts[hi]
            counts[hi] = rank + jnp.where(mine, 1, 0)
            plan_ref[jnp.where(mine, meta_ref[2 * hi] + rank, s.slots)] = near_ref[n * 2] + part
        return carry

    lax.fori_loop(0, pl.cdiv(n_near, 4), pick, 0)
    for hi in range(s.his):
        for u in range(UNROLL):
            at = meta_ref[2 * hi] + counts[hi] + u
            plan_ref[jnp.where(at < meta_ref[2 * hi + 1], at, s.slots)] = -1
    for copy in copies:
        copy.wait()

    def turn(k, carry):
        part = k >> log2(s.tiles)
        rel = (part & (s.cols // 2 - 1)) * 2 + (part >> log2(s.cols // 2))
        at = pl.ds(pl.multiple_of(k * s.side, s.side), s.side)
        rows_ref[((rel ^ col) << log2(s.tiles)) + (k & (s.tiles - 1))] = rows_buf[at, :].T
        return carry

    lax.fori_loop(0, s.slab, turn, 0, unroll=4)

    for hi in range(s.his):
        begin = meta_ref[2 * hi] // UNROLL
        middle = pl.cdiv(meta_ref[2 * hi] + counts[hi], UNROLL)

        def near(group, carry):
            for u in range(UNROLL):
                n = group * UNROLL + u
                entry = jnp.maximum(plan_ref[n], 0)
                at = pl.multiple_of(field(s, entry, 1) * s.side, s.side)
                slots_ref[n] = jnp.dot(
                    a_buf[field(s, entry, 0)],
                    panel[pl.ds(at, s.side), :],
                    preferred_element_type=jnp.float32,
                ).astype(jnp.bfloat16)
            return carry

        def far(group, carry):
            for u in range(UNROLL):
                n = group * UNROLL + u
                slots_ref[n] = a_buf[field(s, late_ref[n * 2], 0)]
            return carry

        lax.fori_loop(begin, middle, near, 0)
        lax.fori_loop(meta_ref[2 * hi + 1] // UNROLL, meta_ref[2 * hi + 2] // UNROLL, far, 0)


def make_products(s, plan, a_own, a_other, near, rows):
    smem = pl.BlockSpec(memory_space=pltpu.SMEM)
    vmem = pl.BlockSpec(memory_space=pltpu.VMEM)
    hbm = pl.BlockSpec(memory_space=pltpu.HBM)
    anywhere = pl.BlockSpec(memory_space=pl.ANY)
    block = (s.side, s.side)
    shapes = [((count,) + block, jnp.bfloat16) for count in (s.slots, s.slab, s.pairs)]
    shapes += [((count * s.side, s.side), jnp.bfloat16) for count in (s.slab, s.near)]
    a_own, own = (pltpu.with_memory_space_constraint(x, pltpu.HBM) for x in (a_own, rows[0]))
    operands = [a_own, a_other, own, *rows[1:], *near]
    label_shape = (s.early * LABEL, s.side)
    return pl.pallas_call(
        functools.partial(product_kernel, s),
        in_specs=[smem] * 3 + [hbm, anywhere, hbm] + [anywhere] * (len(operands) - 3),
        out_specs=[vmem, vmem, smem, smem],
        out_shape=[jax.ShapeDtypeStruct(*shape) for shape in shapes[:2]]
        + [jax.ShapeDtypeStruct((count,), jnp.int32) for count in (s.slots + 1, s.his)],
        scratch_shapes=[pltpu.VMEM(*shape) for shape in shapes[2:]]
        + [
            pltpu.VMEM(label_shape, jnp.bfloat16),
            pltpu.VMEM(label_shape, jnp.int32),
            pltpu.SMEM(label_shape, jnp.int32),
            pltpu.SemaphoreType.DMA((len(operands),)),
            pltpu.SemaphoreType.DMA((s.early + 1,)),
        ],
        compiler_params=pltpu.CompilerParams(vmem_limit_bytes=room(*shapes)),
        cost_estimate=pl.CostEstimate(
            flops=s.pairs * s.side**3, bytes_accessed=1 << 20, transcendentals=0
        ),
    )(*plan, *operands)


def sum_kernel(
    s, plan_ref, counts, late_ref, meta_ref, aggs_ref, slots_ref, rows_ref, far0, far1,
    send0, keep0, send1, keep1, send2, keep2, total, far_buf, picked, sems,
):
    hi = pl.program_id(0)
    high = s.tiles * s.side
    copies = [
        pltpu.make_async_copy(
            ref.at[pl.ds(0, high)], far_buf.at[pl.ds(k * high, high)], sems.at[k]
        )
        for k, ref in enumerate((far0, far1))
    ]

    @pl.when(hi == 0)
    def _():
        for copy in copies:
            copy.start()

    def clear(k, carry):
        total[k] = jnp.zeros(total.shape[1:], jnp.float32)
        return carry

    lax.fori_loop(0, s.blocks, clear, 0)

    def add(entry, product):
        known = jnp.maximum(entry, 0)
        term = jnp.dot(
            rows_ref[known & (s.slab - 1)], product, preferred_element_type=jnp.float32
        )
        cell = field(s, known, 2)
        at = pl.ds(pl.multiple_of((cell & (s.per - 1)) * s.side, s.side), s.side)
        total[cell >> log2(s.per), at, :] += jnp.where(entry >= 0, term, 0.0)

    def near(group, carry):
        for u in range(UNROLL):
            n = group * UNROLL + u
            add(plan_ref[n], slots_ref[n])
        return carry

    begin = meta_ref[2 * hi]
    lax.fori_loop(begin // UNROLL, pl.cdiv(begin + counts[hi], UNROLL), near, 0)

    col = lax.axis_index("col")
    first = meta_ref[2 * hi + 1]

    def pick(n, n_mine):
        slot = first + n
        mine, part = column_part(s, aggs_ref[late_ref[slot * 2 + 1]], col)
        picked[n_mine * 2] = slot
        picked[n_mine * 2 + 1] = late_ref[slot * 2] + part
        return n_mine + jnp.where(mine, 1, 0)

    n_mine = lax.fori_loop(0, meta_ref[s.buckets + 2 + hi], pick, jnp.int32(0))
    for u in range(UNROLL):
        picked[(n_mine + u) * 2] = 0
        picked[(n_mine + u) * 2 + 1] = -1

    @pl.when(hi == 0)
    def _():
        for copy in copies:
            copy.wait()

    def far(group, carry):
        for u in range(UNROLL):
            n = group * UNROLL + u
            slot, entry = picked[n * 2], picked[n * 2 + 1]
            at = field(s, jnp.maximum(entry, 0), 1) * s.side
            piece = far_buf[pl.ds(pl.multiple_of(at, s.side), s.side), :]
            product = jnp.dot(slots_ref[slot], piece, preferred_element_type=jnp.float32)
            add(entry, product.astype(jnp.bfloat16))
        return carry

    lax.fori_loop(0, pl.cdiv(n_mine, UNROLL), far, 0)

    half = s.cols // 2
    weight = {"x": 1, "y": half, "1": 2 * half, "2": 4 * half}
    core = lax.axis_index("col") & 1
    outs = ((send0, keep0), (send1, keep1), (send2, keep2))
    for k, (send, keep) in enumerate(outs):
        for bits in itertools.product(range(2), repeat=4):
            base = [
                sum(weight[link] * bit for link, bit in zip(order, bits)) for order in ORDERS[k]
            ]
            base = jnp.where(core == 0, *base)
            for x in range(half // 2):
                part = total[base + 2 * x, s.splits[k]:s.splits[k + 1], :]
                if bits[0]:
                    send[(*bits[1:], 0, x)] = part.astype(jnp.bfloat16)
                else:
                    keep[(*bits[1:], 0, x)] = part


def make_sums(s, lists, slots, rows_t, far):
    smem = pl.BlockSpec(memory_space=pltpu.SMEM)
    vmem = pl.BlockSpec(memory_space=pltpu.VMEM)
    anywhere = pl.BlockSpec(memory_space=pl.ANY)
    shapes = [
        ((s.slots + s.slab + 2 * s.tiles, s.side, s.side), jnp.bfloat16),
        ((s.blocks, s.tall, s.side), jnp.float32),
    ]
    out_shape, out_specs = [], []
    for k in range(len(ORDERS)):
        last = (s.cols // 4, s.splits[k + 1] - s.splits[k], s.side)
        for dtype in (jnp.bfloat16, jnp.float32):
            out_shape.append(jax.ShapeDtypeStruct((2, 2, 2, s.his) + last, dtype))
            out_specs.append(
                pl.BlockSpec((2, 2, 2, 1) + last, lambda h: (0, 0, 0, h, 0, 0, 0))
            )
            shapes.append(((2 if s.his > 1 else 1, 8) + last, dtype))
    return pl.pallas_call(
        functools.partial(sum_kernel, s),
        grid=(s.his,),
        in_specs=[smem] * 5 + [vmem, vmem, anywhere, anywhere],
        out_specs=out_specs,
        out_shape=out_shape,
        scratch_shapes=[
            pltpu.VMEM((s.blocks, s.tall, s.side), jnp.float32),
            pltpu.VMEM((2 * s.tiles * s.side, s.side), jnp.bfloat16),
            pltpu.SMEM(((s.pairs + UNROLL) * 2,), jnp.int32),
            pltpu.SemaphoreType.DMA((2,)),
        ],
        compiler_params=pltpu.CompilerParams(vmem_limit_bytes=room(*shapes)),
        cost_estimate=pl.CostEstimate(
            flops=s.pairs * s.side**3, bytes_accessed=16 << 20, transcendentals=0
        ),
    )(*lists, slots, rows_t, *far)


def shards(a_blocks, p_tiles, owner, agg_local, a_cols):
    s = Sizes(
        lax.axis_size("row"), lax.axis_size("col"), p_tiles.shape[0], p_tiles.shape[1]
    )
    order = ring_order(s.rows)
    barrier = lax.optimization_barrier

    def ring(value, stream):
        moves = []
        for k in range(s.rows):
            for c in range(s.cols):
                step = 1 if (stream + c) % 2 == 0 else -1
                to = order[(k + step) % s.rows]
                moves.append((order[k] * s.cols + c, to * s.cols + c))
        return lax.ppermute(value, ("row", "col"), moves)

    high = s.tiles * s.side
    aggs = owner[:, 0] * OWN + agg_local
    label = jnp.pad(aggs.astype(jnp.bfloat16)[None], ((0, LABEL - 1), (0, s.side - s.slab)))
    mine = p_tiles.reshape(high, s.side)
    labelled = jnp.concatenate([mine, label], 0)

    first = ring(labelled, 0)
    cols = a_cols[:, 0]
    cols_other = swap(cols, "col", 1)
    cols_other, labelled = barrier((cols_other, labelled))
    second = ring(labelled, 1)
    a_other, p_other = swap(a_blocks[:, 0], "col", 1), swap(mine, "col", 1)
    plan = make_plan(s, jnp.concatenate([cols, cols_other], 0), aggs)

    came, a_other, p_other, mine = barrier((first, a_other, p_other, mine))
    first = ring(first, 0)
    own_near, other_near = {0: labelled, s.rows - 1: came, 1: second}, {0: p_other}
    second = ring(second, 1)
    rows = [mine]
    bit = 2
    while bit < s.cols:
        rows += [swap(piece, "col", bit) for piece in rows]
        bit *= 2

    held = [1, s.rows - 1]
    for step in range(2, s.half - 1):
        came, *rest = barrier((second, *(own_near[away] for away in held), *rows[1:]))
        for away, piece in zip(held, rest):
            other_near[away] = swap(piece, "col", 1)
        if step == 2:
            rows += [p_other] + [swap(piece, "col", 1) for piece in rest[len(held):]]
        own_near[s.rows - step], own_near[step] = first, came
        first, second = ring(first, 0), ring(second, 1)
        held = [step, s.rows - step]

    others = sorted(set(other_near) - {0})
    tie = (first, second, *plan)
    tie += (*(own_near[away] for away in held), *(other_near[away] for away in others))
    first, second, *rest = barrier(tie)
    plan, rest = rest[:len(plan)], rest[len(plan):]
    for away, piece in zip(others, rest[len(held):]):
        other_near[away] = piece
    far = ring(first, 0)
    own_near[s.half + 1], own_near[s.half - 1] = first, second
    for away, piece in zip(held, rest):
        other_near[away] = swap(piece, "col", 1)
    for away in (s.half + 1, s.half - 1):
        other_near[away] = swap(own_near[away], "col", 1)
    near = [own_near[k] for k in sorted(own_near)]
    near += [other_near[k] for k in sorted(other_near)]
    slots, rows_t, picks, counts = make_products(
        s, plan, a_blocks[:, 0], a_other, near, rows
    )
    far, slots, rows_t = barrier((far, slots, rows_t))
    far_other = swap(far, "col", 1)
    lists = (picks, counts, plan[1], plan[2], far[high, :s.slab].astype(jnp.int32))
    parts = make_sums(s, lists, slots, rows_t, [far, far_other])

    sends, keeps = list(parts[0::2]), list(parts[1::2])
    groups = range(len(ORDERS))
    moving = [exchange(sends[k], [order[0] for order in ORDERS[k]]) for k in groups]
    for step in range(1, 5):
        for k in groups:
            got = moving[k]
            if step < 4:
                send = (keeps[k][1] + got[1].astype(jnp.float32)).astype(jnp.bfloat16)
                moving[k] = exchange(send, [order[step] for order in ORDERS[k]])
                keeps[k] = keeps[k][0] + got[0].astype(jnp.float32)
            else:
                keeps[k] = keeps[k] + got.astype(jnp.float32)
    total = jnp.concatenate(keeps, -2)
    tail = [("row", 1 << k) for k in range(3, log2(s.rows))][::-1]
    tail += [("col", 1 << k) for k in range(2, log2(s.cols))][::-1]
    total = total.reshape((2,) * len(tail) + total.shape[-2:])
    for axis in tail:
        got = swap(total[1].astype(jnp.bfloat16), *axis)
        total = total[0] + got.astype(jnp.float32)
    return total.reshape(OWN, s.width, s.side, s.side)


def solution(mesh):
    in_specs = (
        P("row", "col", None, None),
        P(("row", "col"), None, None),
        P("row", None),
        P("row"),
        P("row", "col"),
    )
    out_specs = P("row", "col", None, None)
    return jax.shard_map(shards, mesh=mesh, in_specs=in_specs, out_specs=out_specs, check_vma=False)
```

```python
import functools
import itertools
import math

import jax
import jax.numpy as jnp
from jax import lax
from jax.experimental import pallas as pl
from jax.experimental.pallas import tpu as pltpu
from jax.sharding import PartitionSpec as P

OWN = 2
UNROLL = 8
ORDERS = (("1x2y", "x1y2"), ("xy12", "yx21"), ("y1x2", "2xy1"))
LINKS = {"x": ("col", 2), "y": ("row", 1), "1": ("row", 2), "2": ("row", 4)}


def ring_order(count):
    return list(range(0, count, 2)) + list(range(1, count, 2))[::-1]


def swap(value, axis, bit):
    size = lax.axis_size(axis)
    return lax.ppermute(value, axis, [(i, i ^ bit) for i in range(size)])


def exchange(value, links):
    rows, cols = lax.axis_size("row"), lax.axis_size("col")
    moves = []
    for r in range(rows):
        for c in range(cols):
            axis, bit = LINKS[links[c % 2]]
            to = (r ^ bit, c) if axis == "row" else (r, c ^ bit)
            moves.append((r * cols + c, to[0] * cols + to[1]))
    return lax.ppermute(value, ("row", "col"), moves)


def log2(size):
    power = size.bit_length() - 1
    assert size == 1 << power
    return power


class Sizes:
    def __init__(self, rows, cols, tiles, side):
        self.rows, self.cols, self.tiles, self.side = rows, cols, tiles, side
        self.slab = cols * tiles
        self.pairs = 2 * self.slab
        self.width = OWN * rows // cols
        self.per = OWN * self.width
        self.his = rows // 8
        self.blocks, self.tall = 4 * cols, self.per * side
        third = self.tall // 16 // 3 * 16
        self.splits = (0, third, 2 * third, self.tall)
        self.buckets = 2 * self.his
        self.slots = self.pairs + self.buckets * UNROLL
        self.half = rows // 2
        self.early = rows - 1
        self.near = 2 * self.early * tiles
        self.fields, shift = [], 0
        for size in (self.pairs, 2 * rows * tiles, self.blocks * self.per):
            self.fields.append((shift, size - 1))
            shift += log2(size)
        assert shift <= 31


def field(s, entry, k):
    shift, mask = s.fields[k]
    return (entry >> shift) & mask


def plan_kernel(s, cols_ref, aggs_ref, plan_ref, starts_ref, info, counts):
    row = lax.axis_index("row")
    col = lax.axis_index("col")

    def ring_place(index):
        return jnp.where((index & 1) == 0, index >> 1, s.rows - 1 - (index >> 1))

    here = ring_place(row)
    for b in range(s.buckets):
        counts[b] = 0

    def blank(k, carry):
        plan_ref[k] = -1
        return carry

    lax.fori_loop(0, s.slots + 1, blank, 0, unroll=8)

    def sort(i, carry):
        tile = i & (s.slab - 1)
        side = i >> log2(s.slab)
        other = cols_ref[i]
        other_row = other >> log2(s.slab)
        i_agg = aggs_ref[tile]
        j_agg = aggs_ref[((other_row ^ row) << log2(s.slab)) + (other & (s.slab - 1))]
        rel_col = (j_agg >> log2(s.width)) ^ col
        rel_row = (i_agg >> log2(OWN)) ^ row
        turn = ring_place(other_row) - here
        away = jnp.where(((col ^ side) & 1) == 0, turn, -turn) & (s.rows - 1)
        late = jnp.where(away == s.half, 1, 0)
        order = away - jnp.where(away > s.half, 1, 0) + side * s.early
        piece = jnp.where(late == 1, side, order)
        panel_at = (piece << log2(s.tiles)) + (other & (s.tiles - 1))
        cell = (rel_row & 7) * (s.cols // 2) + (rel_col >> 1)
        cell = (cell << log2(OWN)) + (i_agg & (OWN - 1))
        cell = (cell << log2(s.width)) + (j_agg & (s.width - 1))
        bucket = (rel_row >> 3) * 2 + late
        mine = (rel_col & 1) == 0
        rank = counts[bucket]
        counts[bucket] = rank + jnp.where(mine, 1, 0)
        info[i * 2] = jnp.where(mine, rank * s.buckets + bucket, -1)
        entry = i
        for k, value in enumerate((panel_at, cell)):
            entry = entry + (value << s.fields[k + 1][0])
        info[i * 2 + 1] = entry
        return carry

    lax.fori_loop(0, s.pairs, sort, 0, unroll=4)

    start = jnp.int32(0)
    for b in range(s.buckets):
        starts_ref[b] = start
        start = start + ((counts[b] + UNROLL - 1) & ~(UNROLL - 1))
    starts_ref[s.buckets] = start

    def place(i, carry):
        key = info[i * 2]
        slot = starts_ref[key & (s.buckets - 1)] + (key >> log2(s.buckets))
        plan_ref[jnp.where(key >= 0, slot, s.slots)] = info[i * 2 + 1]
        return carry

    lax.fori_loop(0, s.pairs, place, 0, unroll=4)


def room(*shapes):
    total = sum(math.prod(shape) * jnp.dtype(dtype).itemsize for shape, dtype in shapes)
    return total + (2 << 20)


def make_plan(s, cols, aggs):
    smem = pl.BlockSpec(memory_space=pltpu.SMEM)
    return pl.pallas_call(
        functools.partial(plan_kernel, s),
        in_specs=[smem, smem],
        out_specs=[smem, smem],
        out_shape=[
            jax.ShapeDtypeStruct((s.slots + 1,), jnp.int32),
            jax.ShapeDtypeStruct((s.buckets + 1,), jnp.int32),
        ],
        scratch_shapes=[
            pltpu.SMEM((s.pairs * 2,), jnp.int32),
            pltpu.SMEM((s.buckets,), jnp.int32),
        ],
        compiler_params=pltpu.CompilerParams(vmem_limit_bytes=room()),
        cost_estimate=pl.CostEstimate(flops=1 << 20, bytes_accessed=16 << 20, transcendentals=0),
    )(cols, aggs)


def turn_kernel(s, *refs):
    rows_ref, rows_buf, sems = refs[-3:]
    copies = [
        pltpu.make_async_copy(refs[k], rows_buf.at[pl.ds(k * s.tiles, s.tiles)], sems.at[k])
        for k in range(s.cols)
    ]
    for copy in copies:
        copy.start()
    for copy in copies:
        copy.wait()
    col = lax.axis_index("col")

    def turn(k, carry):
        part = k >> log2(s.tiles)
        rel = (part & (s.cols // 2 - 1)) * 2 + (part >> log2(s.cols // 2))
        rows_ref[((rel ^ col) << log2(s.tiles)) + (k & (s.tiles - 1))] = rows_buf[k].T
        return carry

    lax.fori_loop(0, s.slab, turn, 0, unroll=4)


def turn_rows(s, rows):
    own = pltpu.with_memory_space_constraint(rows[0], pltpu.HBM)
    shape = ((s.slab, s.side, s.side), jnp.bfloat16)
    return pl.pallas_call(
        functools.partial(turn_kernel, s),
        in_specs=[pl.BlockSpec(memory_space=pltpu.HBM)]
        + [pl.BlockSpec(memory_space=pl.ANY)] * (s.cols - 1),
        out_specs=pl.BlockSpec(memory_space=pltpu.VMEM),
        out_shape=jax.ShapeDtypeStruct(*shape),
        scratch_shapes=[pltpu.VMEM(*shape), pltpu.SemaphoreType.DMA((s.cols,))],
        compiler_params=pltpu.CompilerParams(vmem_limit_bytes=room(shape, shape)),
        cost_estimate=pl.CostEstimate(flops=1 << 20, bytes_accessed=16 << 20, transcendentals=0),
    )(own, *rows[1:])


def product_kernel(s, plan_ref, starts_ref, *refs):
    slots_ref, a_buf, panel, sems = refs[-4:]
    copies = []
    for k in range(2):
        copies.append((refs[k], a_buf.at[pl.ds(k * s.slab, s.slab)]))
    for k in range(2 * s.early):
        copies.append((refs[2 + k], panel.at[pl.ds(k * s.tiles, s.tiles)]))
    copies = [pltpu.make_async_copy(src, dst, sems.at[k]) for k, (src, dst) in enumerate(copies)]
    for copy in copies:
        copy.start()
    for copy in copies:
        copy.wait()

    for hi in range(s.his):
        begin = starts_ref[2 * hi] // UNROLL
        middle = starts_ref[2 * hi + 1] // UNROLL
        end = starts_ref[2 * hi + 2] // UNROLL

        def near(group, carry):
            for u in range(UNROLL):
                n = group * UNROLL + u
                entry = jnp.maximum(plan_ref[n], 0)
                slots_ref[n] = jnp.dot(
                    a_buf[field(s, entry, 0)],
                    panel[field(s, entry, 1)],
                    preferred_element_type=jnp.float32,
                ).astype(jnp.bfloat16)
            return carry

        def far(group, carry):
            for u in range(UNROLL):
                n = group * UNROLL + u
                slots_ref[n] = a_buf[field(s, jnp.maximum(plan_ref[n], 0), 0)]
            return carry

        lax.fori_loop(begin, middle, near, 0)
        lax.fori_loop(middle, end, far, 0)


def make_products(s, plan, starts, a_own, a_other, near):
    smem = pl.BlockSpec(memory_space=pltpu.SMEM)
    hbm = pl.BlockSpec(memory_space=pltpu.HBM)
    anywhere = pl.BlockSpec(memory_space=pl.ANY)
    shapes = [
        ((count, s.side, s.side), jnp.bfloat16) for count in (s.slots, s.pairs, s.near)
    ]
    a_own, own = (pltpu.with_memory_space_constraint(x, pltpu.HBM) for x in (a_own, near[0]))
    operands = [a_own, a_other, own, *near[1:]]
    return pl.pallas_call(
        functools.partial(product_kernel, s),
        in_specs=[smem, smem, hbm, anywhere, hbm] + [anywhere] * (len(operands) - 3),
        out_specs=pl.BlockSpec(memory_space=pltpu.VMEM),
        out_shape=jax.ShapeDtypeStruct(*shapes[0]),
        scratch_shapes=[pltpu.VMEM(*shape) for shape in shapes[1:]]
        + [pltpu.SemaphoreType.DMA((len(operands),))],
        compiler_params=pltpu.CompilerParams(vmem_limit_bytes=room(*shapes)),
        cost_estimate=pl.CostEstimate(
            flops=s.pairs * s.side**3, bytes_accessed=1 << 20, transcendentals=0
        ),
    )(plan, starts, *operands)


def sum_kernel(
    s, plan_ref, starts_ref, slots_ref, rows_ref, far0, far1,
    send0, keep0, send1, keep1, send2, keep2, total, far_buf, sems,
):
    hi = pl.program_id(0)
    copies = [
        pltpu.make_async_copy(ref, far_buf.at[pl.ds(k * s.tiles, s.tiles)], sems.at[k])
        for k, ref in enumerate((far0, far1))
    ]

    @pl.when(hi == 0)
    def _():
        for copy in copies:
            copy.start()

    def clear(k, carry):
        total[k] = jnp.zeros(total.shape[1:], jnp.float32)
        return carry

    lax.fori_loop(0, s.blocks, clear, 0)

    def add(n, product):
        entry = plan_ref[n]
        known = jnp.maximum(entry, 0)
        term = jnp.dot(
            rows_ref[known & (s.slab - 1)], product, preferred_element_type=jnp.float32
        )
        cell = field(s, known, 2)
        at = pl.ds(pl.multiple_of((cell & (s.per - 1)) * s.side, s.side), s.side)
        total[cell >> log2(s.per), at, :] += jnp.where(entry >= 0, term, 0.0)

    def near(group, carry):
        for u in range(UNROLL):
            n = group * UNROLL + u
            add(n, slots_ref[n])
        return carry

    def far(group, carry):
        for u in range(UNROLL):
            n = group * UNROLL + u
            piece = far_buf[field(s, jnp.maximum(plan_ref[n], 0), 1)]
            product = jnp.dot(slots_ref[n], piece, preferred_element_type=jnp.float32)
            add(n, product.astype(jnp.bfloat16))
        return carry

    begin = starts_ref[2 * hi] // UNROLL
    middle = starts_ref[2 * hi + 1] // UNROLL
    end = starts_ref[2 * hi + 2] // UNROLL
    lax.fori_loop(begin, middle, near, 0)

    @pl.when(hi == 0)
    def _():
        for copy in copies:
            copy.wait()

    lax.fori_loop(middle, end, far, 0)

    half = s.cols // 2
    weight = {"x": 1, "y": half, "1": 2 * half, "2": 4 * half}
    core = lax.axis_index("col") & 1
    outs = ((send0, keep0), (send1, keep1), (send2, keep2))
    for k, (send, keep) in enumerate(outs):
        for bits in itertools.product(range(2), repeat=4):
            base = [
                sum(weight[link] * bit for link, bit in zip(order, bits)) for order in ORDERS[k]
            ]
            base = jnp.where(core == 0, *base)
            for x in range(half // 2):
                part = total[base + 2 * x, s.splits[k]:s.splits[k + 1], :]
                if bits[0]:
                    send[(*bits[1:], 0, x)] = part.astype(jnp.bfloat16)
                else:
                    keep[(*bits[1:], 0, x)] = part


def make_sums(s, plan, starts, slots, rows_t, far):
    smem = pl.BlockSpec(memory_space=pltpu.SMEM)
    vmem = pl.BlockSpec(memory_space=pltpu.VMEM)
    anywhere = pl.BlockSpec(memory_space=pl.ANY)
    shapes = [
        ((s.slots + s.slab + 2 * s.tiles, s.side, s.side), jnp.bfloat16),
        ((s.blocks, s.tall, s.side), jnp.float32),
    ]
    out_shape, out_specs = [], []
    for k in range(len(ORDERS)):
        last = (s.cols // 4, s.splits[k + 1] - s.splits[k], s.side)
        for dtype in (jnp.bfloat16, jnp.float32):
            out_shape.append(jax.ShapeDtypeStruct((2, 2, 2, s.his) + last, dtype))
            out_specs.append(
                pl.BlockSpec((2, 2, 2, 1) + last, lambda h: (0, 0, 0, h, 0, 0, 0))
            )
            shapes.append(((2 if s.his > 1 else 1, 8) + last, dtype))
    return pl.pallas_call(
        functools.partial(sum_kernel, s),
        grid=(s.his,),
        in_specs=[smem, smem, vmem, vmem, anywhere, anywhere],
        out_specs=out_specs,
        out_shape=out_shape,
        scratch_shapes=[
            pltpu.VMEM((s.blocks, s.tall, s.side), jnp.float32),
            pltpu.VMEM((2 * s.tiles, s.side, s.side), jnp.bfloat16),
            pltpu.SemaphoreType.DMA((2,)),
        ],
        compiler_params=pltpu.CompilerParams(vmem_limit_bytes=room(*shapes)),
        cost_estimate=pl.CostEstimate(
            flops=s.pairs * s.side**3, bytes_accessed=16 << 20, transcendentals=0
        ),
    )(plan, starts, slots, rows_t, *far)


def shards(a_blocks, p_tiles, owner, agg_local, a_cols):
    s = Sizes(
        lax.axis_size("row"), lax.axis_size("col"), p_tiles.shape[0], p_tiles.shape[1]
    )
    order = ring_order(s.rows)
    barrier = lax.optimization_barrier

    def ring(value, stream):
        moves = []
        for k in range(s.rows):
            for c in range(s.cols):
                step = 1 if (stream + c) % 2 == 0 else -1
                to = order[(k + step) % s.rows]
                moves.append((order[k] * s.cols + c, to * s.cols + c))
        return lax.ppermute(value, ("row", "col"), moves)

    first = ring(p_tiles, 0)
    cols = a_cols[:, 0]
    cols_other = swap(cols, "col", 1)
    cols_other, mine = barrier((cols_other, p_tiles))
    second = ring(mine, 1)
    a_other, p_other = swap(a_blocks[:, 0], "col", 1), swap(p_tiles, "col", 1)
    rows = [p_tiles]
    bit = 2
    while bit < s.cols:
        rows += [swap(piece, "col", bit) for piece in rows]
        bit *= 2

    aggs = owner[:, 0] * OWN + agg_local
    aggs, a_other, p_other, came, *rows[1:] = barrier(
        (aggs, a_other, p_other, first, *rows[1:])
    )
    own_near, other_near = {0: p_tiles, s.rows - 1: came, 1: second}, {0: p_other}
    first, second = ring(first, 0), ring(second, 1)
    aggs = [aggs] + [swap(aggs, "row", mask) for mask in (1, 2, 3)]
    aggs = jnp.concatenate(aggs, 0)
    bit = 4
    while bit < s.rows:
        aggs = jnp.concatenate([aggs, swap(aggs, "row", bit)], 0)
        bit *= 2
    plan, starts = make_plan(s, jnp.concatenate([cols, cols_other], 0), aggs)

    held = [1, s.rows - 1]
    for step in range(2, s.half - 1):
        came, *rest = barrier((second, *(own_near[away] for away in held), *rows[1:]))
        for away, piece in zip(held, rest):
            other_near[away] = swap(piece, "col", 1)
        if step == 2:
            rows += [p_other] + [swap(piece, "col", 1) for piece in rest[len(held):]]
        own_near[s.rows - step], own_near[step] = first, came
        first, second = ring(first, 0), ring(second, 1)
        held = [step, s.rows - step]

    others = sorted(set(other_near) - {0})
    first, *rest = barrier((first, *rows[1:]))
    rows_t = turn_rows(s, [p_tiles, *rest])
    tie = (first, second, plan, starts, rows_t)
    tie += (*(own_near[away] for away in held), *(other_near[away] for away in others))
    first, second, plan, starts, rows_t, *rest = barrier(tie)
    for away, piece in zip(others, rest[len(held):]):
        other_near[away] = piece
    far = ring(first, 0)
    own_near[s.half + 1], own_near[s.half - 1] = first, second
    for away, piece in zip(held, rest):
        other_near[away] = swap(piece, "col", 1)
    for away in (s.half + 1, s.half - 1):
        other_near[away] = swap(own_near[away], "col", 1)
    near = [own_near[k] for k in sorted(own_near)]
    near += [other_near[k] for k in sorted(other_near)]
    slots = make_products(s, plan, starts, a_blocks[:, 0], a_other, near)
    far, slots = barrier((far, slots))
    far_other = swap(far, "col", 1)
    parts = make_sums(s, plan, starts, slots, rows_t, [far, far_other])

    sends, keeps = list(parts[0::2]), list(parts[1::2])
    groups = range(len(ORDERS))
    moving = [exchange(sends[k], [order[0] for order in ORDERS[k]]) for k in groups]
    for step in range(1, 5):
        for k in groups:
            got = moving[k]
            if step < 4:
                send = (keeps[k][1] + got[1].astype(jnp.float32)).astype(jnp.bfloat16)
                moving[k] = exchange(send, [order[step] for order in ORDERS[k]])
                keeps[k] = keeps[k][0] + got[0].astype(jnp.float32)
            else:
                keeps[k] = keeps[k] + got.astype(jnp.float32)
    total = jnp.concatenate(keeps, -2)
    tail = [("row", 1 << k) for k in range(3, log2(s.rows))][::-1]
    tail += [("col", 1 << k) for k in range(2, log2(s.cols))][::-1]
    total = total.reshape((2,) * len(tail) + total.shape[-2:])
    for axis in tail:
        got = swap(total[1].astype(jnp.bfloat16), *axis)
        total = total[0] + got.astype(jnp.float32)
    return total.reshape(OWN, s.width, s.side, s.side)


def solution(mesh):
    in_specs = (
        P("row", "col", None, None),
        P(("row", "col"), None, None),
        P("row", None),
        P("row"),
        P("row", "col"),
    )
    out_specs = P("row", "col", None, None)
    return jax.shard_map(shards, mesh=mesh, in_specs=in_specs, out_specs=out_specs, check_vma=False)
```

```python
import functools
import itertools
import math

import jax
import jax.numpy as jnp
from jax import lax
from jax.experimental import pallas as pl
from jax.experimental.pallas import tpu as pltpu
from jax.sharding import PartitionSpec as P

OWN = 2
UNROLL = 8
LOOK_BITS = 12
LABEL = 16
ORDERS = (("1x2y", "x1y2"), ("xy12", "yx21"), ("y1x2", "2xy1"))
LINKS = {"x": ("col", 2), "y": ("row", 1), "1": ("row", 2), "2": ("row", 4)}


def ring_order(count):
    return list(range(0, count, 2)) + list(range(1, count, 2))[::-1]


def swap(value, axis, bit):
    size = lax.axis_size(axis)
    return lax.ppermute(value, axis, [(i, i ^ bit) for i in range(size)])


def exchange(value, links):
    rows, cols = lax.axis_size("row"), lax.axis_size("col")
    moves = []
    for r in range(rows):
        for c in range(cols):
            axis, bit = LINKS[links[c % 2]]
            to = (r ^ bit, c) if axis == "row" else (r, c ^ bit)
            moves.append((r * cols + c, to[0] * cols + to[1]))
    return lax.ppermute(value, ("row", "col"), moves)


def log2(size):
    power = size.bit_length() - 1
    assert size == 1 << power
    return power


class Sizes:
    def __init__(self, rows, cols, tiles, side):
        self.rows, self.cols, self.tiles, self.side = rows, cols, tiles, side
        self.slab = cols * tiles
        self.pairs = 2 * self.slab
        self.width = OWN * rows // cols
        self.per = OWN * self.width
        self.his = rows // 8
        self.blocks, self.tall = 4 * cols, self.per * side
        third = self.tall // 16 // 3 * 16
        self.splits = (0, third, 2 * third, self.tall)
        self.buckets = 2 * self.his
        self.slots = self.pairs + self.buckets * UNROLL
        self.half = rows // 2
        self.early = rows - 1
        self.near = 2 * self.early * tiles
        self.fields, shift = [], 0
        for size in (self.pairs, 2 * rows * tiles, self.blocks * self.per):
            self.fields.append((shift, size - 1))
            shift += log2(size)
        assert shift <= 31


def field(s, entry, k):
    shift, mask = s.fields[k]
    return (entry >> shift) & mask


def column_part(s, j_agg, col):
    rel_col = (j_agg >> log2(s.width)) ^ col
    part = ((rel_col >> 1) << log2(s.per)) + (j_agg & (s.width - 1))
    return (rel_col & 1) == 0, part << s.fields[2][0]


def plan_kernel(s, cols_ref, aggs_ref, near_ref, late_ref, meta_ref, info, counts):
    row = lax.axis_index("row")
    col = lax.axis_index("col")

    def ring_place(index):
        return jnp.where((index & 1) == 0, index >> 1, s.rows - 1 - (index >> 1))

    here = ring_place(row)
    for b in range(s.buckets):
        counts[b] = 0

    def sort(i, carry):
        n_near, n_late = carry
        tile = i & (s.slab - 1)
        side = i >> log2(s.slab)
        other = cols_ref[i]
        i_agg = aggs_ref[tile]
        rel_row = (i_agg >> log2(OWN)) ^ row
        turn = ring_place(other >> log2(s.slab)) - here
        mine = jnp.where((col & 1) == 0, turn, -turn) & (s.rows - 1)
        away = jnp.where(((col ^ side) & 1) == 0, turn, -turn) & (s.rows - 1)
        late = jnp.where(away == s.half, 1, 0)
        order = away - jnp.where(away > s.half, 1, 0) + side * s.early
        piece = jnp.where(late == 1, side, order)
        panel_at = (piece << log2(s.tiles)) + (other & (s.tiles - 1))
        cell = ((rel_row & 7) << (log2(s.cols // 2) + log2(s.per))) + (
            (i_agg & (OWN - 1)) << log2(s.width)
        )
        entry = i + (panel_at << s.fields[1][0]) + (cell << s.fields[2][0])
        slab_at = mine - jnp.where(mine > s.half, 1, 0)
        look = jnp.where(late == 1, 0, slab_at << log2(s.slab)) + (other & (s.slab - 1))
        look = look + ((rel_row >> 3) << LOOK_BITS)
        bucket = (rel_row >> 3) * 2 + late
        counts[bucket] = counts[bucket] + 1
        near_ref[n_near * 2] = entry
        near_ref[n_near * 2 + 1] = look
        info[n_late * 2] = entry
        info[n_late * 2 + 1] = look
        return n_near + 1 - late, n_late + late

    zero = jnp.int32(0)
    n_near, n_late = lax.fori_loop(0, s.pairs, sort, (zero, zero), unroll=4)
    for u in range(4):
        near_ref[(n_near + u) * 2] = 0
        near_ref[(n_near + u) * 2 + 1] = 0

    start = zero
    for b in range(s.buckets):
        meta_ref[b] = start
        start = start + ((counts[b] + UNROLL - 1) & ~(UNROLL - 1))
    meta_ref[s.buckets] = start
    meta_ref[s.buckets + 1] = n_near
    for hi in range(s.his):
        meta_ref[s.buckets + 2 + hi] = counts[2 * hi + 1]
        for u in range(UNROLL):
            at = meta_ref[2 * hi + 1] + counts[2 * hi + 1] + u
            late_ref[jnp.where(at < meta_ref[2 * hi + 2], at, s.slots) * 2] = 0
        counts[2 * hi + 1] = 0

    def place(n, carry):
        look = info[n * 2 + 1]
        bucket = (look >> LOOK_BITS) * 2 + 1
        rank = counts[bucket]
        counts[bucket] = rank + 1
        slot = meta_ref[bucket] + rank
        late_ref[slot * 2] = info[n * 2]
        late_ref[slot * 2 + 1] = look & ((1 << LOOK_BITS) - 1)
        return carry

    lax.fori_loop(0, n_late, place, 0)


def room(*shapes):
    total = sum(math.prod(shape) * jnp.dtype(dtype).itemsize for shape, dtype in shapes)
    return total + (2 << 20)


def make_plan(s, cols, aggs):
    smem = pl.BlockSpec(memory_space=pltpu.SMEM)
    counts = (s.pairs * 2 + 8, (s.slots + 1) * 2, s.buckets + 2 + s.his)
    return pl.pallas_call(
        functools.partial(plan_kernel, s),
        in_specs=[smem, smem],
        out_specs=[smem, smem, smem],
        out_shape=[jax.ShapeDtypeStruct((count,), jnp.int32) for count in counts],
        scratch_shapes=[
            pltpu.SMEM((s.pairs * 2,), jnp.int32),
            pltpu.SMEM((s.buckets,), jnp.int32),
        ],
        compiler_params=pltpu.CompilerParams(vmem_limit_bytes=room()),
        cost_estimate=pl.CostEstimate(flops=1 << 20, bytes_accessed=16 << 20, transcendentals=0),
    )(cols, aggs)


def turn_kernel(s, *refs):
    rows_ref, rows_buf, sems = refs[-3:]
    high = s.tiles * s.side
    copies = [
        pltpu.make_async_copy(refs[k], rows_buf.at[pl.ds(k * high, high)], sems.at[k])
        for k in range(s.cols)
    ]
    for copy in copies:
        copy.start()
    for copy in copies:
        copy.wait()
    col = lax.axis_index("col")

    def turn(k, carry):
        part = k >> log2(s.tiles)
        rel = (part & (s.cols // 2 - 1)) * 2 + (part >> log2(s.cols // 2))
        at = pl.ds(pl.multiple_of(k * s.side, s.side), s.side)
        rows_ref[((rel ^ col) << log2(s.tiles)) + (k & (s.tiles - 1))] = rows_buf[at, :].T
        return carry

    lax.fori_loop(0, s.slab, turn, 0, unroll=4)


def turn_rows(s, rows):
    own = pltpu.with_memory_space_constraint(rows[0], pltpu.HBM)
    shape, flat = (s.slab, s.side, s.side), (s.slab * s.side, s.side)
    return pl.pallas_call(
        functools.partial(turn_kernel, s),
        in_specs=[pl.BlockSpec(memory_space=pltpu.HBM)]
        + [pl.BlockSpec(memory_space=pl.ANY)] * (s.cols - 1),
        out_specs=pl.BlockSpec(memory_space=pltpu.VMEM),
        out_shape=jax.ShapeDtypeStruct(shape, jnp.bfloat16),
        scratch_shapes=[pltpu.VMEM(flat, jnp.bfloat16), pltpu.SemaphoreType.DMA((s.cols,))],
        compiler_params=pltpu.CompilerParams(
            vmem_limit_bytes=room((shape, jnp.bfloat16), (flat, jnp.bfloat16))
        ),
        cost_estimate=pl.CostEstimate(flops=1 << 20, bytes_accessed=16 << 20, transcendentals=0),
    )(own, *rows[1:])


def pick_kernel(s, near_ref, meta_ref, *refs):
    plan_ref, counts, label_buf, label_ints, labels, sems = refs[-6:]
    copies = [
        pltpu.make_async_copy(
            refs[k].at[pl.ds(s.tiles * s.side, LABEL)],
            label_buf.at[pl.ds(k * LABEL, LABEL)],
            sems.at[k],
        )
        for k in range(s.early)
    ]
    for copy in copies:
        copy.start()
    col = lax.axis_index("col")
    for hi in range(s.his):
        counts[hi] = 0
    n_near = meta_ref[s.buckets + 1]
    for copy in copies:
        copy.wait()
    label_ints[...] = label_buf[...].astype(jnp.float32).astype(jnp.int32)
    copy = pltpu.make_async_copy(label_ints, labels, sems.at[s.early])
    copy.start()
    copy.wait()

    def pick(step, carry):
        for n in range(4):
            n = step * 4 + n
            look = near_ref[n * 2 + 1]
            hi = look >> LOOK_BITS
            slab = (look & ((1 << LOOK_BITS) - 1)) >> log2(s.slab)
            j_agg = labels[slab * LABEL, look & (s.slab - 1)]
            mine, part = column_part(s, j_agg, col)
            mine = mine & (n < n_near)
            rank = counts[hi]
            counts[hi] = rank + jnp.where(mine, 1, 0)
            plan_ref[jnp.where(mine, meta_ref[2 * hi] + rank, s.slots)] = near_ref[n * 2] + part
        return carry

    lax.fori_loop(0, pl.cdiv(n_near, 4), pick, 0)
    for hi in range(s.his):
        for u in range(UNROLL):
            at = meta_ref[2 * hi] + counts[hi] + u
            plan_ref[jnp.where(at < meta_ref[2 * hi + 1], at, s.slots)] = -1


def pick_near(s, plan, near):
    smem = pl.BlockSpec(memory_space=pltpu.SMEM)
    shape = (s.early * LABEL, s.side)
    return pl.pallas_call(
        functools.partial(pick_kernel, s),
        in_specs=[smem, smem] + [pl.BlockSpec(memory_space=pl.ANY)] * s.early,
        out_specs=[smem, smem],
        out_shape=[jax.ShapeDtypeStruct((count,), jnp.int32) for count in (s.slots + 1, s.his)],
        scratch_shapes=[
            pltpu.VMEM(shape, jnp.bfloat16),
            pltpu.VMEM(shape, jnp.int32),
            pltpu.SMEM(shape, jnp.int32),
            pltpu.SemaphoreType.DMA((s.early + 1,)),
        ],
        compiler_params=pltpu.CompilerParams(
            vmem_limit_bytes=room((shape, jnp.bfloat16), (shape, jnp.int32))
        ),
        cost_estimate=pl.CostEstimate(flops=1 << 20, bytes_accessed=1 << 20, transcendentals=0),
    )(plan[0], plan[2], *near)


def product_kernel(s, plan_ref, counts, late_ref, meta_ref, *refs):
    slots_ref, a_buf, panel, sems = refs[-4:]
    high = s.tiles * s.side
    copies = []
    for k in range(2):
        copies.append((refs[k], a_buf.at[pl.ds(k * s.slab, s.slab)]))
    for k in range(2 * s.early):
        copies.append((refs[2 + k].at[pl.ds(0, high)], panel.at[pl.ds(k * high, high)]))
    copies = [pltpu.make_async_copy(src, dst, sems.at[k]) for k, (src, dst) in enumerate(copies)]
    for copy in copies:
        copy.start()
    for copy in copies:
        copy.wait()

    for hi in range(s.his):
        begin = meta_ref[2 * hi] // UNROLL
        middle = pl.cdiv(meta_ref[2 * hi] + counts[hi], UNROLL)

        def near(group, carry):
            for u in range(UNROLL):
                n = group * UNROLL + u
                entry = jnp.maximum(plan_ref[n], 0)
                at = pl.multiple_of(field(s, entry, 1) * s.side, s.side)
                slots_ref[n] = jnp.dot(
                    a_buf[field(s, entry, 0)],
                    panel[pl.ds(at, s.side), :],
                    preferred_element_type=jnp.float32,
                ).astype(jnp.bfloat16)
            return carry

        def far(group, carry):
            for u in range(UNROLL):
                n = group * UNROLL + u
                slots_ref[n] = a_buf[field(s, late_ref[n * 2], 0)]
            return carry

        lax.fori_loop(begin, middle, near, 0)
        lax.fori_loop(meta_ref[2 * hi + 1] // UNROLL, meta_ref[2 * hi + 2] // UNROLL, far, 0)


def make_products(s, lists, a_own, a_other, near):
    smem = pl.BlockSpec(memory_space=pltpu.SMEM)
    vmem = pl.BlockSpec(memory_space=pltpu.VMEM)
    hbm = pl.BlockSpec(memory_space=pltpu.HBM)
    anywhere = pl.BlockSpec(memory_space=pl.ANY)
    block = (s.side, s.side)
    shapes = [((count,) + block, jnp.bfloat16) for count in (s.slots, s.pairs)]
    shapes += [((s.near * s.side, s.side), jnp.bfloat16)]
    a_own = pltpu.with_memory_space_constraint(a_own, pltpu.HBM)
    operands = [a_own, a_other, *near]
    return pl.pallas_call(
        functools.partial(product_kernel, s),
        in_specs=[smem] * 4 + [hbm] + [anywhere] * (len(operands) - 1),
        out_specs=vmem,
        out_shape=jax.ShapeDtypeStruct(*shapes[0]),
        scratch_shapes=[pltpu.VMEM(*shape) for shape in shapes[1:]]
        + [pltpu.SemaphoreType.DMA((len(operands),))],
        compiler_params=pltpu.CompilerParams(vmem_limit_bytes=room(*shapes)),
        cost_estimate=pl.CostEstimate(
            flops=s.pairs * s.side**3, bytes_accessed=1 << 20, transcendentals=0
        ),
    )(*lists, *operands)


def sum_kernel(
    s, plan_ref, counts, late_ref, meta_ref, aggs_ref, slots_ref, rows_ref, far0, far1,
    send0, keep0, send1, keep1, send2, keep2, total, far_buf, picked, sems,
):
    hi = pl.program_id(0)
    high = s.tiles * s.side
    copies = [
        pltpu.make_async_copy(
            ref.at[pl.ds(0, high)], far_buf.at[pl.ds(k * high, high)], sems.at[k]
        )
        for k, ref in enumerate((far0, far1))
    ]

    @pl.when(hi == 0)
    def _():
        for copy in copies:
            copy.start()

    def clear(k, carry):
        total[k] = jnp.zeros(total.shape[1:], jnp.float32)
        return carry

    lax.fori_loop(0, s.blocks, clear, 0)

    def add(entry, product):
        known = jnp.maximum(entry, 0)
        term = jnp.dot(
            rows_ref[known & (s.slab - 1)], product, preferred_element_type=jnp.float32
        )
        cell = field(s, known, 2)
        at = pl.ds(pl.multiple_of((cell & (s.per - 1)) * s.side, s.side), s.side)
        total[cell >> log2(s.per), at, :] += jnp.where(entry >= 0, term, 0.0)

    def near(group, carry):
        for u in range(UNROLL):
            n = group * UNROLL + u
            add(plan_ref[n], slots_ref[n])
        return carry

    begin = meta_ref[2 * hi]
    lax.fori_loop(begin // UNROLL, pl.cdiv(begin + counts[hi], UNROLL), near, 0)

    col = lax.axis_index("col")
    first = meta_ref[2 * hi + 1]

    def pick(n, n_mine):
        slot = first + n
        mine, part = column_part(s, aggs_ref[late_ref[slot * 2 + 1]], col)
        picked[n_mine * 2] = slot
        picked[n_mine * 2 + 1] = late_ref[slot * 2] + part
        return n_mine + jnp.where(mine, 1, 0)

    n_mine = lax.fori_loop(0, meta_ref[s.buckets + 2 + hi], pick, jnp.int32(0))
    for u in range(UNROLL):
        picked[(n_mine + u) * 2] = 0
        picked[(n_mine + u) * 2 + 1] = -1

    @pl.when(hi == 0)
    def _():
        for copy in copies:
            copy.wait()

    def far(group, carry):
        for u in range(UNROLL):
            n = group * UNROLL + u
            slot, entry = picked[n * 2], picked[n * 2 + 1]
            at = field(s, jnp.maximum(entry, 0), 1) * s.side
            piece = far_buf[pl.ds(pl.multiple_of(at, s.side), s.side), :]
            product = jnp.dot(slots_ref[slot], piece, preferred_element_type=jnp.float32)
            add(entry, product.astype(jnp.bfloat16))
        return carry

    lax.fori_loop(0, pl.cdiv(n_mine, UNROLL), far, 0)

    half = s.cols // 2
    weight = {"x": 1, "y": half, "1": 2 * half, "2": 4 * half}
    core = lax.axis_index("col") & 1
    outs = ((send0, keep0), (send1, keep1), (send2, keep2))
    for k, (send, keep) in enumerate(outs):
        for bits in itertools.product(range(2), repeat=4):
            base = [
                sum(weight[link] * bit for link, bit in zip(order, bits)) for order in ORDERS[k]
            ]
            base = jnp.where(core == 0, *base)
            for x in range(half // 2):
                part = total[base + 2 * x, s.splits[k]:s.splits[k + 1], :]
                if bits[0]:
                    send[(*bits[1:], 0, x)] = part.astype(jnp.bfloat16)
                else:
                    keep[(*bits[1:], 0, x)] = part


def make_sums(s, lists, slots, rows_t, far):
    smem = pl.BlockSpec(memory_space=pltpu.SMEM)
    vmem = pl.BlockSpec(memory_space=pltpu.VMEM)
    anywhere = pl.BlockSpec(memory_space=pl.ANY)
    shapes = [
        ((s.slots + s.slab + 2 * s.tiles, s.side, s.side), jnp.bfloat16),
        ((s.blocks, s.tall, s.side), jnp.float32),
    ]
    out_shape, out_specs = [], []
    for k in range(len(ORDERS)):
        last = (s.cols // 4, s.splits[k + 1] - s.splits[k], s.side)
        for dtype in (jnp.bfloat16, jnp.float32):
            out_shape.append(jax.ShapeDtypeStruct((2, 2, 2, s.his) + last, dtype))
            out_specs.append(
                pl.BlockSpec((2, 2, 2, 1) + last, lambda h: (0, 0, 0, h, 0, 0, 0))
            )
            shapes.append(((2 if s.his > 1 else 1, 8) + last, dtype))
    return pl.pallas_call(
        functools.partial(sum_kernel, s),
        grid=(s.his,),
        in_specs=[smem] * 5 + [vmem, vmem, anywhere, anywhere],
        out_specs=out_specs,
        out_shape=out_shape,
        scratch_shapes=[
            pltpu.VMEM((s.blocks, s.tall, s.side), jnp.float32),
            pltpu.VMEM((2 * s.tiles * s.side, s.side), jnp.bfloat16),
            pltpu.SMEM(((s.pairs + UNROLL) * 2,), jnp.int32),
            pltpu.SemaphoreType.DMA((2,)),
        ],
        compiler_params=pltpu.CompilerParams(vmem_limit_bytes=room(*shapes)),
        cost_estimate=pl.CostEstimate(
            flops=s.pairs * s.side**3, bytes_accessed=16 << 20, transcendentals=0
        ),
    )(*lists, slots, rows_t, *far)


def shards(a_blocks, p_tiles, owner, agg_local, a_cols):
    s = Sizes(
        lax.axis_size("row"), lax.axis_size("col"), p_tiles.shape[0], p_tiles.shape[1]
    )
    order = ring_order(s.rows)
    barrier = lax.optimization_barrier

    def ring(value, stream):
        moves = []
        for k in range(s.rows):
            for c in range(s.cols):
                step = 1 if (stream + c) % 2 == 0 else -1
                to = order[(k + step) % s.rows]
                moves.append((order[k] * s.cols + c, to * s.cols + c))
        return lax.ppermute(value, ("row", "col"), moves)

    high = s.tiles * s.side
    aggs = owner[:, 0] * OWN + agg_local
    label = jnp.pad(aggs.astype(jnp.bfloat16)[None], ((0, LABEL - 1), (0, s.side - s.slab)))
    mine = p_tiles.reshape(high, s.side)
    labelled = jnp.concatenate([mine, label], 0)

    first = ring(labelled, 0)
    cols = a_cols[:, 0]
    cols_other = swap(cols, "col", 1)
    cols_other, labelled = barrier((cols_other, labelled))
    second = ring(labelled, 1)
    a_other, p_other = swap(a_blocks[:, 0], "col", 1), swap(mine, "col", 1)
    rows = [mine]
    bit = 2
    while bit < s.cols:
        rows += [swap(piece, "col", bit) for piece in rows]
        bit *= 2
    rows += [p_other] + [swap(piece, "col", 1) for piece in rows[1:]]
    plan = make_plan(s, jnp.concatenate([cols, cols_other], 0), aggs)
    own_near, other_near = {0: labelled, s.rows - 1: first, 1: second}, {0: p_other}
    first, second = ring(first, 0), ring(second, 1)

    held = [1, s.rows - 1]
    for step in range(2, s.half - 1):
        came, *rest = barrier((second, *(own_near[away] for away in held)))
        for away, piece in zip(held, rest):
            other_near[away] = swap(piece, "col", 1)
        own_near[s.rows - step], own_near[step] = first, came
        first, second = ring(first, 0), ring(second, 1)
        held = [step, s.rows - step]

    others = sorted(set(other_near) - {0})
    first, *rest = barrier((first, *rows[1:]))
    rows_t = turn_rows(s, [mine, *rest])
    tie = (first, rows_t, second, *plan)
    tie += (*(own_near[away] for away in held), *(other_near[away] for away in others))
    first, rows_t, second, *rest = barrier(tie)
    plan, rest = rest[:len(plan)], rest[len(plan):]
    for away, piece in zip(others, rest[len(held):]):
        other_near[away] = piece
    far = ring(first, 0)
    own_near[s.half + 1], own_near[s.half - 1] = first, second
    for away, piece in zip(held, rest):
        other_near[away] = swap(piece, "col", 1)
    for away in (s.half + 1, s.half - 1):
        other_near[away] = swap(own_near[away], "col", 1)
    near = [own_near[k] for k in sorted(own_near)]
    lists = (*pick_near(s, plan, near), plan[1], plan[2])
    near += [other_near[k] for k in sorted(other_near)]
    slots = make_products(s, lists, a_blocks[:, 0], a_other, near)
    far, slots = barrier((far, slots))
    far_other = swap(far, "col", 1)
    lists += (far[high, :s.slab].astype(jnp.int32),)
    parts = make_sums(s, lists, slots, rows_t, [far, far_other])

    sends, keeps = list(parts[0::2]), list(parts[1::2])
    groups = range(len(ORDERS))
    moving = [exchange(sends[k], [order[0] for order in ORDERS[k]]) for k in groups]
    for step in range(1, 5):
        for k in groups:
            got = moving[k]
            if step < 4:
                send = (keeps[k][1] + got[1].astype(jnp.float32)).astype(jnp.bfloat16)
                moving[k] = exchange(send, [order[step] for order in ORDERS[k]])
                keeps[k] = keeps[k][0] + got[0].astype(jnp.float32)
            else:
                keeps[k] = keeps[k] + got.astype(jnp.float32)
    total = jnp.concatenate(keeps, -2)
    tail = [("row", 1 << k) for k in range(3, log2(s.rows))][::-1]
    tail += [("col", 1 << k) for k in range(2, log2(s.cols))][::-1]
    total = total.reshape((2,) * len(tail) + total.shape[-2:])
    for axis in tail:
        got = swap(total[1].astype(jnp.bfloat16), *axis)
        total = total[0] + got.astype(jnp.float32)
    return total.reshape(OWN, s.width, s.side, s.side)


def solution(mesh):
    in_specs = (
        P("row", "col", None, None),
        P(("row", "col"), None, None),
        P("row", None),
        P("row"),
        P("row", "col"),
    )
    out_specs = P("row", "col", None, None)
    return jax.shard_map(shards, mesh=mesh, in_specs=in_specs, out_specs=out_specs, check_vma=False)
```

```python
import functools
import itertools
import math

import jax
import jax.numpy as jnp
from jax import lax
from jax.experimental import pallas as pl
from jax.experimental.pallas import tpu as pltpu
from jax.sharding import PartitionSpec as P

OWN = 2
UNROLL = 8
ORDERS = (("yx21", "1yx2"), ("xy12", "x1y2"), ("2xy1", "y1x2"))
LINKS = {"x": ("col", 2), "y": ("row", 1), "1": ("row", 2), "2": ("row", 4)}


def ring_order(count):
    return list(range(0, count, 2)) + list(range(1, count, 2))[::-1]


def swap(value, axis, bit):
    size = lax.axis_size(axis)
    return lax.ppermute(value, axis, [(i, i ^ bit) for i in range(size)])


def exchange(value, links):
    rows, cols = lax.axis_size("row"), lax.axis_size("col")
    moves = []
    for r in range(rows):
        for c in range(cols):
            axis, bit = LINKS[links[c % 2]]
            to = (r ^ bit, c) if axis == "row" else (r, c ^ bit)
            moves.append((r * cols + c, to[0] * cols + to[1]))
    return lax.ppermute(value, ("row", "col"), moves)


def log2(size):
    power = size.bit_length() - 1
    assert size == 1 << power
    return power


class Sizes:
    def __init__(self, rows, cols, tiles, side):
        self.rows, self.cols, self.tiles, self.side = rows, cols, tiles, side
        self.slab = cols * tiles
        self.pairs = 2 * self.slab
        self.width = OWN * rows // cols
        self.per = OWN * self.width
        self.his = rows // 8
        self.blocks, self.tall = 4 * cols, self.per * side
        third = self.tall // 16 // 3 * 16
        self.splits = (0, third, 2 * third, self.tall)
        self.buckets = 2 * self.his
        self.slots = self.pairs + self.buckets * UNROLL
        self.half = rows // 2
        self.early = rows - 1
        self.near = 2 * self.early * tiles
        self.fields, shift = [], 0
        for size in (self.pairs, 2 * rows * tiles, self.blocks * self.per):
            self.fields.append((shift, size - 1))
            shift += log2(size)
        assert shift <= 31


def field(s, entry, k):
    shift, mask = s.fields[k]
    return (entry >> shift) & mask


def plan_kernel(s, cols_ref, aggs_ref, plan_ref, starts_ref, info, counts):
    row = lax.axis_index("row")
    col = lax.axis_index("col")

    def ring_place(index):
        return jnp.where((index & 1) == 0, index >> 1, s.rows - 1 - (index >> 1))

    here = ring_place(row)
    for b in range(s.buckets):
        counts[b] = 0

    def blank(k, carry):
        plan_ref[k] = -1
        return carry

    lax.fori_loop(0, s.slots + 1, blank, 0, unroll=8)

    def sort(i, carry):
        tile = i & (s.slab - 1)
        side = i >> log2(s.slab)
        other = cols_ref[i]
        other_row = other >> log2(s.slab)
        i_agg = aggs_ref[tile]
        j_agg = aggs_ref[((other_row ^ row) << log2(s.slab)) + (other & (s.slab - 1))]
        rel_col = (j_agg >> log2(s.width)) ^ col
        rel_row = (i_agg >> log2(OWN)) ^ row
        turn = ring_place(other_row) - here
        away = jnp.where(((col ^ side) & 1) == 0, turn, -turn) & (s.rows - 1)
        late = jnp.where(away == s.half, 1, 0)
        order = away - jnp.where(away > s.half, 1, 0) + side * s.early
        piece = jnp.where(late == 1, side, order)
        panel_at = (piece << log2(s.tiles)) + (other & (s.tiles - 1))
        cell = (rel_row & 7) * (s.cols // 2) + (rel_col >> 1)
        cell = (cell << log2(OWN)) + (i_agg & (OWN - 1))
        cell = (cell << log2(s.width)) + (j_agg & (s.width - 1))
        bucket = (rel_row >> 3) * 2 + late
        mine = (rel_col & 1) == 0
        rank = counts[bucket]
        counts[bucket] = rank + jnp.where(mine, 1, 0)
        info[i * 2] = jnp.where(mine, rank * s.buckets + bucket, -1)
        entry = i
        for k, value in enumerate((panel_at, cell)):
            entry = entry + (value << s.fields[k + 1][0])
        info[i * 2 + 1] = entry
        return carry

    lax.fori_loop(0, s.pairs, sort, 0, unroll=4)

    start = jnp.int32(0)
    for b in range(s.buckets):
        starts_ref[b] = start
        start = start + ((counts[b] + UNROLL - 1) & ~(UNROLL - 1))
    starts_ref[s.buckets] = start

    def place(i, carry):
        key = info[i * 2]
        slot = starts_ref[key & (s.buckets - 1)] + (key >> log2(s.buckets))
        plan_ref[jnp.where(key >= 0, slot, s.slots)] = info[i * 2 + 1]
        return carry

    lax.fori_loop(0, s.pairs, place, 0, unroll=4)


def room(*shapes):
    total = sum(math.prod(shape) * jnp.dtype(dtype).itemsize for shape, dtype in shapes)
    return total + (2 << 20)


def make_plan(s, cols, aggs):
    smem = pl.BlockSpec(memory_space=pltpu.SMEM)
    return pl.pallas_call(
        functools.partial(plan_kernel, s),
        in_specs=[smem, smem],
        out_specs=[smem, smem],
        out_shape=[
            jax.ShapeDtypeStruct((s.slots + 1,), jnp.int32),
            jax.ShapeDtypeStruct((s.buckets + 1,), jnp.int32),
        ],
        scratch_shapes=[
            pltpu.SMEM((s.pairs * 2,), jnp.int32),
            pltpu.SMEM((s.buckets,), jnp.int32),
        ],
        compiler_params=pltpu.CompilerParams(vmem_limit_bytes=room()),
        cost_estimate=pl.CostEstimate(flops=1 << 20, bytes_accessed=16 << 20, transcendentals=0),
    )(cols, aggs)


def turn_kernel(s, *refs):
    rows_ref, rows_buf, sems = refs[-3:]
    copies = [
        pltpu.make_async_copy(refs[k], rows_buf.at[pl.ds(k * s.tiles, s.tiles)], sems.at[k])
        for k in range(s.cols)
    ]
    for copy in copies:
        copy.start()
    for copy in copies:
        copy.wait()
    col = lax.axis_index("col")

    def turn(k, carry):
        part = k >> log2(s.tiles)
        rel = (part & (s.cols // 2 - 1)) * 2 + (part >> log2(s.cols // 2))
        rows_ref[((rel ^ col) << log2(s.tiles)) + (k & (s.tiles - 1))] = rows_buf[k].T
        return carry

    lax.fori_loop(0, s.slab, turn, 0, unroll=4)


def turn_rows(s, rows):
    own = pltpu.with_memory_space_constraint(rows[0], pltpu.HBM)
    shape = ((s.slab, s.side, s.side), jnp.bfloat16)
    return pl.pallas_call(
        functools.partial(turn_kernel, s),
        in_specs=[pl.BlockSpec(memory_space=pltpu.HBM)]
        + [pl.BlockSpec(memory_space=pl.ANY)] * (s.cols - 1),
        out_specs=pl.BlockSpec(memory_space=pltpu.VMEM),
        out_shape=jax.ShapeDtypeStruct(*shape),
        scratch_shapes=[pltpu.VMEM(*shape), pltpu.SemaphoreType.DMA((s.cols,))],
        compiler_params=pltpu.CompilerParams(vmem_limit_bytes=room(shape, shape)),
        cost_estimate=pl.CostEstimate(flops=0, bytes_accessed=0, transcendentals=0),
    )(own, *rows[1:])


def product_kernel(s, plan_ref, starts_ref, *refs):
    slots_ref, a_buf, panel, sems = refs[-4:]
    copies = []
    for k in range(2):
        copies.append((refs[k], a_buf.at[pl.ds(k * s.slab, s.slab)]))
    for k in range(2 * s.early):
        copies.append((refs[2 + k], panel.at[pl.ds(k * s.tiles, s.tiles)]))
    copies = [pltpu.make_async_copy(src, dst, sems.at[k]) for k, (src, dst) in enumerate(copies)]
    for copy in copies:
        copy.start()
    for copy in copies:
        copy.wait()

    for hi in range(s.his):
        begin = starts_ref[2 * hi] // UNROLL
        middle = starts_ref[2 * hi + 1] // UNROLL
        end = starts_ref[2 * hi + 2] // UNROLL

        def near(group, carry):
            for u in range(UNROLL):
                n = group * UNROLL + u
                entry = jnp.maximum(plan_ref[n], 0)
                slots_ref[n] = jnp.dot(
                    a_buf[field(s, entry, 0)],
                    panel[field(s, entry, 1)],
                    preferred_element_type=jnp.float32,
                ).astype(jnp.bfloat16)
            return carry

        def far(group, carry):
            for u in range(UNROLL):
                n = group * UNROLL + u
                slots_ref[n] = a_buf[field(s, jnp.maximum(plan_ref[n], 0), 0)]
            return carry

        lax.fori_loop(begin, middle, near, 0)
        lax.fori_loop(middle, end, far, 0)


def make_products(s, plan, starts, a_own, a_other, near):
    smem = pl.BlockSpec(memory_space=pltpu.SMEM)
    hbm = pl.BlockSpec(memory_space=pltpu.HBM)
    anywhere = pl.BlockSpec(memory_space=pl.ANY)
    shapes = [
        ((count, s.side, s.side), jnp.bfloat16) for count in (s.slots, s.pairs, s.near)
    ]
    a_own, own = (pltpu.with_memory_space_constraint(x, pltpu.HBM) for x in (a_own, near[0]))
    operands = [a_own, a_other, own, *near[1:]]
    return pl.pallas_call(
        functools.partial(product_kernel, s),
        in_specs=[smem, smem, hbm, anywhere, hbm] + [anywhere] * (len(operands) - 3),
        out_specs=pl.BlockSpec(memory_space=pltpu.VMEM),
        out_shape=jax.ShapeDtypeStruct(*shapes[0]),
        scratch_shapes=[pltpu.VMEM(*shape) for shape in shapes[1:]]
        + [pltpu.SemaphoreType.DMA((len(operands),))],
        compiler_params=pltpu.CompilerParams(vmem_limit_bytes=room(*shapes)),
        cost_estimate=pl.CostEstimate(
            flops=s.pairs * s.side**3, bytes_accessed=1 << 20, transcendentals=0
        ),
    )(plan, starts, *operands)


def sum_kernel(
    s, plan_ref, starts_ref, slots_ref, rows_ref, far0, far1,
    send0, keep0, send1, keep1, send2, keep2, total, far_buf, sems,
):
    hi = pl.program_id(0)
    copies = [
        pltpu.make_async_copy(ref, far_buf.at[pl.ds(k * s.tiles, s.tiles)], sems.at[k])
        for k, ref in enumerate((far0, far1))
    ]

    @pl.when(hi == 0)
    def _():
        for copy in copies:
            copy.start()

    def clear(k, carry):
        total[k] = jnp.zeros(total.shape[1:], jnp.float32)
        return carry

    lax.fori_loop(0, s.blocks, clear, 0)

    def add(n, product):
        entry = plan_ref[n]
        known = jnp.maximum(entry, 0)
        term = jnp.dot(
            rows_ref[known & (s.slab - 1)], product, preferred_element_type=jnp.float32
        )
        cell = field(s, known, 2)
        at = pl.ds(pl.multiple_of((cell & (s.per - 1)) * s.side, s.side), s.side)
        total[cell >> log2(s.per), at, :] += jnp.where(entry >= 0, term, 0.0)

    def near(group, carry):
        for u in range(UNROLL):
            n = group * UNROLL + u
            add(n, slots_ref[n])
        return carry

    def far(group, carry):
        for u in range(UNROLL):
            n = group * UNROLL + u
            piece = far_buf[field(s, jnp.maximum(plan_ref[n], 0), 1)]
            product = jnp.dot(slots_ref[n], piece, preferred_element_type=jnp.float32)
            add(n, product.astype(jnp.bfloat16))
        return carry

    begin = starts_ref[2 * hi] // UNROLL
    middle = starts_ref[2 * hi + 1] // UNROLL
    end = starts_ref[2 * hi + 2] // UNROLL
    lax.fori_loop(begin, middle, near, 0)

    @pl.when(hi == 0)
    def _():
        for copy in copies:
            copy.wait()

    lax.fori_loop(middle, end, far, 0)

    half = s.cols // 2
    weight = {"x": 1, "y": half, "1": 2 * half, "2": 4 * half}
    core = lax.axis_index("col") & 1
    outs = ((send0, keep0), (send1, keep1), (send2, keep2))
    for k, (send, keep) in enumerate(outs):
        for bits in itertools.product(range(2), repeat=4):
            base = [
                sum(weight[link] * bit for link, bit in zip(order, bits)) for order in ORDERS[k]
            ]
            base = jnp.where(core == 0, *base)
            for x in range(half // 2):
                part = total[base + 2 * x, s.splits[k]:s.splits[k + 1], :]
                if bits[0]:
                    send[(*bits[1:], 0, x)] = part.astype(jnp.bfloat16)
                else:
                    keep[(*bits[1:], 0, x)] = part


def make_sums(s, plan, starts, slots, rows_t, far):
    smem = pl.BlockSpec(memory_space=pltpu.SMEM)
    vmem = pl.BlockSpec(memory_space=pltpu.VMEM)
    anywhere = pl.BlockSpec(memory_space=pl.ANY)
    shapes = [
        ((s.slots + s.slab + 2 * s.tiles, s.side, s.side), jnp.bfloat16),
        ((s.blocks, s.tall, s.side), jnp.float32),
    ]
    out_shape, out_specs = [], []
    for k in range(len(ORDERS)):
        last = (s.cols // 4, s.splits[k + 1] - s.splits[k], s.side)
        for dtype in (jnp.bfloat16, jnp.float32):
            out_shape.append(jax.ShapeDtypeStruct((2, 2, 2, s.his) + last, dtype))
            out_specs.append(
                pl.BlockSpec((2, 2, 2, 1) + last, lambda h: (0, 0, 0, h, 0, 0, 0))
            )
            shapes.append(((2 if s.his > 1 else 1, 8) + last, dtype))
    return pl.pallas_call(
        functools.partial(sum_kernel, s),
        grid=(s.his,),
        in_specs=[smem, smem, vmem, vmem, anywhere, anywhere],
        out_specs=out_specs,
        out_shape=out_shape,
        scratch_shapes=[
            pltpu.VMEM((s.blocks, s.tall, s.side), jnp.float32),
            pltpu.VMEM((2 * s.tiles, s.side, s.side), jnp.bfloat16),
            pltpu.SemaphoreType.DMA((2,)),
        ],
        compiler_params=pltpu.CompilerParams(vmem_limit_bytes=room(*shapes)),
        cost_estimate=pl.CostEstimate(
            flops=s.pairs * s.side**3, bytes_accessed=16 << 20, transcendentals=0
        ),
    )(plan, starts, slots, rows_t, *far)


def shards(a_blocks, p_tiles, owner, agg_local, a_cols):
    s = Sizes(
        lax.axis_size("row"), lax.axis_size("col"), p_tiles.shape[0], p_tiles.shape[1]
    )
    order = ring_order(s.rows)
    barrier = lax.optimization_barrier

    def ring(value, stream):
        moves = []
        for k in range(s.rows):
            for c in range(s.cols):
                step = 1 if (stream + c) % 2 == 0 else -1
                to = order[(k + step) % s.rows]
                moves.append((order[k] * s.cols + c, to * s.cols + c))
        return lax.ppermute(value, ("row", "col"), moves)

    first = ring(p_tiles, 0)
    cols = a_cols[:, 0]
    cols_other = swap(cols, "col", 1)
    cols_other, mine = barrier((cols_other, p_tiles))
    second = ring(mine, 1)
    a_other, p_other = swap(a_blocks[:, 0], "col", 1), swap(p_tiles, "col", 1)

    aggs = owner[:, 0] * OWN + agg_local
    came, aggs, a_other, p_other = barrier((first, aggs, a_other, p_other))
    first = ring(first, 0)
    aggs = [aggs] + [swap(aggs, "row", mask) for mask in (1, 2, 3)]
    own_near, other_near = {0: p_tiles, s.rows - 1: came, 1: second}, {0: p_other}
    second = ring(second, 1)
    aggs, mine = barrier((jnp.concatenate(aggs, 0), p_tiles))
    bit = 4
    while bit < s.rows:
        aggs = jnp.concatenate([aggs, swap(aggs, "row", bit)], 0)
        bit *= 2
    rows = [mine]
    bit = 2
    while bit < s.cols:
        rows += [swap(piece, "col", bit) for piece in rows]
        bit *= 2
    plan, starts = make_plan(s, jnp.concatenate([cols, cols_other], 0), aggs)

    held = [1, s.rows - 1]
    for step in range(2, s.half - 1):
        came, *rest = barrier((second, *(own_near[away] for away in held), *rows[1:]))
        for away, piece in zip(held, rest):
            other_near[away] = swap(piece, "col", 1)
        if step == 2:
            rows += [p_other] + [swap(piece, "col", 1) for piece in rest[len(held):]]
        own_near[s.rows - step], own_near[step] = first, came
        first, second = ring(first, 0), ring(second, 1)
        held = [step, s.rows - step]

    others = sorted(set(other_near) - {0})
    rows_t = turn_rows(s, rows)
    tie = (first, second, plan, starts, rows_t)
    tie += (*(own_near[away] for away in held), *(other_near[away] for away in others))
    first, second, plan, starts, rows_t, *rest = barrier(tie)
    for away, piece in zip(others, rest[len(held):]):
        other_near[away] = piece
    far = ring(first, 0)
    own_near[s.half + 1], own_near[s.half - 1] = first, second
    for away, piece in zip(held, rest):
        other_near[away] = swap(piece, "col", 1)
    for away in (s.half + 1, s.half - 1):
        other_near[away] = swap(own_near[away], "col", 1)
    near = [own_near[k] for k in sorted(own_near)]
    near += [other_near[k] for k in sorted(other_near)]
    slots = make_products(s, plan, starts, a_blocks[:, 0], a_other, near)
    far, slots = barrier((far, slots))
    far_other = swap(far, "col", 1)
    parts = make_sums(s, plan, starts, slots, rows_t, [far, far_other])

    sends, keeps = list(parts[0::2]), list(parts[1::2])
    groups = range(len(ORDERS))
    moving = [exchange(sends[k], [order[0] for order in ORDERS[k]]) for k in groups]
    for step in range(1, 5):
        for k in groups:
            got = moving[k]
            if step < 4:
                send = (keeps[k][1] + got[1].astype(jnp.float32)).astype(jnp.bfloat16)
                moving[k] = exchange(send, [order[step] for order in ORDERS[k]])
                keeps[k] = keeps[k][0] + got[0].astype(jnp.float32)
            else:
                keeps[k] = keeps[k] + got.astype(jnp.float32)
    total = jnp.concatenate(keeps, -2)
    tail = [("row", 1 << k) for k in range(3, log2(s.rows))][::-1]
    tail += [("col", 1 << k) for k in range(2, log2(s.cols))][::-1]
    total = total.reshape((2,) * len(tail) + total.shape[-2:])
    for axis in tail:
        got = swap(total[1].astype(jnp.bfloat16), *axis)
        total = total[0] + got.astype(jnp.float32)
    return total.reshape(OWN, s.width, s.side, s.side)


def solution(mesh):
    in_specs = (
        P("row", "col", None, None),
        P(("row", "col"), None, None),
        P("row", None),
        P("row"),
        P("row", "col"),
    )
    out_specs = P("row", "col", None, None)
    return jax.shard_map(shards, mesh=mesh, in_specs=in_specs, out_specs=out_specs, check_vma=False)
```

```python
import functools
import itertools
import math

import jax
import jax.numpy as jnp
from jax import lax
from jax.experimental import pallas as pl
from jax.experimental.pallas import tpu as pltpu
from jax.sharding import PartitionSpec as P

OWN = 2
UNROLL = 8
ORDERS = (("xy12", "1yx2"), ("yx12", "2yx1"))
LINKS = {"x": ("col", 2), "y": ("row", 1), "1": ("row", 2), "2": ("row", 4)}


def ring_order(count):
    return list(range(0, count, 2)) + list(range(1, count, 2))[::-1]


def swap(value, axis, bit):
    size = lax.axis_size(axis)
    return lax.ppermute(value, axis, [(i, i ^ bit) for i in range(size)])


def exchange(value, links):
    rows, cols = lax.axis_size("row"), lax.axis_size("col")
    moves = []
    for r in range(rows):
        for c in range(cols):
            axis, bit = LINKS[links[c % 2]]
            to = (r ^ bit, c) if axis == "row" else (r, c ^ bit)
            moves.append((r * cols + c, to[0] * cols + to[1]))
    return lax.ppermute(value, ("row", "col"), moves)


def log2(size):
    power = size.bit_length() - 1
    assert size == 1 << power
    return power


class Sizes:
    def __init__(self, rows, cols, tiles, side):
        self.rows, self.cols, self.tiles, self.side = rows, cols, tiles, side
        self.slab = cols * tiles
        self.pairs = 2 * self.slab
        self.width = OWN * rows // cols
        self.per = OWN * self.width
        self.his = rows // 8
        self.blocks, self.tall = 4 * cols, self.per * side
        share = self.tall // 16 // len(ORDERS) * 16
        self.splits = tuple(share * k for k in range(len(ORDERS))) + (self.tall,)
        self.buckets = 2 * self.his
        self.slots = self.pairs + self.buckets * UNROLL
        self.half = rows // 2
        self.early = rows - 1
        self.near = 2 * self.early * tiles
        self.fields, shift = [], 0
        for size in (self.pairs, 2 * rows * tiles, self.blocks * self.per):
            self.fields.append((shift, size - 1))
            shift += log2(size)
        assert shift <= 31


def field(s, entry, k):
    shift, mask = s.fields[k]
    return (entry >> shift) & mask


def plan_kernel(s, cols_ref, aggs_ref, plan_ref, starts_ref, info, counts):
    row = lax.axis_index("row")
    col = lax.axis_index("col")

    def ring_place(index):
        return jnp.where((index & 1) == 0, index >> 1, s.rows - 1 - (index >> 1))

    here = ring_place(row)
    for b in range(s.buckets):
        counts[b] = 0

    def blank(k, carry):
        plan_ref[k] = -1
        return carry

    lax.fori_loop(0, s.slots + 1, blank, 0, unroll=8)

    def sort(i, carry):
        tile = i & (s.slab - 1)
        side = i >> log2(s.slab)
        other = cols_ref[i]
        other_row = other >> log2(s.slab)
        i_agg = aggs_ref[tile]
        j_agg = aggs_ref[((other_row ^ row) << log2(s.slab)) + (other & (s.slab - 1))]
        rel_col = (j_agg >> log2(s.width)) ^ col
        rel_row = (i_agg >> log2(OWN)) ^ row
        turn = ring_place(other_row) - here
        away = jnp.where(((col ^ side) & 1) == 0, turn, -turn) & (s.rows - 1)
        late = jnp.where(away == s.half, 1, 0)
        order = away - jnp.where(away > s.half, 1, 0) + side * s.early
        piece = jnp.where(late == 1, side, order)
        panel_at = (piece << log2(s.tiles)) + (other & (s.tiles - 1))
        cell = (rel_row & 7) * (s.cols // 2) + (rel_col >> 1)
        cell = (cell << log2(OWN)) + (i_agg & (OWN - 1))
        cell = (cell << log2(s.width)) + (j_agg & (s.width - 1))
        bucket = (rel_row >> 3) * 2 + late
        mine = (rel_col & 1) == 0
        rank = counts[bucket]
        counts[bucket] = rank + jnp.where(mine, 1, 0)
        info[i * 2] = jnp.where(mine, rank * s.buckets + bucket, -1)
        entry = i
        for k, value in enumerate((panel_at, cell)):
            entry = entry + (value << s.fields[k + 1][0])
        info[i * 2 + 1] = entry
        return carry

    lax.fori_loop(0, s.pairs, sort, 0, unroll=4)

    start = jnp.int32(0)
    for b in range(s.buckets):
        starts_ref[b] = start
        start = start + ((counts[b] + UNROLL - 1) & ~(UNROLL - 1))
    starts_ref[s.buckets] = start

    def place(i, carry):
        key = info[i * 2]
        slot = starts_ref[key & (s.buckets - 1)] + (key >> log2(s.buckets))
        plan_ref[jnp.where(key >= 0, slot, s.slots)] = info[i * 2 + 1]
        return carry

    lax.fori_loop(0, s.pairs, place, 0, unroll=4)


def room(*shapes):
    total = sum(math.prod(shape) * jnp.dtype(dtype).itemsize for shape, dtype in shapes)
    return total + (2 << 20)


def make_plan(s, cols, aggs):
    smem = pl.BlockSpec(memory_space=pltpu.SMEM)
    return pl.pallas_call(
        functools.partial(plan_kernel, s),
        in_specs=[smem, smem],
        out_specs=[smem, smem],
        out_shape=[
            jax.ShapeDtypeStruct((s.slots + 1,), jnp.int32),
            jax.ShapeDtypeStruct((s.buckets + 1,), jnp.int32),
        ],
        scratch_shapes=[
            pltpu.SMEM((s.pairs * 2,), jnp.int32),
            pltpu.SMEM((s.buckets,), jnp.int32),
        ],
        compiler_params=pltpu.CompilerParams(vmem_limit_bytes=room()),
        cost_estimate=pl.CostEstimate(flops=1 << 20, bytes_accessed=16 << 20, transcendentals=0),
    )(cols, aggs)


def turn_kernel(s, *refs):
    rows_ref, rows_buf, sems = refs[-3:]
    copies = [
        pltpu.make_async_copy(refs[k], rows_buf.at[pl.ds(k * s.tiles, s.tiles)], sems.at[k])
        for k in range(s.cols)
    ]
    for copy in copies:
        copy.start()
    for copy in copies:
        copy.wait()
    col = lax.axis_index("col")

    def turn(k, carry):
        part = k >> log2(s.tiles)
        rel = (part & (s.cols // 2 - 1)) * 2 + (part >> log2(s.cols // 2))
        rows_ref[((rel ^ col) << log2(s.tiles)) + (k & (s.tiles - 1))] = rows_buf[k].T
        return carry

    lax.fori_loop(0, s.slab, turn, 0, unroll=4)


def turn_rows(s, rows):
    own = pltpu.with_memory_space_constraint(rows[0], pltpu.HBM)
    shape = ((s.slab, s.side, s.side), jnp.bfloat16)
    return pl.pallas_call(
        functools.partial(turn_kernel, s),
        in_specs=[pl.BlockSpec(memory_space=pltpu.HBM)]
        + [pl.BlockSpec(memory_space=pl.ANY)] * (s.cols - 1),
        out_specs=pl.BlockSpec(memory_space=pltpu.VMEM),
        out_shape=jax.ShapeDtypeStruct(*shape),
        scratch_shapes=[pltpu.VMEM(*shape), pltpu.SemaphoreType.DMA((s.cols,))],
        compiler_params=pltpu.CompilerParams(vmem_limit_bytes=room(shape, shape)),
        cost_estimate=pl.CostEstimate(flops=0, bytes_accessed=0, transcendentals=0),
    )(own, *rows[1:])


def product_kernel(s, plan_ref, starts_ref, *refs):
    slots_ref, a_buf, panel, sems = refs[-4:]
    copies = []
    for k in range(2):
        copies.append((refs[k], a_buf.at[pl.ds(k * s.slab, s.slab)]))
    for k in range(2 * s.early):
        copies.append((refs[2 + k], panel.at[pl.ds(k * s.tiles, s.tiles)]))
    copies = [pltpu.make_async_copy(src, dst, sems.at[k]) for k, (src, dst) in enumerate(copies)]
    for copy in copies:
        copy.start()
    for copy in copies:
        copy.wait()

    for hi in range(s.his):
        begin = starts_ref[2 * hi] // UNROLL
        middle = starts_ref[2 * hi + 1] // UNROLL
        end = starts_ref[2 * hi + 2] // UNROLL

        def near(group, carry):
            for u in range(UNROLL):
                n = group * UNROLL + u
                entry = jnp.maximum(plan_ref[n], 0)
                slots_ref[n] = jnp.dot(
                    a_buf[field(s, entry, 0)],
                    panel[field(s, entry, 1)],
                    preferred_element_type=jnp.float32,
                ).astype(jnp.bfloat16)
            return carry

        def far(group, carry):
            for u in range(UNROLL):
                n = group * UNROLL + u
                slots_ref[n] = a_buf[field(s, jnp.maximum(plan_ref[n], 0), 0)]
            return carry

        lax.fori_loop(begin, middle, near, 0)
        lax.fori_loop(middle, end, far, 0)


def make_products(s, plan, starts, a_own, a_other, near):
    smem = pl.BlockSpec(memory_space=pltpu.SMEM)
    hbm = pl.BlockSpec(memory_space=pltpu.HBM)
    anywhere = pl.BlockSpec(memory_space=pl.ANY)
    shapes = [
        ((count, s.side, s.side), jnp.bfloat16) for count in (s.slots, s.pairs, s.near)
    ]
    a_own, own = (pltpu.with_memory_space_constraint(x, pltpu.HBM) for x in (a_own, near[0]))
    operands = [a_own, a_other, own, *near[1:]]
    return pl.pallas_call(
        functools.partial(product_kernel, s),
        in_specs=[smem, smem, hbm, anywhere, hbm] + [anywhere] * (len(operands) - 3),
        out_specs=pl.BlockSpec(memory_space=pltpu.VMEM),
        out_shape=jax.ShapeDtypeStruct(*shapes[0]),
        scratch_shapes=[pltpu.VMEM(*shape) for shape in shapes[1:]]
        + [pltpu.SemaphoreType.DMA((len(operands),))],
        compiler_params=pltpu.CompilerParams(vmem_limit_bytes=room(*shapes)),
        cost_estimate=pl.CostEstimate(
            flops=s.pairs * s.side**3, bytes_accessed=1 << 20, transcendentals=0
        ),
    )(plan, starts, *operands)


def sum_kernel(s, plan_ref, starts_ref, slots_ref, rows_ref, far0, far1, *refs):
    outs, (total, far_buf, sems) = refs[:-3], refs[-3:]
    hi = pl.program_id(0)
    copies = [
        pltpu.make_async_copy(ref, far_buf.at[pl.ds(k * s.tiles, s.tiles)], sems.at[k])
        for k, ref in enumerate((far0, far1))
    ]

    @pl.when(hi == 0)
    def _():
        for copy in copies:
            copy.start()

    def clear(k, carry):
        total[k] = jnp.zeros(total.shape[1:], jnp.float32)
        return carry

    lax.fori_loop(0, s.blocks, clear, 0)

    def add(n, product):
        entry = plan_ref[n]
        known = jnp.maximum(entry, 0)
        term = jnp.dot(
            rows_ref[known & (s.slab - 1)], product, preferred_element_type=jnp.float32
        )
        cell = field(s, known, 2)
        at = pl.ds(pl.multiple_of((cell & (s.per - 1)) * s.side, s.side), s.side)
        total[cell >> log2(s.per), at, :] += jnp.where(entry >= 0, term, 0.0)

    def near(group, carry):
        for u in range(UNROLL):
            n = group * UNROLL + u
            add(n, slots_ref[n])
        return carry

    def far(group, carry):
        for u in range(UNROLL):
            n = group * UNROLL + u
            piece = far_buf[field(s, jnp.maximum(plan_ref[n], 0), 1)]
            product = jnp.dot(slots_ref[n], piece, preferred_element_type=jnp.float32)
            add(n, product.astype(jnp.bfloat16))
        return carry

    begin = starts_ref[2 * hi] // UNROLL
    middle = starts_ref[2 * hi + 1] // UNROLL
    end = starts_ref[2 * hi + 2] // UNROLL
    lax.fori_loop(begin, middle, near, 0)

    @pl.when(hi == 0)
    def _():
        for copy in copies:
            copy.wait()

    lax.fori_loop(middle, end, far, 0)

    half = s.cols // 2
    weight = {"x": 1, "y": half, "1": 2 * half, "2": 4 * half}
    core = lax.axis_index("col") & 1
    for k, (send, keep) in enumerate(zip(outs[0::2], outs[1::2])):
        for bits in itertools.product(range(2), repeat=4):
            base = [
                sum(weight[link] * bit for link, bit in zip(order, bits)) for order in ORDERS[k]
            ]
            base = jnp.where(core == 0, *base)
            for x in range(half // 2):
                part = total[base + 2 * x, s.splits[k]:s.splits[k + 1], :]
                if bits[0]:
                    send[(*bits[1:], 0, x)] = part.astype(jnp.bfloat16)
                else:
                    keep[(*bits[1:], 0, x)] = part


def make_sums(s, plan, starts, slots, rows_t, far):
    smem = pl.BlockSpec(memory_space=pltpu.SMEM)
    vmem = pl.BlockSpec(memory_space=pltpu.VMEM)
    anywhere = pl.BlockSpec(memory_space=pl.ANY)
    shapes = [
        ((s.slots + s.slab + 2 * s.tiles, s.side, s.side), jnp.bfloat16),
        ((s.blocks, s.tall, s.side), jnp.float32),
    ]
    out_shape, out_specs = [], []
    for k in range(len(ORDERS)):
        last = (s.cols // 4, s.splits[k + 1] - s.splits[k], s.side)
        for dtype in (jnp.bfloat16, jnp.float32):
            out_shape.append(jax.ShapeDtypeStruct((2, 2, 2, s.his) + last, dtype))
            out_specs.append(
                pl.BlockSpec((2, 2, 2, 1) + last, lambda h: (0, 0, 0, h, 0, 0, 0))
            )
            shapes.append(((2 if s.his > 1 else 1, 8) + last, dtype))
    return pl.pallas_call(
        functools.partial(sum_kernel, s),
        grid=(s.his,),
        in_specs=[smem, smem, vmem, vmem, anywhere, anywhere],
        out_specs=out_specs,
        out_shape=out_shape,
        scratch_shapes=[
            pltpu.VMEM((s.blocks, s.tall, s.side), jnp.float32),
            pltpu.VMEM((2 * s.tiles, s.side, s.side), jnp.bfloat16),
            pltpu.SemaphoreType.DMA((2,)),
        ],
        compiler_params=pltpu.CompilerParams(vmem_limit_bytes=room(*shapes)),
        cost_estimate=pl.CostEstimate(
            flops=s.pairs * s.side**3, bytes_accessed=16 << 20, transcendentals=0
        ),
    )(plan, starts, slots, rows_t, *far)


def shards(a_blocks, p_tiles, owner, agg_local, a_cols):
    s = Sizes(
        lax.axis_size("row"), lax.axis_size("col"), p_tiles.shape[0], p_tiles.shape[1]
    )
    order = ring_order(s.rows)
    barrier = lax.optimization_barrier

    def ring(value, stream):
        moves = []
        for k in range(s.rows):
            for c in range(s.cols):
                step = 1 if (stream + c) % 2 == 0 else -1
                to = order[(k + step) % s.rows]
                moves.append((order[k] * s.cols + c, to * s.cols + c))
        return lax.ppermute(value, ("row", "col"), moves)

    first = ring(p_tiles, 0)
    cols = a_cols[:, 0]
    cols_other = swap(cols, "col", 1)
    cols_other, mine = barrier((cols_other, p_tiles))
    second = ring(mine, 1)
    a_other, p_other = swap(a_blocks[:, 0], "col", 1), swap(p_tiles, "col", 1)

    aggs = owner[:, 0] * OWN + agg_local
    came, aggs, a_other, p_other = barrier((first, aggs, a_other, p_other))
    first = ring(first, 0)
    aggs = [aggs] + [swap(aggs, "row", mask) for mask in (1, 2, 3)]
    own_near, other_near = {0: p_tiles, s.rows - 1: came, 1: second}, {0: p_other}
    second = ring(second, 1)
    aggs, mine = barrier((jnp.concatenate(aggs, 0), p_tiles))
    bit = 4
    while bit < s.rows:
        aggs = jnp.concatenate([aggs, swap(aggs, "row", bit)], 0)
        bit *= 2
    rows = [mine]
    bit = 2
    while bit < s.cols:
        rows += [swap(piece, "col", bit) for piece in rows]
        bit *= 2
    plan, starts = make_plan(s, jnp.concatenate([cols, cols_other], 0), aggs)

    held = [1, s.rows - 1]
    for step in range(2, s.half - 1):
        came, *rest = barrier((second, *(own_near[away] for away in held), *rows[1:]))
        for away, piece in zip(held, rest):
            other_near[away] = swap(piece, "col", 1)
        if step == 2:
            rows += [p_other] + [swap(piece, "col", 1) for piece in rest[len(held):]]
        own_near[s.rows - step], own_near[step] = first, came
        first, second = ring(first, 0), ring(second, 1)
        held = [step, s.rows - step]

    others = sorted(set(other_near) - {0})
    rows_t = turn_rows(s, rows)
    tie = (first, second, plan, starts, rows_t)
    tie += (*(own_near[away] for away in held), *(other_near[away] for away in others))
    first, second, plan, starts, rows_t, *rest = barrier(tie)
    for away, piece in zip(others, rest[len(held):]):
        other_near[away] = piece
    far = ring(first, 0)
    own_near[s.half + 1], own_near[s.half - 1] = first, second
    for away, piece in zip(held, rest):
        other_near[away] = swap(piece, "col", 1)
    for away in (s.half + 1, s.half - 1):
        other_near[away] = swap(own_near[away], "col", 1)
    near = [own_near[k] for k in sorted(own_near)]
    near += [other_near[k] for k in sorted(other_near)]
    slots = make_products(s, plan, starts, a_blocks[:, 0], a_other, near)
    far, slots = barrier((far, slots))
    far_other = swap(far, "col", 1)
    parts = make_sums(s, plan, starts, slots, rows_t, [far, far_other])

    sends, keeps = list(parts[0::2]), list(parts[1::2])
    groups = range(len(ORDERS))
    moving = [exchange(sends[k], [order[0] for order in ORDERS[k]]) for k in groups]
    for step in range(1, 5):
        for k in groups:
            got = moving[k]
            if step < 4:
                send = (keeps[k][1] + got[1].astype(jnp.float32)).astype(jnp.bfloat16)
                moving[k] = exchange(send, [order[step] for order in ORDERS[k]])
                keeps[k] = keeps[k][0] + got[0].astype(jnp.float32)
            else:
                keeps[k] = keeps[k] + got.astype(jnp.float32)
    total = jnp.concatenate(keeps, -2)
    tail = [("row", 1 << k) for k in range(3, log2(s.rows))][::-1]
    tail += [("col", 1 << k) for k in range(2, log2(s.cols))][::-1]
    total = total.reshape((2,) * len(tail) + total.shape[-2:])
    for axis in tail:
        got = swap(total[1].astype(jnp.bfloat16), *axis)
        total = total[0] + got.astype(jnp.float32)
    return total.reshape(OWN, s.width, s.side, s.side)


def solution(mesh):
    in_specs = (
        P("row", "col", None, None),
        P(("row", "col"), None, None),
        P("row", None),
        P("row"),
        P("row", "col"),
    )
    out_specs = P("row", "col", None, None)
    return jax.shard_map(shards, mesh=mesh, in_specs=in_specs, out_specs=out_specs, check_vma=False)
```

```python
import functools
import itertools
import math

import jax
import jax.numpy as jnp
from jax import lax
from jax.experimental import pallas as pl
from jax.experimental.pallas import tpu as pltpu
from jax.sharding import PartitionSpec as P

OWN = 2
UNROLL = 8
ORDERS = (("xy12", "y1x2"), ("yx21", "12yx"), ("xy12", "2x1y"))
LINKS = {"x": ("col", 2), "y": ("row", 1), "1": ("row", 2), "2": ("row", 4)}


def ring_order(count):
    return list(range(0, count, 2)) + list(range(1, count, 2))[::-1]


def swap(value, axis, bit):
    size = lax.axis_size(axis)
    return lax.ppermute(value, axis, [(i, i ^ bit) for i in range(size)])


def exchange(value, links):
    rows, cols = lax.axis_size("row"), lax.axis_size("col")
    moves = []
    for r in range(rows):
        for c in range(cols):
            axis, bit = LINKS[links[c % 2]]
            to = (r ^ bit, c) if axis == "row" else (r, c ^ bit)
            moves.append((r * cols + c, to[0] * cols + to[1]))
    return lax.ppermute(value, ("row", "col"), moves)


def log2(size):
    power = size.bit_length() - 1
    assert size == 1 << power
    return power


class Sizes:
    def __init__(self, rows, cols, tiles, side):
        self.rows, self.cols, self.tiles, self.side = rows, cols, tiles, side
        self.slab = cols * tiles
        self.pairs = 2 * self.slab
        self.width = OWN * rows // cols
        self.per = OWN * self.width
        self.his = rows // 8
        self.blocks, self.tall = 4 * cols, self.per * side
        third = self.tall // 16 // 3 * 16
        self.splits = (0, third, 2 * third, self.tall)
        self.buckets = 2 * self.his
        self.slots = self.pairs + self.buckets * UNROLL
        self.half = rows // 2
        self.early = rows - 1
        self.near = 2 * self.early * tiles
        self.fields, shift = [], 0
        for size in (self.pairs, 2 * rows * tiles, self.blocks * self.per):
            self.fields.append((shift, size - 1))
            shift += log2(size)
        assert shift <= 31


def field(s, entry, k):
    shift, mask = s.fields[k]
    return (entry >> shift) & mask


def plan_kernel(s, cols_ref, aggs_ref, plan_ref, starts_ref, info, counts):
    row = lax.axis_index("row")
    col = lax.axis_index("col")

    def ring_place(index):
        return jnp.where((index & 1) == 0, index >> 1, s.rows - 1 - (index >> 1))

    here = ring_place(row)
    for b in range(s.buckets):
        counts[b] = 0

    def blank(k, carry):
        plan_ref[k] = -1
        return carry

    lax.fori_loop(0, s.slots + 1, blank, 0, unroll=8)

    def sort(i, carry):
        tile = i & (s.slab - 1)
        side = i >> log2(s.slab)
        other = cols_ref[i]
        other_row = other >> log2(s.slab)
        i_agg = aggs_ref[tile]
        j_agg = aggs_ref[((other_row ^ row) << log2(s.slab)) + (other & (s.slab - 1))]
        rel_col = (j_agg >> log2(s.width)) ^ col
        rel_row = (i_agg >> log2(OWN)) ^ row
        turn = ring_place(other_row) - here
        away = jnp.where(((col ^ side) & 1) == 0, turn, -turn) & (s.rows - 1)
        late = jnp.where(away == s.half, 1, 0)
        order = away - jnp.where(away > s.half, 1, 0) + side * s.early
        piece = jnp.where(late == 1, side, order)
        panel_at = (piece << log2(s.tiles)) + (other & (s.tiles - 1))
        cell = (rel_row & 7) * (s.cols // 2) + (rel_col >> 1)
        cell = (cell << log2(OWN)) + (i_agg & (OWN - 1))
        cell = (cell << log2(s.width)) + (j_agg & (s.width - 1))
        bucket = (rel_row >> 3) * 2 + late
        mine = (rel_col & 1) == 0
        rank = counts[bucket]
        counts[bucket] = rank + jnp.where(mine, 1, 0)
        info[i * 2] = jnp.where(mine, rank * s.buckets + bucket, -1)
        entry = i
        for k, value in enumerate((panel_at, cell)):
            entry = entry + (value << s.fields[k + 1][0])
        info[i * 2 + 1] = entry
        return carry

    lax.fori_loop(0, s.pairs, sort, 0, unroll=4)

    start = jnp.int32(0)
    for b in range(s.buckets):
        starts_ref[b] = start
        start = start + ((counts[b] + UNROLL - 1) & ~(UNROLL - 1))
    starts_ref[s.buckets] = start

    def place(i, carry):
        key = info[i * 2]
        slot = starts_ref[key & (s.buckets - 1)] + (key >> log2(s.buckets))
        plan_ref[jnp.where(key >= 0, slot, s.slots)] = info[i * 2 + 1]
        return carry

    lax.fori_loop(0, s.pairs, place, 0, unroll=4)


def room(*shapes):
    total = sum(math.prod(shape) * jnp.dtype(dtype).itemsize for shape, dtype in shapes)
    return total + (2 << 20)


def make_plan(s, cols, aggs):
    smem = pl.BlockSpec(memory_space=pltpu.SMEM)
    return pl.pallas_call(
        functools.partial(plan_kernel, s),
        in_specs=[smem, smem],
        out_specs=[smem, smem],
        out_shape=[
            jax.ShapeDtypeStruct((s.slots + 1,), jnp.int32),
            jax.ShapeDtypeStruct((s.buckets + 1,), jnp.int32),
        ],
        scratch_shapes=[
            pltpu.SMEM((s.pairs * 2,), jnp.int32),
            pltpu.SMEM((s.buckets,), jnp.int32),
        ],
        compiler_params=pltpu.CompilerParams(vmem_limit_bytes=room()),
        cost_estimate=pl.CostEstimate(flops=1 << 20, bytes_accessed=16 << 20, transcendentals=0),
    )(cols, aggs)


def turn_kernel(s, *refs):
    rows_ref, rows_buf, sems = refs[-3:]
    copies = [
        pltpu.make_async_copy(refs[k], rows_buf.at[pl.ds(k * s.tiles, s.tiles)], sems.at[k])
        for k in range(s.cols)
    ]
    for copy in copies:
        copy.start()
    for copy in copies:
        copy.wait()
    col = lax.axis_index("col")

    def turn(k, carry):
        part = k >> log2(s.tiles)
        rel = (part & (s.cols // 2 - 1)) * 2 + (part >> log2(s.cols // 2))
        rows_ref[((rel ^ col) << log2(s.tiles)) + (k & (s.tiles - 1))] = rows_buf[k].T
        return carry

    lax.fori_loop(0, s.slab, turn, 0, unroll=4)


def turn_rows(s, rows):
    own = pltpu.with_memory_space_constraint(rows[0], pltpu.HBM)
    shape = ((s.slab, s.side, s.side), jnp.bfloat16)
    return pl.pallas_call(
        functools.partial(turn_kernel, s),
        in_specs=[pl.BlockSpec(memory_space=pltpu.HBM)]
        + [pl.BlockSpec(memory_space=pl.ANY)] * (s.cols - 1),
        out_specs=pl.BlockSpec(memory_space=pltpu.VMEM),
        out_shape=jax.ShapeDtypeStruct(*shape),
        scratch_shapes=[pltpu.VMEM(*shape), pltpu.SemaphoreType.DMA((s.cols,))],
        compiler_params=pltpu.CompilerParams(vmem_limit_bytes=room(shape, shape)),
        cost_estimate=pl.CostEstimate(flops=0, bytes_accessed=0, transcendentals=0),
    )(own, *rows[1:])


def product_kernel(s, plan_ref, starts_ref, *refs):
    slots_ref, a_buf, panel, sems = refs[-4:]
    copies = []
    for k in range(2):
        copies.append((refs[k], a_buf.at[pl.ds(k * s.slab, s.slab)]))
    for k in range(2 * s.early):
        copies.append((refs[2 + k], panel.at[pl.ds(k * s.tiles, s.tiles)]))
    copies = [pltpu.make_async_copy(src, dst, sems.at[k]) for k, (src, dst) in enumerate(copies)]
    for copy in copies:
        copy.start()
    for copy in copies:
        copy.wait()

    for hi in range(s.his):
        begin = starts_ref[2 * hi] // UNROLL
        middle = starts_ref[2 * hi + 1] // UNROLL
        end = starts_ref[2 * hi + 2] // UNROLL

        def near(group, carry):
            for u in range(UNROLL):
                n = group * UNROLL + u
                entry = jnp.maximum(plan_ref[n], 0)
                slots_ref[n] = jnp.dot(
                    a_buf[field(s, entry, 0)],
                    panel[field(s, entry, 1)],
                    preferred_element_type=jnp.float32,
                ).astype(jnp.bfloat16)
            return carry

        def far(group, carry):
            for u in range(UNROLL):
                n = group * UNROLL + u
                slots_ref[n] = a_buf[field(s, jnp.maximum(plan_ref[n], 0), 0)]
            return carry

        lax.fori_loop(begin, middle, near, 0)
        lax.fori_loop(middle, end, far, 0)


def make_products(s, plan, starts, a_own, a_other, near):
    smem = pl.BlockSpec(memory_space=pltpu.SMEM)
    hbm = pl.BlockSpec(memory_space=pltpu.HBM)
    anywhere = pl.BlockSpec(memory_space=pl.ANY)
    shapes = [
        ((count, s.side, s.side), jnp.bfloat16) for count in (s.slots, s.pairs, s.near)
    ]
    a_own, own = (pltpu.with_memory_space_constraint(x, pltpu.HBM) for x in (a_own, near[0]))
    operands = [a_own, a_other, own, *near[1:]]
    return pl.pallas_call(
        functools.partial(product_kernel, s),
        in_specs=[smem, smem, hbm, anywhere, hbm] + [anywhere] * (len(operands) - 3),
        out_specs=pl.BlockSpec(memory_space=pltpu.VMEM),
        out_shape=jax.ShapeDtypeStruct(*shapes[0]),
        scratch_shapes=[pltpu.VMEM(*shape) for shape in shapes[1:]]
        + [pltpu.SemaphoreType.DMA((len(operands),))],
        compiler_params=pltpu.CompilerParams(vmem_limit_bytes=room(*shapes)),
        cost_estimate=pl.CostEstimate(
            flops=s.pairs * s.side**3, bytes_accessed=1 << 20, transcendentals=0
        ),
    )(plan, starts, *operands)


def sum_kernel(
    s, plan_ref, starts_ref, slots_ref, rows_ref, far0, far1,
    send0, keep0, send1, keep1, send2, keep2, total, far_buf, sems,
):
    hi = pl.program_id(0)
    copies = [
        pltpu.make_async_copy(ref, far_buf.at[pl.ds(k * s.tiles, s.tiles)], sems.at[k])
        for k, ref in enumerate((far0, far1))
    ]

    @pl.when(hi == 0)
    def _():
        for copy in copies:
            copy.start()

    def clear(k, carry):
        total[k] = jnp.zeros(total.shape[1:], jnp.float32)
        return carry

    lax.fori_loop(0, s.blocks, clear, 0)

    def add(n, product):
        entry = plan_ref[n]
        known = jnp.maximum(entry, 0)
        term = jnp.dot(
            rows_ref[known & (s.slab - 1)], product, preferred_element_type=jnp.float32
        )
        cell = field(s, known, 2)
        at = pl.ds(pl.multiple_of((cell & (s.per - 1)) * s.side, s.side), s.side)
        total[cell >> log2(s.per), at, :] += jnp.where(entry >= 0, term, 0.0)

    def near(group, carry):
        for u in range(UNROLL):
            n = group * UNROLL + u
            add(n, slots_ref[n])
        return carry

    def far(group, carry):
        for u in range(UNROLL):
            n = group * UNROLL + u
            piece = far_buf[field(s, jnp.maximum(plan_ref[n], 0), 1)]
            product = jnp.dot(slots_ref[n], piece, preferred_element_type=jnp.float32)
            add(n, product.astype(jnp.bfloat16))
        return carry

    begin = starts_ref[2 * hi] // UNROLL
    middle = starts_ref[2 * hi + 1] // UNROLL
    end = starts_ref[2 * hi + 2] // UNROLL
    lax.fori_loop(begin, middle, near, 0)

    @pl.when(hi == 0)
    def _():
        for copy in copies:
            copy.wait()

    lax.fori_loop(middle, end, far, 0)

    half = s.cols // 2
    weight = {"x": 1, "y": half, "1": 2 * half, "2": 4 * half}
    core = lax.axis_index("col") & 1
    outs = ((send0, keep0), (send1, keep1), (send2, keep2))
    for k, (send, keep) in enumerate(outs):
        for bits in itertools.product(range(2), repeat=4):
            base = [
                sum(weight[link] * bit for link, bit in zip(order, bits)) for order in ORDERS[k]
            ]
            base = jnp.where(core == 0, *base)
            for x in range(half // 2):
                part = total[base + 2 * x, s.splits[k]:s.splits[k + 1], :]
                if bits[0]:
                    send[(*bits[1:], 0, x)] = part.astype(jnp.bfloat16)
                else:
                    keep[(*bits[1:], 0, x)] = part


def make_sums(s, plan, starts, slots, rows_t, far):
    smem = pl.BlockSpec(memory_space=pltpu.SMEM)
    vmem = pl.BlockSpec(memory_space=pltpu.VMEM)
    anywhere = pl.BlockSpec(memory_space=pl.ANY)
    shapes = [
        ((s.slots + s.slab + 2 * s.tiles, s.side, s.side), jnp.bfloat16),
        ((s.blocks, s.tall, s.side), jnp.float32),
    ]
    out_shape, out_specs = [], []
    for k in range(len(ORDERS)):
        last = (s.cols // 4, s.splits[k + 1] - s.splits[k], s.side)
        for dtype in (jnp.bfloat16, jnp.float32):
            out_shape.append(jax.ShapeDtypeStruct((2, 2, 2, s.his) + last, dtype))
            out_specs.append(
                pl.BlockSpec((2, 2, 2, 1) + last, lambda h: (0, 0, 0, h, 0, 0, 0))
            )
            shapes.append(((2 if s.his > 1 else 1, 8) + last, dtype))
    return pl.pallas_call(
        functools.partial(sum_kernel, s),
        grid=(s.his,),
        in_specs=[smem, smem, vmem, vmem, anywhere, anywhere],
        out_specs=out_specs,
        out_shape=out_shape,
        scratch_shapes=[
            pltpu.VMEM((s.blocks, s.tall, s.side), jnp.float32),
            pltpu.VMEM((2 * s.tiles, s.side, s.side), jnp.bfloat16),
            pltpu.SemaphoreType.DMA((2,)),
        ],
        compiler_params=pltpu.CompilerParams(vmem_limit_bytes=room(*shapes)),
        cost_estimate=pl.CostEstimate(
            flops=s.pairs * s.side**3, bytes_accessed=16 << 20, transcendentals=0
        ),
    )(plan, starts, slots, rows_t, *far)


def shards(a_blocks, p_tiles, owner, agg_local, a_cols):
    s = Sizes(
        lax.axis_size("row"), lax.axis_size("col"), p_tiles.shape[0], p_tiles.shape[1]
    )
    order = ring_order(s.rows)
    barrier = lax.optimization_barrier

    def ring(value, stream):
        moves = []
        for k in range(s.rows):
            for c in range(s.cols):
                step = 1 if (stream + c) % 2 == 0 else -1
                to = order[(k + step) % s.rows]
                moves.append((order[k] * s.cols + c, to * s.cols + c))
        return lax.ppermute(value, ("row", "col"), moves)

    first = ring(p_tiles, 0)
    cols = a_cols[:, 0]
    cols_other = swap(cols, "col", 1)
    cols_other, mine = barrier((cols_other, p_tiles))
    second = ring(mine, 1)
    a_other, p_other = swap(a_blocks[:, 0], "col", 1), swap(p_tiles, "col", 1)

    aggs = owner[:, 0] * OWN + agg_local
    came, aggs, a_other, p_other = barrier((first, aggs, a_other, p_other))
    first = ring(first, 0)
    aggs = [aggs] + [swap(aggs, "row", mask) for mask in (1, 2, 3)]
    own_near, other_near = {0: p_tiles, s.rows - 1: came, 1: second}, {0: p_other}
    second = ring(second, 1)
    aggs, mine = barrier((jnp.concatenate(aggs, 0), p_tiles))
    bit = 4
    while bit < s.rows:
        aggs = jnp.concatenate([aggs, swap(aggs, "row", bit)], 0)
        bit *= 2
    rows = [mine]
    bit = 2
    while bit < s.cols:
        rows += [swap(piece, "col", bit) for piece in rows]
        bit *= 2
    plan, starts = make_plan(s, jnp.concatenate([cols, cols_other], 0), aggs)

    held = [1, s.rows - 1]
    for step in range(2, s.half - 1):
        came, *rest = barrier((second, *(own_near[away] for away in held), *rows[1:]))
        for away, piece in zip(held, rest):
            other_near[away] = swap(piece, "col", 1)
        if step == 2:
            rows += [p_other] + [swap(piece, "col", 1) for piece in rest[len(held):]]
        own_near[s.rows - step], own_near[step] = first, came
        first, second = ring(first, 0), ring(second, 1)
        held = [step, s.rows - step]

    others = sorted(set(other_near) - {0})
    rows_t = turn_rows(s, rows)
    tie = (first, second, plan, starts, rows_t)
    tie += (*(own_near[away] for away in held), *(other_near[away] for away in others))
    first, second, plan, starts, rows_t, *rest = barrier(tie)
    for away, piece in zip(others, rest[len(held):]):
        other_near[away] = piece
    far = ring(first, 0)
    own_near[s.half + 1], own_near[s.half - 1] = first, second
    for away, piece in zip(held, rest):
        other_near[away] = swap(piece, "col", 1)
    for away in (s.half + 1, s.half - 1):
        other_near[away] = swap(own_near[away], "col", 1)
    near = [own_near[k] for k in sorted(own_near)]
    near += [other_near[k] for k in sorted(other_near)]
    slots = make_products(s, plan, starts, a_blocks[:, 0], a_other, near)
    far, slots = barrier((far, slots))
    far_other = swap(far, "col", 1)
    parts = make_sums(s, plan, starts, slots, rows_t, [far, far_other])

    sends, keeps = list(parts[0::2]), list(parts[1::2])
    groups = range(len(ORDERS))
    moving = [exchange(sends[k], [order[0] for order in ORDERS[k]]) for k in groups]
    for step in range(1, 5):
        for k in groups:
            got = moving[k]
            if step < 4:
                send = (keeps[k][1] + got[1].astype(jnp.float32)).astype(jnp.bfloat16)
                moving[k] = exchange(send, [order[step] for order in ORDERS[k]])
                keeps[k] = keeps[k][0] + got[0].astype(jnp.float32)
            else:
                keeps[k] = keeps[k] + got.astype(jnp.float32)
    total = jnp.concatenate(keeps, -2)
    tail = [("row", 1 << k) for k in range(3, log2(s.rows))][::-1]
    tail += [("col", 1 << k) for k in range(2, log2(s.cols))][::-1]
    total = total.reshape((2,) * len(tail) + total.shape[-2:])
    for axis in tail:
        got = swap(total[1].astype(jnp.bfloat16), *axis)
        total = total[0] + got.astype(jnp.float32)
    return total.reshape(OWN, s.width, s.side, s.side)


def solution(mesh):
    in_specs = (
        P("row", "col", None, None),
        P(("row", "col"), None, None),
        P("row", None),
        P("row"),
        P("row", "col"),
    )
    out_specs = P("row", "col", None, None)
    return jax.shard_map(shards, mesh=mesh, in_specs=in_specs, out_specs=out_specs, check_vma=False)
```

```python
import functools
import itertools
import math

import jax
import jax.numpy as jnp
from jax import lax
from jax.experimental import pallas as pl
from jax.experimental.pallas import tpu as pltpu
from jax.sharding import PartitionSpec as P

OWN = 2
UNROLL = 8
ORDERS = (("xy12", "y1x2"), ("yx21", "12yx"), ("xy12", "2x1y"))
LINKS = {"x": ("col", 2), "y": ("row", 1), "1": ("row", 2), "2": ("row", 4)}


def ring_order(count):
    return list(range(0, count, 2)) + list(range(1, count, 2))[::-1]


def swap(value, axis, bit):
    size = lax.axis_size(axis)
    return lax.ppermute(value, axis, [(i, i ^ bit) for i in range(size)])


def exchange(value, links):
    rows, cols = lax.axis_size("row"), lax.axis_size("col")
    moves = []
    for r in range(rows):
        for c in range(cols):
            axis, bit = LINKS[links[c % 2]]
            to = (r ^ bit, c) if axis == "row" else (r, c ^ bit)
            moves.append((r * cols + c, to[0] * cols + to[1]))
    return lax.ppermute(value, ("row", "col"), moves)


def log2(size):
    power = size.bit_length() - 1
    assert size == 1 << power
    return power


class Sizes:
    def __init__(self, rows, cols, tiles, side):
        self.rows, self.cols, self.tiles, self.side = rows, cols, tiles, side
        self.slab = cols * tiles
        self.pairs = 2 * self.slab
        self.width = OWN * rows // cols
        self.per = OWN * self.width
        self.his = rows // 8
        self.blocks, self.tall = 4 * cols, self.per * side
        third = self.tall // 16 // 3 * 16
        self.splits = (0, third, 2 * third, self.tall)
        self.buckets = 2 * self.his
        self.slots = self.pairs + self.buckets * UNROLL
        self.half = rows // 2
        self.early = rows - 1
        self.near = 2 * self.early * tiles
        self.fields, shift = [], 0
        for size in (self.pairs, 2 * rows * tiles, self.blocks * self.per):
            self.fields.append((shift, size - 1))
            shift += log2(size)
        assert shift <= 31


def field(s, entry, k):
    shift, mask = s.fields[k]
    return (entry >> shift) & mask


def plan_kernel(s, cols_ref, aggs_ref, plan_ref, starts_ref, info, counts):
    row = lax.axis_index("row")
    col = lax.axis_index("col")

    def ring_place(index):
        return jnp.where((index & 1) == 0, index >> 1, s.rows - 1 - (index >> 1))

    here = ring_place(row)
    for b in range(s.buckets):
        counts[b] = 0

    def blank(k, carry):
        plan_ref[k] = -1
        return carry

    lax.fori_loop(0, s.slots + 1, blank, 0, unroll=8)

    def sort(i, carry):
        tile = i & (s.slab - 1)
        side = i >> log2(s.slab)
        other = cols_ref[i]
        other_row = other >> log2(s.slab)
        i_agg = aggs_ref[tile]
        j_agg = aggs_ref[((other_row ^ row) << log2(s.slab)) + (other & (s.slab - 1))]
        rel_col = (j_agg >> log2(s.width)) ^ col
        rel_row = (i_agg >> log2(OWN)) ^ row
        turn = ring_place(other_row) - here
        away = jnp.where(((col ^ side) & 1) == 0, turn, -turn) & (s.rows - 1)
        late = jnp.where(away == s.half, 1, 0)
        order = away - jnp.where(away > s.half, 1, 0) + side * s.early
        piece = jnp.where(late == 1, side, order)
        panel_at = (piece << log2(s.tiles)) + (other & (s.tiles - 1))
        cell = (rel_row & 7) * (s.cols // 2) + (rel_col >> 1)
        cell = (cell << log2(OWN)) + (i_agg & (OWN - 1))
        cell = (cell << log2(s.width)) + (j_agg & (s.width - 1))
        bucket = (rel_row >> 3) * 2 + late
        mine = (rel_col & 1) == 0
        rank = counts[bucket]
        counts[bucket] = rank + jnp.where(mine, 1, 0)
        info[i * 2] = jnp.where(mine, rank * s.buckets + bucket, -1)
        entry = i
        for k, value in enumerate((panel_at, cell)):
            entry = entry + (value << s.fields[k + 1][0])
        info[i * 2 + 1] = entry
        return carry

    lax.fori_loop(0, s.pairs, sort, 0, unroll=4)

    start = jnp.int32(0)
    for b in range(s.buckets):
        starts_ref[b] = start
        start = start + ((counts[b] + UNROLL - 1) & ~(UNROLL - 1))
    starts_ref[s.buckets] = start

    def place(i, carry):
        key = info[i * 2]
        slot = starts_ref[key & (s.buckets - 1)] + (key >> log2(s.buckets))
        plan_ref[jnp.where(key >= 0, slot, s.slots)] = info[i * 2 + 1]
        return carry

    lax.fori_loop(0, s.pairs, place, 0, unroll=4)


def room(*shapes):
    total = sum(math.prod(shape) * jnp.dtype(dtype).itemsize for shape, dtype in shapes)
    return total + (2 << 20)


def make_plan(s, cols, aggs):
    smem = pl.BlockSpec(memory_space=pltpu.SMEM)
    return pl.pallas_call(
        functools.partial(plan_kernel, s),
        in_specs=[smem, smem],
        out_specs=[smem, smem],
        out_shape=[
            jax.ShapeDtypeStruct((s.slots + 1,), jnp.int32),
            jax.ShapeDtypeStruct((s.buckets + 1,), jnp.int32),
        ],
        scratch_shapes=[
            pltpu.SMEM((s.pairs * 2,), jnp.int32),
            pltpu.SMEM((s.buckets,), jnp.int32),
        ],
        compiler_params=pltpu.CompilerParams(vmem_limit_bytes=room()),
        cost_estimate=pl.CostEstimate(flops=1 << 20, bytes_accessed=16 << 20, transcendentals=0),
    )(cols, aggs)


def turn_kernel(s, *refs):
    rows_ref, rows_buf, sems = refs[-3:]
    copies = [
        pltpu.make_async_copy(refs[k], rows_buf.at[pl.ds(k * s.tiles, s.tiles)], sems.at[k])
        for k in range(s.cols)
    ]
    for copy in copies:
        copy.start()
    for copy in copies:
        copy.wait()
    col = lax.axis_index("col")

    def turn(k, carry):
        part = k >> log2(s.tiles)
        rel = (part & (s.cols // 2 - 1)) * 2 + (part >> log2(s.cols // 2))
        rows_ref[((rel ^ col) << log2(s.tiles)) + (k & (s.tiles - 1))] = rows_buf[k].T
        return carry

    lax.fori_loop(0, s.slab, turn, 0, unroll=4)


def turn_rows(s, rows):
    own = pltpu.with_memory_space_constraint(rows[0], pltpu.HBM)
    shape = ((s.slab, s.side, s.side), jnp.bfloat16)
    return pl.pallas_call(
        functools.partial(turn_kernel, s),
        in_specs=[pl.BlockSpec(memory_space=pltpu.HBM)]
        + [pl.BlockSpec(memory_space=pl.ANY)] * (s.cols - 1),
        out_specs=pl.BlockSpec(memory_space=pltpu.VMEM),
        out_shape=jax.ShapeDtypeStruct(*shape),
        scratch_shapes=[pltpu.VMEM(*shape), pltpu.SemaphoreType.DMA((s.cols,))],
        compiler_params=pltpu.CompilerParams(vmem_limit_bytes=room(shape, shape)),
        cost_estimate=pl.CostEstimate(flops=0, bytes_accessed=0, transcendentals=0),
    )(own, *rows[1:])


def product_kernel(s, plan_ref, starts_ref, *refs):
    slots_ref, a_buf, panel, sems = refs[-4:]
    copies = []
    for k in range(2):
        copies.append((refs[k], a_buf.at[pl.ds(k * s.slab, s.slab)]))
    for k in range(2 * s.early):
        copies.append((refs[2 + k], panel.at[pl.ds(k * s.tiles, s.tiles)]))
    copies = [pltpu.make_async_copy(src, dst, sems.at[k]) for k, (src, dst) in enumerate(copies)]
    for copy in copies:
        copy.start()
    for copy in copies:
        copy.wait()

    for hi in range(s.his):
        begin = starts_ref[2 * hi] // UNROLL
        middle = starts_ref[2 * hi + 1] // UNROLL
        end = starts_ref[2 * hi + 2] // UNROLL

        def near(group, carry):
            for u in range(UNROLL):
                n = group * UNROLL + u
                entry = jnp.maximum(plan_ref[n], 0)
                slots_ref[n] = jnp.dot(
                    a_buf[field(s, entry, 0)],
                    panel[field(s, entry, 1)],
                    preferred_element_type=jnp.float32,
                ).astype(jnp.bfloat16)
            return carry

        def far(group, carry):
            for u in range(UNROLL):
                n = group * UNROLL + u
                slots_ref[n] = a_buf[field(s, jnp.maximum(plan_ref[n], 0), 0)]
            return carry

        lax.fori_loop(begin, middle, near, 0)
        lax.fori_loop(middle, end, far, 0)


def make_products(s, plan, starts, a_own, a_other, near):
    smem = pl.BlockSpec(memory_space=pltpu.SMEM)
    hbm = pl.BlockSpec(memory_space=pltpu.HBM)
    anywhere = pl.BlockSpec(memory_space=pl.ANY)
    shapes = [
        ((count, s.side, s.side), jnp.bfloat16) for count in (s.slots, s.pairs, s.near)
    ]
    a_own, own = (pltpu.with_memory_space_constraint(x, pltpu.HBM) for x in (a_own, near[0]))
    operands = [a_own, a_other, own, *near[1:]]
    return pl.pallas_call(
        functools.partial(product_kernel, s),
        in_specs=[smem, smem, hbm, anywhere, hbm] + [anywhere] * (len(operands) - 3),
        out_specs=pl.BlockSpec(memory_space=pltpu.VMEM),
        out_shape=jax.ShapeDtypeStruct(*shapes[0]),
        scratch_shapes=[pltpu.VMEM(*shape) for shape in shapes[1:]]
        + [pltpu.SemaphoreType.DMA((len(operands),))],
        compiler_params=pltpu.CompilerParams(vmem_limit_bytes=room(*shapes)),
        cost_estimate=pl.CostEstimate(
            flops=s.pairs * s.side**3, bytes_accessed=1 << 20, transcendentals=0
        ),
    )(plan, starts, *operands)


def add_term(s, rows_ref, total, entry, product):
    known = jnp.maximum(entry, 0)
    term = jnp.dot(rows_ref[known & (s.slab - 1)], product, preferred_element_type=jnp.float32)
    cell = field(s, known, 2)
    at = pl.ds(pl.multiple_of((cell & (s.per - 1)) * s.side, s.side), s.side)
    total[cell >> log2(s.per), at, :] += jnp.where(entry >= 0, term, 0.0)


def sum_near(s, hi, plan_ref, starts_ref, slots_ref, rows_ref, total):
    def clear(k, carry):
        total[k] = jnp.zeros(total.shape[1:], jnp.float32)
        return carry

    def near(group, carry):
        for u in range(UNROLL):
            n = group * UNROLL + u
            add_term(s, rows_ref, total, plan_ref[n], slots_ref[n])
        return carry

    lax.fori_loop(0, s.blocks, clear, 0)
    lax.fori_loop(starts_ref[2 * hi] // UNROLL, starts_ref[2 * hi + 1] // UNROLL, near, 0)


def sum_kernel(s, plan_ref, starts_ref, slots_ref, rows_ref, far0, far1, *refs):
    if s.his == 1:
        hi, (total, *outs), (far_buf, sems) = 0, refs[1:-2], refs[-2:]
    else:
        hi, outs, (total, far_buf, sems) = pl.program_id(0), refs[:-3], refs[-3:]
    copies = [
        pltpu.make_async_copy(ref, far_buf.at[pl.ds(k * s.tiles, s.tiles)], sems.at[k])
        for k, ref in enumerate((far0, far1))
    ]

    @pl.when(hi == 0)
    def _():
        for copy in copies:
            copy.start()

    if s.his > 1:
        sum_near(s, hi, plan_ref, starts_ref, slots_ref, rows_ref, total)

    @pl.when(hi == 0)
    def _():
        for copy in copies:
            copy.wait()

    def far(group, carry):
        for u in range(UNROLL):
            n = group * UNROLL + u
            entry = plan_ref[n]
            piece = far_buf[field(s, jnp.maximum(entry, 0), 1)]
            product = jnp.dot(slots_ref[n], piece, preferred_element_type=jnp.float32)
            add_term(s, rows_ref, total, entry, product.astype(jnp.bfloat16))
        return carry

    middle = starts_ref[2 * hi + 1] // UNROLL
    lax.fori_loop(middle, starts_ref[2 * hi + 2] // UNROLL, far, 0)

    half = s.cols // 2
    weight = {"x": 1, "y": half, "1": 2 * half, "2": 4 * half}
    core = lax.axis_index("col") & 1
    for k, (send, keep) in enumerate(zip(outs[0::2], outs[1::2])):
        for bits in itertools.product(range(2), repeat=4):
            base = [
                sum(weight[link] * bit for link, bit in zip(order, bits)) for order in ORDERS[k]
            ]
            base = jnp.where(core == 0, *base)
            for x in range(half // 2):
                part = total[base + 2 * x, s.splits[k]:s.splits[k + 1], :]
                if bits[0]:
                    send[(*bits[1:], 0, x)] = part.astype(jnp.bfloat16)
                else:
                    keep[(*bits[1:], 0, x)] = part


def total_shape(s):
    return (s.blocks, s.tall, s.side), jnp.float32


def make_near_sums(s, plan, starts, slots, rows_t):
    smem = pl.BlockSpec(memory_space=pltpu.SMEM)
    vmem = pl.BlockSpec(memory_space=pltpu.VMEM)
    return pl.pallas_call(
        functools.partial(sum_near, s, 0),
        in_specs=[smem, smem, vmem, vmem],
        out_specs=vmem,
        out_shape=jax.ShapeDtypeStruct(*total_shape(s)),
        compiler_params=pltpu.CompilerParams(vmem_limit_bytes=room(total_shape(s))),
        cost_estimate=pl.CostEstimate(
            flops=s.pairs * s.side**3, bytes_accessed=1 << 20, transcendentals=0
        ),
    )(plan, starts, slots, rows_t)


def make_sums(s, plan, starts, slots, rows_t, far, total):
    smem = pl.BlockSpec(memory_space=pltpu.SMEM)
    vmem = pl.BlockSpec(memory_space=pltpu.VMEM)
    anywhere = pl.BlockSpec(memory_space=pl.ANY)
    shapes = [
        ((s.slots + s.slab + 2 * s.tiles, s.side, s.side), jnp.bfloat16),
        total_shape(s),
    ]
    in_specs = [smem, smem, vmem, vmem, anywhere, anywhere]
    out_shape, out_specs = [], []
    for k in range(len(ORDERS)):
        last = (s.cols // 4, s.splits[k + 1] - s.splits[k], s.side)
        for dtype in (jnp.bfloat16, jnp.float32):
            out_shape.append(jax.ShapeDtypeStruct((2, 2, 2, s.his) + last, dtype))
            out_specs.append(
                pl.BlockSpec((2, 2, 2, 1) + last, lambda h: (0, 0, 0, h, 0, 0, 0))
            )
            shapes.append(((2 if s.his > 1 else 1, 8) + last, dtype))
    scratch = [
        pltpu.VMEM((2 * s.tiles, s.side, s.side), jnp.bfloat16),
        pltpu.SemaphoreType.DMA((2,)),
    ]
    operands = [plan, starts, slots, rows_t, *far]
    aliases = {}
    if s.his == 1:
        aliases = {len(operands): 0}
        operands.append(total)
        in_specs.append(vmem)
        out_shape.insert(0, jax.ShapeDtypeStruct(*total_shape(s)))
        out_specs = [vmem] * len(out_shape)
    else:
        scratch.insert(0, pltpu.VMEM(*total_shape(s)))
    parts = pl.pallas_call(
        functools.partial(sum_kernel, s),
        grid=() if s.his == 1 else (s.his,),
        in_specs=in_specs,
        out_specs=out_specs,
        out_shape=out_shape,
        scratch_shapes=scratch,
        input_output_aliases=aliases,
        compiler_params=pltpu.CompilerParams(vmem_limit_bytes=room(*shapes)),
        cost_estimate=pl.CostEstimate(
            flops=s.pairs * s.side**3, bytes_accessed=16 << 20, transcendentals=0
        ),
    )(*operands)
    return parts[len(aliases):]


def shards(a_blocks, p_tiles, owner, agg_local, a_cols):
    s = Sizes(
        lax.axis_size("row"), lax.axis_size("col"), p_tiles.shape[0], p_tiles.shape[1]
    )
    order = ring_order(s.rows)
    barrier = lax.optimization_barrier

    def ring(value, stream):
        moves = []
        for k in range(s.rows):
            for c in range(s.cols):
                step = 1 if (stream + c) % 2 == 0 else -1
                to = order[(k + step) % s.rows]
                moves.append((order[k] * s.cols + c, to * s.cols + c))
        return lax.ppermute(value, ("row", "col"), moves)

    first = ring(p_tiles, 0)
    cols = a_cols[:, 0]
    cols_other = swap(cols, "col", 1)
    cols_other, mine = barrier((cols_other, p_tiles))
    second = ring(mine, 1)
    a_other, p_other = swap(a_blocks[:, 0], "col", 1), swap(p_tiles, "col", 1)

    aggs = owner[:, 0] * OWN + agg_local
    came, aggs, a_other, p_other = barrier((first, aggs, a_other, p_other))
    first = ring(first, 0)
    aggs = [aggs] + [swap(aggs, "row", mask) for mask in (1, 2, 3)]
    own_near, other_near = {0: p_tiles, s.rows - 1: came, 1: second}, {0: p_other}
    second = ring(second, 1)
    aggs, mine = barrier((jnp.concatenate(aggs, 0), p_tiles))
    bit = 4
    while bit < s.rows:
        aggs = jnp.concatenate([aggs, swap(aggs, "row", bit)], 0)
        bit *= 2
    rows = [mine]
    bit = 2
    while bit < s.cols:
        rows += [swap(piece, "col", bit) for piece in rows]
        bit *= 2
    plan, starts = make_plan(s, jnp.concatenate([cols, cols_other], 0), aggs)

    held = [1, s.rows - 1]
    for step in range(2, s.half - 1):
        came, *rest = barrier((second, *(own_near[away] for away in held), *rows[1:]))
        for away, piece in zip(held, rest):
            other_near[away] = swap(piece, "col", 1)
        if step == 2:
            rows += [p_other] + [swap(piece, "col", 1) for piece in rest[len(held):]]
        own_near[s.rows - step], own_near[step] = first, came
        first, second = ring(first, 0), ring(second, 1)
        held = [step, s.rows - step]

    others = sorted(set(other_near) - {0})
    rows_t = turn_rows(s, rows)
    tie = (first, second, plan, starts, rows_t)
    tie += (*(own_near[away] for away in held), *(other_near[away] for away in others))
    first, second, plan, starts, rows_t, *rest = barrier(tie)
    for away, piece in zip(others, rest[len(held):]):
        other_near[away] = piece
    far = ring(first, 0)
    own_near[s.half + 1], own_near[s.half - 1] = first, second
    for away, piece in zip(held, rest):
        other_near[away] = swap(piece, "col", 1)
    for away in (s.half + 1, s.half - 1):
        other_near[away] = swap(own_near[away], "col", 1)
    near = [own_near[k] for k in sorted(own_near)]
    near += [other_near[k] for k in sorted(other_near)]
    slots = make_products(s, plan, starts, a_blocks[:, 0], a_other, near)
    total = None
    if s.his == 1:
        total = make_near_sums(s, plan, starts, slots, rows_t)
        far, total = barrier((far, total))
    else:
        far, slots = barrier((far, slots))
    far_other = swap(far, "col", 1)
    parts = make_sums(s, plan, starts, slots, rows_t, [far, far_other], total)

    sends, keeps = list(parts[0::2]), list(parts[1::2])
    groups = range(len(ORDERS))
    moving = [exchange(sends[k], [order[0] for order in ORDERS[k]]) for k in groups]
    for step in range(1, 5):
        for k in groups:
            got = moving[k]
            if step < 4:
                send = (keeps[k][1] + got[1].astype(jnp.float32)).astype(jnp.bfloat16)
                moving[k] = exchange(send, [order[step] for order in ORDERS[k]])
                keeps[k] = keeps[k][0] + got[0].astype(jnp.float32)
            else:
                keeps[k] = keeps[k] + got.astype(jnp.float32)
    total = jnp.concatenate(keeps, -2)
    tail = [("row", 1 << k) for k in range(3, log2(s.rows))][::-1]
    tail += [("col", 1 << k) for k in range(2, log2(s.cols))][::-1]
    total = total.reshape((2,) * len(tail) + total.shape[-2:])
    for axis in tail:
        got = swap(total[1].astype(jnp.bfloat16), *axis)
        total = total[0] + got.astype(jnp.float32)
    return total.reshape(OWN, s.width, s.side, s.side)


def solution(mesh):
    in_specs = (
        P("row", "col", None, None),
        P(("row", "col"), None, None),
        P("row", None),
        P("row"),
        P("row", "col"),
    )
    out_specs = P("row", "col", None, None)
    return jax.shard_map(shards, mesh=mesh, in_specs=in_specs, out_specs=out_specs, check_vma=False)
```

```python
import functools
import itertools
import math

import jax
import jax.numpy as jnp
from jax import lax
from jax.experimental import pallas as pl
from jax.experimental.pallas import tpu as pltpu
from jax.sharding import PartitionSpec as P

OWN = 2
UNROLL = 8
ORDERS = (("xy12", "y1x2"), ("yx21", "12yx"), ("xy12", "2x1y"))
LINKS = {"x": ("col", 2), "y": ("row", 1), "1": ("row", 2), "2": ("row", 4)}


def ring_order(count):
    return list(range(0, count, 2)) + list(range(1, count, 2))[::-1]


def swap(value, axis, bit):
    size = lax.axis_size(axis)
    return lax.ppermute(value, axis, [(i, i ^ bit) for i in range(size)])


def exchange(value, links):
    rows, cols = lax.axis_size("row"), lax.axis_size("col")
    moves = []
    for r in range(rows):
        for c in range(cols):
            axis, bit = LINKS[links[c % 2]]
            to = (r ^ bit, c) if axis == "row" else (r, c ^ bit)
            moves.append((r * cols + c, to[0] * cols + to[1]))
    return lax.ppermute(value, ("row", "col"), moves)


def log2(size):
    power = size.bit_length() - 1
    assert size == 1 << power
    return power


class Sizes:
    def __init__(self, rows, cols, tiles, side):
        self.rows, self.cols, self.tiles, self.side = rows, cols, tiles, side
        self.slab = cols * tiles
        self.pairs = 2 * self.slab
        self.width = OWN * rows // cols
        self.per = OWN * self.width
        self.his = rows // 8
        self.blocks, self.tall = 4 * cols, self.per * side
        third = self.tall // 16 // 3 * 16
        self.splits = (0, third, 2 * third, self.tall)
        self.buckets = 2 * self.his
        self.slots = self.pairs + self.buckets * UNROLL
        self.half = rows // 2
        self.early = rows - 1
        self.near = 2 * self.early * tiles
        self.fields, shift = [], 0
        for size in (self.pairs, 2 * rows * tiles, self.blocks * self.per):
            self.fields.append((shift, size - 1))
            shift += log2(size)
        assert shift <= 31


def field(s, entry, k):
    shift, mask = s.fields[k]
    return (entry >> shift) & mask


def plan_kernel(
    s, cols_ref, aggs_ref, own_ref, other_ref, plan_ref, starts_ref, pair_ref, info, counts, sems
):
    copies = [
        pltpu.make_async_copy(ref, pair_ref.at[pl.ds(k * s.slab, s.slab)], sems.at[k])
        for k, ref in enumerate((own_ref, other_ref))
    ]
    for copy in copies:
        copy.start()
    row = lax.axis_index("row")
    col = lax.axis_index("col")

    def ring_place(index):
        return jnp.where((index & 1) == 0, index >> 1, s.rows - 1 - (index >> 1))

    here = ring_place(row)
    for b in range(s.buckets):
        counts[b] = 0

    def blank(k, carry):
        plan_ref[k] = -1
        return carry

    lax.fori_loop(0, s.slots + 1, blank, 0, unroll=8)

    def sort(i, carry):
        tile = i & (s.slab - 1)
        side = i >> log2(s.slab)
        other = cols_ref[i]
        other_row = other >> log2(s.slab)
        i_agg = aggs_ref[tile]
        j_agg = aggs_ref[((other_row ^ row) << log2(s.slab)) + (other & (s.slab - 1))]
        rel_col = (j_agg >> log2(s.width)) ^ col
        rel_row = (i_agg >> log2(OWN)) ^ row
        turn = ring_place(other_row) - here
        away = jnp.where(((col ^ side) & 1) == 0, turn, -turn) & (s.rows - 1)
        late = jnp.where(away == s.half, 1, 0)
        order = away - jnp.where(away > s.half, 1, 0) + side * s.early
        piece = jnp.where(late == 1, side, order)
        panel_at = (piece << log2(s.tiles)) + (other & (s.tiles - 1))
        cell = (rel_row & 7) * (s.cols // 2) + (rel_col >> 1)
        cell = (cell << log2(OWN)) + (i_agg & (OWN - 1))
        cell = (cell << log2(s.width)) + (j_agg & (s.width - 1))
        bucket = (rel_row >> 3) * 2 + late
        mine = (rel_col & 1) == 0
        rank = counts[bucket]
        counts[bucket] = rank + jnp.where(mine, 1, 0)
        info[i * 2] = jnp.where(mine, rank * s.buckets + bucket, -1)
        entry = i
        for k, value in enumerate((panel_at, cell)):
            entry = entry + (value << s.fields[k + 1][0])
        info[i * 2 + 1] = entry
        return carry

    lax.fori_loop(0, s.pairs, sort, 0, unroll=4)

    start = jnp.int32(0)
    for b in range(s.buckets):
        starts_ref[b] = start
        start = start + ((counts[b] + UNROLL - 1) & ~(UNROLL - 1))
    starts_ref[s.buckets] = start

    def place(i, carry):
        key = info[i * 2]
        slot = starts_ref[key & (s.buckets - 1)] + (key >> log2(s.buckets))
        plan_ref[jnp.where(key >= 0, slot, s.slots)] = info[i * 2 + 1]
        return carry

    lax.fori_loop(0, s.pairs, place, 0, unroll=4)
    for copy in copies:
        copy.wait()


def room(*shapes):
    total = sum(math.prod(shape) * jnp.dtype(dtype).itemsize for shape, dtype in shapes)
    return total + (2 << 20)


def make_plan(s, cols, aggs, a_own, a_other):
    smem, vmem, hbm = (
        pl.BlockSpec(memory_space=space) for space in (pltpu.SMEM, pltpu.VMEM, pltpu.HBM)
    )
    a_own = pltpu.with_memory_space_constraint(a_own, pltpu.HBM)
    pair_shape = ((s.pairs, s.side, s.side), jnp.bfloat16)
    return pl.pallas_call(
        functools.partial(plan_kernel, s),
        in_specs=[smem, smem, hbm, pl.BlockSpec(memory_space=pl.ANY)],
        out_specs=[smem, smem, vmem],
        out_shape=[
            jax.ShapeDtypeStruct((s.slots + 1,), jnp.int32),
            jax.ShapeDtypeStruct((s.buckets + 1,), jnp.int32),
            jax.ShapeDtypeStruct(*pair_shape),
        ],
        scratch_shapes=[
            pltpu.SMEM((s.pairs * 2,), jnp.int32),
            pltpu.SMEM((s.buckets,), jnp.int32),
            pltpu.SemaphoreType.DMA((2,)),
        ],
        compiler_params=pltpu.CompilerParams(vmem_limit_bytes=room(pair_shape)),
        cost_estimate=pl.CostEstimate(flops=1 << 20, bytes_accessed=16 << 20, transcendentals=0),
    )(cols, aggs, a_own, a_other)


def turn_kernel(s, *refs):
    rows_ref, rows_buf, sems = refs[-3:]
    copies = [
        pltpu.make_async_copy(refs[k], rows_buf.at[pl.ds(k * s.tiles, s.tiles)], sems.at[k])
        for k in range(s.cols)
    ]
    for copy in copies:
        copy.start()
    for copy in copies:
        copy.wait()
    col = lax.axis_index("col")

    def turn(k, carry):
        part = k >> log2(s.tiles)
        rel = (part & (s.cols // 2 - 1)) * 2 + (part >> log2(s.cols // 2))
        rows_ref[((rel ^ col) << log2(s.tiles)) + (k & (s.tiles - 1))] = rows_buf[k].T
        return carry

    lax.fori_loop(0, s.slab, turn, 0, unroll=4)


def turn_rows(s, rows):
    own = pltpu.with_memory_space_constraint(rows[0], pltpu.HBM)
    shape = ((s.slab, s.side, s.side), jnp.bfloat16)
    return pl.pallas_call(
        functools.partial(turn_kernel, s),
        in_specs=[pl.BlockSpec(memory_space=pltpu.HBM)]
        + [pl.BlockSpec(memory_space=pl.ANY)] * (s.cols - 1),
        out_specs=pl.BlockSpec(memory_space=pltpu.VMEM),
        out_shape=jax.ShapeDtypeStruct(*shape),
        scratch_shapes=[pltpu.VMEM(*shape), pltpu.SemaphoreType.DMA((s.cols,))],
        compiler_params=pltpu.CompilerParams(vmem_limit_bytes=room(shape, shape)),
        cost_estimate=pl.CostEstimate(flops=0, bytes_accessed=0, transcendentals=0),
    )(own, *rows[1:])


def product_kernel(s, plan_ref, starts_ref, a_buf, *refs):
    slots_ref, panel, sems = refs[-3:]
    copies = []
    for k in range(2 * s.early):
        copies.append((refs[k], panel.at[pl.ds(k * s.tiles, s.tiles)]))
    copies = [pltpu.make_async_copy(src, dst, sems.at[k]) for k, (src, dst) in enumerate(copies)]
    for copy in copies:
        copy.start()
    for copy in copies:
        copy.wait()

    for hi in range(s.his):
        begin = starts_ref[2 * hi] // UNROLL
        middle = starts_ref[2 * hi + 1] // UNROLL
        end = starts_ref[2 * hi + 2] // UNROLL

        def near(group, carry):
            for u in range(UNROLL):
                n = group * UNROLL + u
                entry = jnp.maximum(plan_ref[n], 0)
                slots_ref[n] = jnp.dot(
                    a_buf[field(s, entry, 0)],
                    panel[field(s, entry, 1)],
                    preferred_element_type=jnp.float32,
                ).astype(jnp.bfloat16)
            return carry

        def far(group, carry):
            for u in range(UNROLL):
                n = group * UNROLL + u
                slots_ref[n] = a_buf[field(s, jnp.maximum(plan_ref[n], 0), 0)]
            return carry

        lax.fori_loop(begin, middle, near, 0)
        lax.fori_loop(middle, end, far, 0)


def make_products(s, plan, starts, a_pair, near):
    smem, vmem, hbm = (
        pl.BlockSpec(memory_space=space) for space in (pltpu.SMEM, pltpu.VMEM, pltpu.HBM)
    )
    anywhere = pl.BlockSpec(memory_space=pl.ANY)
    shapes = [((count, s.side, s.side), jnp.bfloat16) for count in (s.slots, s.near)]
    own = pltpu.with_memory_space_constraint(near[0], pltpu.HBM)
    return pl.pallas_call(
        functools.partial(product_kernel, s),
        in_specs=[smem, smem, vmem, hbm] + [anywhere] * (len(near) - 1),
        out_specs=vmem,
        out_shape=jax.ShapeDtypeStruct(*shapes[0]),
        scratch_shapes=[pltpu.VMEM(*shapes[1]), pltpu.SemaphoreType.DMA((len(near),))],
        compiler_params=pltpu.CompilerParams(vmem_limit_bytes=room(*shapes)),
        cost_estimate=pl.CostEstimate(
            flops=s.pairs * s.side**3, bytes_accessed=1 << 20, transcendentals=0
        ),
    )(plan, starts, a_pair, own, *near[1:])


def add_term(s, rows_ref, total, entry, product):
    known = jnp.maximum(entry, 0)
    term = jnp.dot(rows_ref[known & (s.slab - 1)], product, preferred_element_type=jnp.float32)
    cell = field(s, known, 2)
    at = pl.ds(pl.multiple_of((cell & (s.per - 1)) * s.side, s.side), s.side)
    total[cell >> log2(s.per), at, :] += jnp.where(entry >= 0, term, 0.0)


def sum_near(s, hi, plan_ref, starts_ref, slots_ref, rows_ref, total):
    def clear(k, carry):
        total[k] = jnp.zeros(total.shape[1:], jnp.float32)
        return carry

    def near(group, carry):
        for u in range(UNROLL):
            n = group * UNROLL + u
            add_term(s, rows_ref, total, plan_ref[n], slots_ref[n])
        return carry

    lax.fori_loop(0, s.blocks, clear, 0)
    lax.fori_loop(starts_ref[2 * hi] // UNROLL, starts_ref[2 * hi + 1] // UNROLL, near, 0)


def sum_kernel(s, plan_ref, starts_ref, slots_ref, rows_ref, far0, far1, *refs):
    if s.his == 1:
        hi, (total, *outs), (far_buf, sems) = 0, refs[1:-2], refs[-2:]
    else:
        hi, outs, (total, far_buf, sems) = pl.program_id(0), refs[:-3], refs[-3:]
    copies = [
        pltpu.make_async_copy(ref, far_buf.at[pl.ds(k * s.tiles, s.tiles)], sems.at[k])
        for k, ref in enumerate((far0, far1))
    ]

    @pl.when(hi == 0)
    def _():
        for copy in copies:
            copy.start()

    if s.his > 1:
        sum_near(s, hi, plan_ref, starts_ref, slots_ref, rows_ref, total)

    @pl.when(hi == 0)
    def _():
        for copy in copies:
            copy.wait()

    def far(group, carry):
        for u in range(UNROLL):
            n = group * UNROLL + u
            entry = plan_ref[n]
            piece = far_buf[field(s, jnp.maximum(entry, 0), 1)]
            product = jnp.dot(slots_ref[n], piece, preferred_element_type=jnp.float32)
            add_term(s, rows_ref, total, entry, product.astype(jnp.bfloat16))
        return carry

    middle = starts_ref[2 * hi + 1] // UNROLL
    lax.fori_loop(middle, starts_ref[2 * hi + 2] // UNROLL, far, 0)

    half = s.cols // 2
    weight = {"x": 1, "y": half, "1": 2 * half, "2": 4 * half}
    core = lax.axis_index("col") & 1
    for k, (send, keep) in enumerate(zip(outs[0::2], outs[1::2])):
        for bits in itertools.product(range(2), repeat=4):
            base = [
                sum(weight[link] * bit for link, bit in zip(order, bits)) for order in ORDERS[k]
            ]
            base = jnp.where(core == 0, *base)
            for x in range(half // 2):
                part = total[base + 2 * x, s.splits[k]:s.splits[k + 1], :]
                if bits[0]:
                    send[(*bits[1:], 0, x)] = part.astype(jnp.bfloat16)
                else:
                    keep[(*bits[1:], 0, x)] = part


def total_shape(s):
    return (s.blocks, s.tall, s.side), jnp.float32


def make_near_sums(s, plan, starts, slots, rows_t):
    smem = pl.BlockSpec(memory_space=pltpu.SMEM)
    vmem = pl.BlockSpec(memory_space=pltpu.VMEM)
    return pl.pallas_call(
        functools.partial(sum_near, s, 0),
        in_specs=[smem, smem, vmem, vmem],
        out_specs=vmem,
        out_shape=jax.ShapeDtypeStruct(*total_shape(s)),
        compiler_params=pltpu.CompilerParams(vmem_limit_bytes=room(total_shape(s))),
        cost_estimate=pl.CostEstimate(
            flops=s.pairs * s.side**3, bytes_accessed=1 << 20, transcendentals=0
        ),
    )(plan, starts, slots, rows_t)


def make_sums(s, plan, starts, slots, rows_t, far, total):
    smem = pl.BlockSpec(memory_space=pltpu.SMEM)
    vmem = pl.BlockSpec(memory_space=pltpu.VMEM)
    anywhere = pl.BlockSpec(memory_space=pl.ANY)
    shapes = [
        ((s.slots + s.slab + 2 * s.tiles, s.side, s.side), jnp.bfloat16),
        total_shape(s),
    ]
    in_specs = [smem, smem, vmem, vmem, anywhere, anywhere]
    out_shape, out_specs = [], []
    for k in range(len(ORDERS)):
        last = (s.cols // 4, s.splits[k + 1] - s.splits[k], s.side)
        for dtype in (jnp.bfloat16, jnp.float32):
            out_shape.append(jax.ShapeDtypeStruct((2, 2, 2, s.his) + last, dtype))
            out_specs.append(
                pl.BlockSpec((2, 2, 2, 1) + last, lambda h: (0, 0, 0, h, 0, 0, 0))
            )
            shapes.append(((2 if s.his > 1 else 1, 8) + last, dtype))
    scratch = [
        pltpu.VMEM((2 * s.tiles, s.side, s.side), jnp.bfloat16),
        pltpu.SemaphoreType.DMA((2,)),
    ]
    operands = [plan, starts, slots, rows_t, *far]
    aliases = {}
    if s.his == 1:
        aliases = {len(operands): 0}
        operands.append(total)
        in_specs.append(vmem)
        out_shape.insert(0, jax.ShapeDtypeStruct(*total_shape(s)))
        out_specs = [vmem] * len(out_shape)
    else:
        scratch.insert(0, pltpu.VMEM(*total_shape(s)))
    parts = pl.pallas_call(
        functools.partial(sum_kernel, s),
        grid=() if s.his == 1 else (s.his,),
        in_specs=in_specs,
        out_specs=out_specs,
        out_shape=out_shape,
        scratch_shapes=scratch,
        input_output_aliases=aliases,
        compiler_params=pltpu.CompilerParams(vmem_limit_bytes=room(*shapes)),
        cost_estimate=pl.CostEstimate(
            flops=s.pairs * s.side**3, bytes_accessed=16 << 20, transcendentals=0
        ),
    )(*operands)
    return parts[len(aliases):]


def shards(a_blocks, p_tiles, owner, agg_local, a_cols):
    s = Sizes(
        lax.axis_size("row"), lax.axis_size("col"), p_tiles.shape[0], p_tiles.shape[1]
    )
    order = ring_order(s.rows)
    barrier = lax.optimization_barrier

    def ring(value, stream):
        moves = []
        for k in range(s.rows):
            for c in range(s.cols):
                step = 1 if (stream + c) % 2 == 0 else -1
                to = order[(k + step) % s.rows]
                moves.append((order[k] * s.cols + c, to * s.cols + c))
        return lax.ppermute(value, ("row", "col"), moves)

    first = ring(p_tiles, 0)
    cols = a_cols[:, 0]
    cols_other = swap(cols, "col", 1)
    cols_other, mine = barrier((cols_other, p_tiles))
    second = ring(mine, 1)
    a_other, p_other = swap(a_blocks[:, 0], "col", 1), swap(p_tiles, "col", 1)

    aggs = owner[:, 0] * OWN + agg_local
    came, aggs, a_other, p_other = barrier((first, aggs, a_other, p_other))
    first = ring(first, 0)
    aggs = [aggs] + [swap(aggs, "row", mask) for mask in (1, 2, 3)]
    own_near, other_near = {0: p_tiles, s.rows - 1: came, 1: second}, {0: p_other}
    second = ring(second, 1)
    aggs, mine = barrier((jnp.concatenate(aggs, 0), p_tiles))
    bit = 4
    while bit < s.rows:
        aggs = jnp.concatenate([aggs, swap(aggs, "row", bit)], 0)
        bit *= 2
    rows = [mine]
    bit = 2
    while bit < s.cols:
        rows += [swap(piece, "col", bit) for piece in rows]
        bit *= 2
    plan, starts, a_pair = make_plan(
        s, jnp.concatenate([cols, cols_other], 0), aggs, a_blocks[:, 0], a_other
    )

    held = [1, s.rows - 1]
    for step in range(2, s.half - 1):
        came, *rest = barrier((second, *(own_near[away] for away in held), *rows[1:]))
        for away, piece in zip(held, rest):
            other_near[away] = swap(piece, "col", 1)
        if step == 2:
            rows += [p_other] + [swap(piece, "col", 1) for piece in rest[len(held):]]
        own_near[s.rows - step], own_near[step] = first, came
        first, second = ring(first, 0), ring(second, 1)
        held = [step, s.rows - step]

    others = sorted(set(other_near) - {0})
    rows_t = turn_rows(s, rows)
    tie = (first, second, plan, starts, rows_t, a_pair)
    tie += (*(own_near[away] for away in held), *(other_near[away] for away in others))
    first, second, plan, starts, rows_t, a_pair, *rest = barrier(tie)
    for away, piece in zip(others, rest[len(held):]):
        other_near[away] = piece
    far = ring(first, 0)
    own_near[s.half + 1], own_near[s.half - 1] = first, second
    for away, piece in zip(held, rest):
        other_near[away] = swap(piece, "col", 1)
    for away in (s.half + 1, s.half - 1):
        other_near[away] = swap(own_near[away], "col", 1)
    near = [own_near[k] for k in sorted(own_near)]
    near += [other_near[k] for k in sorted(other_near)]
    slots = make_products(s, plan, starts, a_pair, near)
    total = None
    if s.his == 1:
        total = make_near_sums(s, plan, starts, slots, rows_t)
        far, total = barrier((far, total))
    else:
        far, slots = barrier((far, slots))
    far_other = swap(far, "col", 1)
    parts = make_sums(s, plan, starts, slots, rows_t, [far, far_other], total)

    sends, keeps = list(parts[0::2]), list(parts[1::2])
    groups = range(len(ORDERS))
    moving = [exchange(sends[k], [order[0] for order in ORDERS[k]]) for k in groups]
    for step in range(1, 5):
        for k in groups:
            got = moving[k]
            if step < 4:
                send = (keeps[k][1] + got[1].astype(jnp.float32)).astype(jnp.bfloat16)
                moving[k] = exchange(send, [order[step] for order in ORDERS[k]])
                keeps[k] = keeps[k][0] + got[0].astype(jnp.float32)
            else:
                keeps[k] = keeps[k] + got.astype(jnp.float32)
    total = jnp.concatenate(keeps, -2)
    tail = [("row", 1 << k) for k in range(3, log2(s.rows))][::-1]
    tail += [("col", 1 << k) for k in range(2, log2(s.cols))][::-1]
    total = total.reshape((2,) * len(tail) + total.shape[-2:])
    for axis in tail:
        got = swap(total[1].astype(jnp.bfloat16), *axis)
        total = total[0] + got.astype(jnp.float32)
    return total.reshape(OWN, s.width, s.side, s.side)


def solution(mesh):
    in_specs = (
        P("row", "col", None, None),
        P(("row", "col"), None, None),
        P("row", None),
        P("row"),
        P("row", "col"),
    )
    out_specs = P("row", "col", None, None)
    return jax.shard_map(shards, mesh=mesh, in_specs=in_specs, out_specs=out_specs, check_vma=False)
```

```python
import functools
import itertools
import math

import jax
import jax.numpy as jnp
from jax import lax
from jax.experimental import pallas as pl
from jax.experimental.pallas import tpu as pltpu
from jax.sharding import PartitionSpec as P

OWN = 2
UNROLL = 8
ORDERS = (("yx12", "x1y2"), ("xy21", "12xy"), ("yx12", "2yx1"))
LINKS = {"x": ("col", 2), "y": ("row", 1), "1": ("row", 2), "2": ("row", 4)}


def ring_order(count):
    return list(range(0, count, 2)) + list(range(1, count, 2))[::-1]


def swap(value, axis, bit):
    size = lax.axis_size(axis)
    return lax.ppermute(value, axis, [(i, i ^ bit) for i in range(size)])


def exchange(value, links):
    rows, cols = lax.axis_size("row"), lax.axis_size("col")
    moves = []
    for r in range(rows):
        for c in range(cols):
            axis, bit = LINKS[links[c % 2]]
            to = (r ^ bit, c) if axis == "row" else (r, c ^ bit)
            moves.append((r * cols + c, to[0] * cols + to[1]))
    return lax.ppermute(value, ("row", "col"), moves)


def log2(size):
    power = size.bit_length() - 1
    assert size == 1 << power
    return power


class Sizes:
    def __init__(self, rows, cols, tiles, side):
        self.rows, self.cols, self.tiles, self.side = rows, cols, tiles, side
        self.slab = cols * tiles
        self.pairs = 2 * self.slab
        self.width = OWN * rows // cols
        self.per = OWN * self.width
        self.his = rows // 8
        self.blocks, self.tall = 4 * cols, self.per * side
        third = self.tall // 16 // 3 * 16
        self.splits = (0, third, 2 * third, self.tall)
        self.buckets = 2 * self.his
        self.slots = self.pairs + self.buckets * UNROLL
        self.half = rows // 2
        self.early = rows - 1
        self.near = 2 * self.early * tiles
        self.fields, shift = [], 0
        for size in (self.pairs, 2 * rows * tiles, self.blocks * self.per):
            self.fields.append((shift, size - 1))
            shift += log2(size)
        assert shift <= 31


def field(s, entry, k):
    shift, mask = s.fields[k]
    return (entry >> shift) & mask


def plan_kernel(
    s, cols_ref, aggs_ref, own_ref, other_ref, plan_ref, starts_ref, pair_ref, info, counts, sems
):
    copies = [
        pltpu.make_async_copy(ref, pair_ref.at[pl.ds(k * s.slab, s.slab)], sems.at[k])
        for k, ref in enumerate((own_ref, other_ref))
    ]
    for copy in copies:
        copy.start()
    row = lax.axis_index("row")
    col = lax.axis_index("col")

    def ring_place(index):
        return jnp.where((index & 1) == 0, index >> 1, s.rows - 1 - (index >> 1))

    here = ring_place(row)
    for b in range(s.buckets):
        counts[b] = 0

    def blank(k, carry):
        plan_ref[k] = -1
        return carry

    lax.fori_loop(0, s.slots + 1, blank, 0, unroll=8)

    def sort(i, carry):
        tile = i & (s.slab - 1)
        side = i >> log2(s.slab)
        other = cols_ref[i]
        other_row = other >> log2(s.slab)
        i_agg = aggs_ref[tile]
        j_agg = aggs_ref[((other_row ^ row) << log2(s.slab)) + (other & (s.slab - 1))]
        rel_col = (j_agg >> log2(s.width)) ^ col
        rel_row = (i_agg >> log2(OWN)) ^ row
        turn = ring_place(other_row) - here
        away = jnp.where(((col ^ side) & 1) == 0, turn, -turn) & (s.rows - 1)
        late = jnp.where(away == s.half, 1, 0)
        order = away - jnp.where(away > s.half, 1, 0) + side * s.early
        piece = jnp.where(late == 1, side, order)
        panel_at = (piece << log2(s.tiles)) + (other & (s.tiles - 1))
        cell = (rel_row & 7) * (s.cols // 2) + (rel_col >> 1)
        cell = (cell << log2(OWN)) + (i_agg & (OWN - 1))
        cell = (cell << log2(s.width)) + (j_agg & (s.width - 1))
        bucket = (rel_row >> 3) * 2 + late
        mine = (rel_col & 1) == 0
        rank = counts[bucket]
        counts[bucket] = rank + jnp.where(mine, 1, 0)
        info[i * 2] = jnp.where(mine, rank * s.buckets + bucket, -1)
        entry = i
        for k, value in enumerate((panel_at, cell)):
            entry = entry + (value << s.fields[k + 1][0])
        info[i * 2 + 1] = entry
        return carry

    lax.fori_loop(0, s.pairs, sort, 0, unroll=4)

    start = jnp.int32(0)
    for b in range(s.buckets):
        starts_ref[b] = start
        start = start + ((counts[b] + UNROLL - 1) & ~(UNROLL - 1))
    starts_ref[s.buckets] = start

    def place(i, carry):
        key = info[i * 2]
        slot = starts_ref[key & (s.buckets - 1)] + (key >> log2(s.buckets))
        plan_ref[jnp.where(key >= 0, slot, s.slots)] = info[i * 2 + 1]
        return carry

    lax.fori_loop(0, s.pairs, place, 0, unroll=4)
    for copy in copies:
        copy.wait()


def room(*shapes):
    total = sum(math.prod(shape) * jnp.dtype(dtype).itemsize for shape, dtype in shapes)
    return total + (2 << 20)


def make_plan(s, cols, aggs, a_own, a_other):
    smem, vmem, hbm = (
        pl.BlockSpec(memory_space=space) for space in (pltpu.SMEM, pltpu.VMEM, pltpu.HBM)
    )
    a_own = pltpu.with_memory_space_constraint(a_own, pltpu.HBM)
    pair_shape = ((s.pairs, s.side, s.side), jnp.bfloat16)
    return pl.pallas_call(
        functools.partial(plan_kernel, s),
        in_specs=[smem, smem, hbm, pl.BlockSpec(memory_space=pl.ANY)],
        out_specs=[smem, smem, vmem],
        out_shape=[
            jax.ShapeDtypeStruct((s.slots + 1,), jnp.int32),
            jax.ShapeDtypeStruct((s.buckets + 1,), jnp.int32),
            jax.ShapeDtypeStruct(*pair_shape),
        ],
        scratch_shapes=[
            pltpu.SMEM((s.pairs * 2,), jnp.int32),
            pltpu.SMEM((s.buckets,), jnp.int32),
            pltpu.SemaphoreType.DMA((2,)),
        ],
        compiler_params=pltpu.CompilerParams(vmem_limit_bytes=room(pair_shape)),
        cost_estimate=pl.CostEstimate(flops=1 << 20, bytes_accessed=16 << 20, transcendentals=0),
    )(cols, aggs, a_own, a_other)


def turn_kernel(s, *refs):
    rows_ref, rows_buf, sems = refs[-3:]
    copies = [
        pltpu.make_async_copy(refs[k], rows_buf.at[pl.ds(k * s.tiles, s.tiles)], sems.at[k])
        for k in range(s.cols)
    ]
    for copy in copies:
        copy.start()
    for copy in copies:
        copy.wait()
    col = lax.axis_index("col")

    def turn(k, carry):
        part = k >> log2(s.tiles)
        rel = (part & (s.cols // 2 - 1)) * 2 + (part >> log2(s.cols // 2))
        rows_ref[((rel ^ col) << log2(s.tiles)) + (k & (s.tiles - 1))] = rows_buf[k].T
        return carry

    lax.fori_loop(0, s.slab, turn, 0, unroll=4)


def turn_rows(s, rows):
    own = pltpu.with_memory_space_constraint(rows[0], pltpu.HBM)
    shape = ((s.slab, s.side, s.side), jnp.bfloat16)
    return pl.pallas_call(
        functools.partial(turn_kernel, s),
        in_specs=[pl.BlockSpec(memory_space=pltpu.HBM)]
        + [pl.BlockSpec(memory_space=pl.ANY)] * (s.cols - 1),
        out_specs=pl.BlockSpec(memory_space=pltpu.VMEM),
        out_shape=jax.ShapeDtypeStruct(*shape),
        scratch_shapes=[pltpu.VMEM(*shape), pltpu.SemaphoreType.DMA((s.cols,))],
        compiler_params=pltpu.CompilerParams(vmem_limit_bytes=room(shape, shape)),
        cost_estimate=pl.CostEstimate(flops=0, bytes_accessed=0, transcendentals=0),
    )(own, *rows[1:])


def product_kernel(s, plan_ref, starts_ref, a_buf, *refs):
    slots_ref, panel, sems = refs[-3:]
    copies = []
    for k in range(2 * s.early):
        copies.append((refs[k], panel.at[pl.ds(k * s.tiles, s.tiles)]))
    copies = [pltpu.make_async_copy(src, dst, sems.at[k]) for k, (src, dst) in enumerate(copies)]
    for copy in copies:
        copy.start()
    for copy in copies:
        copy.wait()

    for hi in range(s.his):
        begin = starts_ref[2 * hi] // UNROLL
        middle = starts_ref[2 * hi + 1] // UNROLL
        end = starts_ref[2 * hi + 2] // UNROLL

        def near(group, carry):
            for u in range(UNROLL):
                n = group * UNROLL + u
                entry = jnp.maximum(plan_ref[n], 0)
                slots_ref[n] = jnp.dot(
                    a_buf[field(s, entry, 0)],
                    panel[field(s, entry, 1)],
                    preferred_element_type=jnp.float32,
                ).astype(jnp.bfloat16)
            return carry

        def far(group, carry):
            for u in range(UNROLL):
                n = group * UNROLL + u
                slots_ref[n] = a_buf[field(s, jnp.maximum(plan_ref[n], 0), 0)]
            return carry

        lax.fori_loop(begin, middle, near, 0)
        lax.fori_loop(middle, end, far, 0)


def make_products(s, plan, starts, a_pair, near):
    smem, vmem, hbm = (
        pl.BlockSpec(memory_space=space) for space in (pltpu.SMEM, pltpu.VMEM, pltpu.HBM)
    )
    anywhere = pl.BlockSpec(memory_space=pl.ANY)
    shapes = [((count, s.side, s.side), jnp.bfloat16) for count in (s.slots, s.near)]
    own = pltpu.with_memory_space_constraint(near[0], pltpu.HBM)
    return pl.pallas_call(
        functools.partial(product_kernel, s),
        in_specs=[smem, smem, vmem, hbm] + [anywhere] * (len(near) - 1),
        out_specs=vmem,
        out_shape=jax.ShapeDtypeStruct(*shapes[0]),
        scratch_shapes=[pltpu.VMEM(*shapes[1]), pltpu.SemaphoreType.DMA((len(near),))],
        compiler_params=pltpu.CompilerParams(vmem_limit_bytes=room(*shapes)),
        cost_estimate=pl.CostEstimate(
            flops=s.pairs * s.side**3, bytes_accessed=1 << 20, transcendentals=0
        ),
    )(plan, starts, a_pair, own, *near[1:])


def add_term(s, rows_ref, total, entry, product):
    known = jnp.maximum(entry, 0)
    term = jnp.dot(rows_ref[known & (s.slab - 1)], product, preferred_element_type=jnp.float32)
    cell = field(s, known, 2)
    at = pl.ds(pl.multiple_of((cell & (s.per - 1)) * s.side, s.side), s.side)
    total[cell >> log2(s.per), at, :] += jnp.where(entry >= 0, term, 0.0)


def sum_near(s, hi, plan_ref, starts_ref, slots_ref, rows_ref, total):
    def clear(k, carry):
        total[k] = jnp.zeros(total.shape[1:], jnp.float32)
        return carry

    def near(group, carry):
        for u in range(UNROLL):
            n = group * UNROLL + u
            add_term(s, rows_ref, total, plan_ref[n], slots_ref[n])
        return carry

    lax.fori_loop(0, s.blocks, clear, 0)
    lax.fori_loop(starts_ref[2 * hi] // UNROLL, starts_ref[2 * hi + 1] // UNROLL, near, 0)


def sum_kernel(s, plan_ref, starts_ref, slots_ref, rows_ref, far0, far1, *refs):
    if s.his == 1:
        hi, (total, *outs), (far_buf, sems) = 0, refs[1:-2], refs[-2:]
    else:
        hi, outs, (total, far_buf, sems) = pl.program_id(0), refs[:-3], refs[-3:]
    copies = [
        pltpu.make_async_copy(ref, far_buf.at[pl.ds(k * s.tiles, s.tiles)], sems.at[k])
        for k, ref in enumerate((far0, far1))
    ]

    @pl.when(hi == 0)
    def _():
        for copy in copies:
            copy.start()

    if s.his > 1:
        sum_near(s, hi, plan_ref, starts_ref, slots_ref, rows_ref, total)

    @pl.when(hi == 0)
    def _():
        for copy in copies:
            copy.wait()

    def far(group, carry):
        for u in range(UNROLL):
            n = group * UNROLL + u
            entry = plan_ref[n]
            piece = far_buf[field(s, jnp.maximum(entry, 0), 1)]
            product = jnp.dot(slots_ref[n], piece, preferred_element_type=jnp.float32)
            add_term(s, rows_ref, total, entry, product.astype(jnp.bfloat16))
        return carry

    middle = starts_ref[2 * hi + 1] // UNROLL
    lax.fori_loop(middle, starts_ref[2 * hi + 2] // UNROLL, far, 0)

    half = s.cols // 2
    weight = {"x": 1, "y": half, "1": 2 * half, "2": 4 * half}
    core = lax.axis_index("col") & 1
    for k, (send, keep) in enumerate(zip(outs[0::2], outs[1::2])):
        for bits in itertools.product(range(2), repeat=4):
            base = [
                sum(weight[link] * bit for link, bit in zip(order, bits)) for order in ORDERS[k]
            ]
            base = jnp.where(core == 0, *base)
            for x in range(half // 2):
                part = total[base + 2 * x, s.splits[k]:s.splits[k + 1], :]
                if bits[0]:
                    send[(*bits[1:], 0, x)] = part.astype(jnp.bfloat16)
                else:
                    keep[(*bits[1:], 0, x)] = part


def total_shape(s):
    return (s.blocks, s.tall, s.side), jnp.float32


def make_near_sums(s, plan, starts, slots, rows_t):
    smem = pl.BlockSpec(memory_space=pltpu.SMEM)
    vmem = pl.BlockSpec(memory_space=pltpu.VMEM)
    return pl.pallas_call(
        functools.partial(sum_near, s, 0),
        in_specs=[smem, smem, vmem, vmem],
        out_specs=vmem,
        out_shape=jax.ShapeDtypeStruct(*total_shape(s)),
        compiler_params=pltpu.CompilerParams(vmem_limit_bytes=room(total_shape(s))),
        cost_estimate=pl.CostEstimate(
            flops=s.pairs * s.side**3, bytes_accessed=1 << 20, transcendentals=0
        ),
    )(plan, starts, slots, rows_t)


def make_sums(s, plan, starts, slots, rows_t, far, total):
    smem = pl.BlockSpec(memory_space=pltpu.SMEM)
    vmem = pl.BlockSpec(memory_space=pltpu.VMEM)
    anywhere = pl.BlockSpec(memory_space=pl.ANY)
    shapes = [
        ((s.slots + s.slab + 2 * s.tiles, s.side, s.side), jnp.bfloat16),
        total_shape(s),
    ]
    in_specs = [smem, smem, vmem, vmem, anywhere, anywhere]
    out_shape, out_specs = [], []
    for k in range(len(ORDERS)):
        last = (s.cols // 4, s.splits[k + 1] - s.splits[k], s.side)
        for dtype in (jnp.bfloat16, jnp.float32):
            out_shape.append(jax.ShapeDtypeStruct((2, 2, 2, s.his) + last, dtype))
            out_specs.append(
                pl.BlockSpec((2, 2, 2, 1) + last, lambda h: (0, 0, 0, h, 0, 0, 0))
            )
            shapes.append(((2 if s.his > 1 else 1, 8) + last, dtype))
    scratch = [
        pltpu.VMEM((2 * s.tiles, s.side, s.side), jnp.bfloat16),
        pltpu.SemaphoreType.DMA((2,)),
    ]
    operands = [plan, starts, slots, rows_t, *far]
    aliases = {}
    if s.his == 1:
        aliases = {len(operands): 0}
        operands.append(total)
        in_specs.append(vmem)
        out_shape.insert(0, jax.ShapeDtypeStruct(*total_shape(s)))
        out_specs = [vmem] * len(out_shape)
    else:
        scratch.insert(0, pltpu.VMEM(*total_shape(s)))
    parts = pl.pallas_call(
        functools.partial(sum_kernel, s),
        grid=() if s.his == 1 else (s.his,),
        in_specs=in_specs,
        out_specs=out_specs,
        out_shape=out_shape,
        scratch_shapes=scratch,
        input_output_aliases=aliases,
        compiler_params=pltpu.CompilerParams(vmem_limit_bytes=room(*shapes)),
        cost_estimate=pl.CostEstimate(
            flops=s.pairs * s.side**3, bytes_accessed=16 << 20, transcendentals=0
        ),
    )(*operands)
    return parts[len(aliases):]


def shards(a_blocks, p_tiles, owner, agg_local, a_cols):
    s = Sizes(
        lax.axis_size("row"), lax.axis_size("col"), p_tiles.shape[0], p_tiles.shape[1]
    )
    order = ring_order(s.rows)
    barrier = lax.optimization_barrier

    def ring(value, stream):
        moves = []
        for k in range(s.rows):
            for c in range(s.cols):
                step = 1 if (stream + c) % 2 == 0 else -1
                to = order[(k + step) % s.rows]
                moves.append((order[k] * s.cols + c, to * s.cols + c))
        return lax.ppermute(value, ("row", "col"), moves)

    first = ring(p_tiles, 0)
    cols = a_cols[:, 0]
    cols_other = swap(cols, "col", 1)
    cols_other, mine = barrier((cols_other, p_tiles))
    second = ring(mine, 1)
    a_other, p_other = swap(a_blocks[:, 0], "col", 1), swap(p_tiles, "col", 1)

    aggs = owner[:, 0] * OWN + agg_local
    came, aggs, a_other, p_other = barrier((first, aggs, a_other, p_other))
    first = ring(first, 0)
    aggs = [aggs] + [swap(aggs, "row", mask) for mask in (1, 2, 3)]
    own_near, other_near = {0: p_tiles, s.rows - 1: came, 1: second}, {0: p_other}
    second = ring(second, 1)
    aggs, mine = barrier((jnp.concatenate(aggs, 0), p_tiles))
    bit = 4
    while bit < s.rows:
        aggs = jnp.concatenate([aggs, swap(aggs, "row", bit)], 0)
        bit *= 2
    rows = [mine]
    bit = 2
    while bit < s.cols:
        rows += [swap(piece, "col", bit) for piece in rows]
        bit *= 2
    plan, starts, a_pair = make_plan(
        s, jnp.concatenate([cols, cols_other], 0), aggs, a_blocks[:, 0], a_other
    )

    held = [1, s.rows - 1]
    for step in range(2, s.half - 1):
        came, *rest = barrier((second, *(own_near[away] for away in held), *rows[1:]))
        for away, piece in zip(held, rest):
            other_near[away] = swap(piece, "col", 1)
        if step == 2:
            rows += [p_other] + [swap(piece, "col", 1) for piece in rest[len(held):]]
        own_near[s.rows - step], own_near[step] = first, came
        first, second = ring(first, 0), ring(second, 1)
        held = [step, s.rows - step]

    others = sorted(set(other_near) - {0})
    rows_t = turn_rows(s, rows)
    tie = (first, second, plan, starts, rows_t, a_pair)
    tie += (*(own_near[away] for away in held), *(other_near[away] for away in others))
    first, second, plan, starts, rows_t, a_pair, *rest = barrier(tie)
    for away, piece in zip(others, rest[len(held):]):
        other_near[away] = piece
    far = ring(first, 0)
    own_near[s.half + 1], own_near[s.half - 1] = first, second
    for away, piece in zip(held, rest):
        other_near[away] = swap(piece, "col", 1)
    for away in (s.half + 1, s.half - 1):
        other_near[away] = swap(own_near[away], "col", 1)
    near = [own_near[k] for k in sorted(own_near)]
    near += [other_near[k] for k in sorted(other_near)]
    slots = make_products(s, plan, starts, a_pair, near)
    total = None
    if s.his == 1:
        total = make_near_sums(s, plan, starts, slots, rows_t)
        far, total = barrier((far, total))
    else:
        far, slots = barrier((far, slots))
    far_other = swap(far, "col", 1)
    parts = make_sums(s, plan, starts, slots, rows_t, [far, far_other], total)

    sends, keeps = list(parts[0::2]), list(parts[1::2])
    groups = range(len(ORDERS))
    moving = [exchange(sends[k], [order[0] for order in ORDERS[k]]) for k in groups]
    for step in range(1, 5):
        for k in groups:
            got = moving[k]
            if step < 4:
                send = (keeps[k][1] + got[1].astype(jnp.float32)).astype(jnp.bfloat16)
                moving[k] = exchange(send, [order[step] for order in ORDERS[k]])
                keeps[k] = keeps[k][0] + got[0].astype(jnp.float32)
            else:
                keeps[k] = keeps[k] + got.astype(jnp.float32)
    total = jnp.concatenate(keeps, -2)
    tail = [("row", 1 << k) for k in range(3, log2(s.rows))][::-1]
    tail += [("col", 1 << k) for k in range(2, log2(s.cols))][::-1]
    total = total.reshape((2,) * len(tail) + total.shape[-2:])
    for axis in tail:
        got = swap(total[1].astype(jnp.bfloat16), *axis)
        total = total[0] + got.astype(jnp.float32)
    return total.reshape(OWN, s.width, s.side, s.side)


def solution(mesh):
    in_specs = (
        P("row", "col", None, None),
        P(("row", "col"), None, None),
        P("row", None),
        P("row"),
        P("row", "col"),
    )
    out_specs = P("row", "col", None, None)
    return jax.shard_map(shards, mesh=mesh, in_specs=in_specs, out_specs=out_specs, check_vma=False)
```

```python
import functools
import itertools
import math

import jax
import jax.numpy as jnp
from jax import lax
from jax.experimental import pallas as pl
from jax.experimental.pallas import tpu as pltpu
from jax.sharding import PartitionSpec as P

OWN = 2
UNROLL = 8
ORDERS = (("xy12", "yx12"), ("y12x", "1xy2"), ("xy12", "2xy1"))
LINKS = {"x": ("col", 2), "y": ("row", 1), "1": ("row", 2), "2": ("row", 4)}


def ring_order(count):
    return list(range(0, count, 2)) + list(range(1, count, 2))[::-1]


def swap(value, axis, bit):
    size = lax.axis_size(axis)
    return lax.ppermute(value, axis, [(i, i ^ bit) for i in range(size)])


def exchange(value, links):
    rows, cols = lax.axis_size("row"), lax.axis_size("col")
    moves = []
    for r in range(rows):
        for c in range(cols):
            axis, bit = LINKS[links[c % 2]]
            to = (r ^ bit, c) if axis == "row" else (r, c ^ bit)
            moves.append((r * cols + c, to[0] * cols + to[1]))
    return lax.ppermute(value, ("row", "col"), moves)


def log2(size):
    power = size.bit_length() - 1
    assert size == 1 << power
    return power


class Sizes:
    def __init__(self, rows, cols, tiles, side):
        self.rows, self.cols, self.tiles, self.side = rows, cols, tiles, side
        self.slab = cols * tiles
        self.pairs = 2 * self.slab
        self.width = OWN * rows // cols
        self.per = OWN * self.width
        self.his = rows // 8
        self.blocks, self.tall = 4 * cols, self.per * side
        third = self.tall // 16 // 3 * 16
        self.splits = (0, third, 2 * third, self.tall)
        self.buckets = 2 * self.his
        self.slots = self.pairs + self.buckets * UNROLL
        self.half = rows // 2
        self.early = rows - 1
        self.near = 2 * self.early * tiles
        self.fields, shift = [], 0
        for size in (self.pairs, 2 * rows * tiles, self.blocks * self.per):
            self.fields.append((shift, size - 1))
            shift += log2(size)
        assert shift <= 31


def field(s, entry, k):
    shift, mask = s.fields[k]
    return (entry >> shift) & mask


def plan_kernel(
    s, cols_ref, aggs_ref, own_ref, other_ref, plan_ref, starts_ref, pair_ref, info, counts, sems
):
    copies = [
        pltpu.make_async_copy(ref, pair_ref.at[pl.ds(k * s.slab, s.slab)], sems.at[k])
        for k, ref in enumerate((own_ref, other_ref))
    ]
    for copy in copies:
        copy.start()
    row = lax.axis_index("row")
    col = lax.axis_index("col")

    def ring_place(index):
        return jnp.where((index & 1) == 0, index >> 1, s.rows - 1 - (index >> 1))

    here = ring_place(row)
    for b in range(s.buckets):
        counts[b] = 0

    def blank(k, carry):
        plan_ref[k] = -1
        return carry

    lax.fori_loop(0, s.slots + 1, blank, 0, unroll=8)

    def sort(i, carry):
        tile = i & (s.slab - 1)
        side = i >> log2(s.slab)
        other = cols_ref[i]
        other_row = other >> log2(s.slab)
        i_agg = aggs_ref[tile]
        j_agg = aggs_ref[((other_row ^ row) << log2(s.slab)) + (other & (s.slab - 1))]
        rel_col = (j_agg >> log2(s.width)) ^ col
        rel_row = (i_agg >> log2(OWN)) ^ row
        turn = ring_place(other_row) - here
        away = jnp.where(((col ^ side) & 1) == 0, turn, -turn) & (s.rows - 1)
        late = jnp.where(away == s.half, 1, 0)
        order = away - jnp.where(away > s.half, 1, 0) + side * s.early
        piece = jnp.where(late == 1, side, order)
        panel_at = (piece << log2(s.tiles)) + (other & (s.tiles - 1))
        cell = (rel_row & 7) * (s.cols // 2) + (rel_col >> 1)
        cell = (cell << log2(OWN)) + (i_agg & (OWN - 1))
        cell = (cell << log2(s.width)) + (j_agg & (s.width - 1))
        bucket = (rel_row >> 3) * 2 + late
        mine = (rel_col & 1) == 0
        rank = counts[bucket]
        counts[bucket] = rank + jnp.where(mine, 1, 0)
        info[i * 2] = jnp.where(mine, rank * s.buckets + bucket, -1)
        entry = i
        for k, value in enumerate((panel_at, cell)):
            entry = entry + (value << s.fields[k + 1][0])
        info[i * 2 + 1] = entry
        return carry

    lax.fori_loop(0, s.pairs, sort, 0, unroll=4)

    start = jnp.int32(0)
    for b in range(s.buckets):
        starts_ref[b] = start
        start = start + ((counts[b] + UNROLL - 1) & ~(UNROLL - 1))
    starts_ref[s.buckets] = start

    def place(i, carry):
        key = info[i * 2]
        slot = starts_ref[key & (s.buckets - 1)] + (key >> log2(s.buckets))
        plan_ref[jnp.where(key >= 0, slot, s.slots)] = info[i * 2 + 1]
        return carry

    lax.fori_loop(0, s.pairs, place, 0, unroll=4)
    for copy in copies:
        copy.wait()


def room(*shapes):
    total = sum(math.prod(shape) * jnp.dtype(dtype).itemsize for shape, dtype in shapes)
    return total + (2 << 20)


def make_plan(s, cols, aggs, a_own, a_other):
    smem, vmem, hbm = (
        pl.BlockSpec(memory_space=space) for space in (pltpu.SMEM, pltpu.VMEM, pltpu.HBM)
    )
    a_own = pltpu.with_memory_space_constraint(a_own, pltpu.HBM)
    pair_shape = ((s.pairs, s.side, s.side), jnp.bfloat16)
    return pl.pallas_call(
        functools.partial(plan_kernel, s),
        in_specs=[smem, smem, hbm, pl.BlockSpec(memory_space=pl.ANY)],
        out_specs=[smem, smem, vmem],
        out_shape=[
            jax.ShapeDtypeStruct((s.slots + 1,), jnp.int32),
            jax.ShapeDtypeStruct((s.buckets + 1,), jnp.int32),
            jax.ShapeDtypeStruct(*pair_shape),
        ],
        scratch_shapes=[
            pltpu.SMEM((s.pairs * 2,), jnp.int32),
            pltpu.SMEM((s.buckets,), jnp.int32),
            pltpu.SemaphoreType.DMA((2,)),
        ],
        compiler_params=pltpu.CompilerParams(vmem_limit_bytes=room(pair_shape)),
        cost_estimate=pl.CostEstimate(flops=1 << 20, bytes_accessed=16 << 20, transcendentals=0),
    )(cols, aggs, a_own, a_other)


def turn_kernel(s, *refs):
    rows_ref, rows_buf, sems = refs[-3:]
    copies = [
        pltpu.make_async_copy(refs[k], rows_buf.at[pl.ds(k * s.tiles, s.tiles)], sems.at[k])
        for k in range(s.cols)
    ]
    for copy in copies:
        copy.start()
    for copy in copies:
        copy.wait()
    col = lax.axis_index("col")

    def turn(k, carry):
        part = k >> log2(s.tiles)
        rel = (part & (s.cols // 2 - 1)) * 2 + (part >> log2(s.cols // 2))
        rows_ref[((rel ^ col) << log2(s.tiles)) + (k & (s.tiles - 1))] = rows_buf[k].T
        return carry

    lax.fori_loop(0, s.slab, turn, 0, unroll=4)


def turn_rows(s, rows):
    own = pltpu.with_memory_space_constraint(rows[0], pltpu.HBM)
    shape = ((s.slab, s.side, s.side), jnp.bfloat16)
    return pl.pallas_call(
        functools.partial(turn_kernel, s),
        in_specs=[pl.BlockSpec(memory_space=pltpu.HBM)]
        + [pl.BlockSpec(memory_space=pl.ANY)] * (s.cols - 1),
        out_specs=pl.BlockSpec(memory_space=pltpu.VMEM),
        out_shape=jax.ShapeDtypeStruct(*shape),
        scratch_shapes=[pltpu.VMEM(*shape), pltpu.SemaphoreType.DMA((s.cols,))],
        compiler_params=pltpu.CompilerParams(vmem_limit_bytes=room(shape, shape)),
        cost_estimate=pl.CostEstimate(flops=0, bytes_accessed=0, transcendentals=0),
    )(own, *rows[1:])


def product_kernel(s, plan_ref, starts_ref, a_buf, *refs):
    slots_ref, panel, sems = refs[-3:]
    copies = []
    for k in range(2 * s.early):
        copies.append((refs[k], panel.at[pl.ds(k * s.tiles, s.tiles)]))
    copies = [pltpu.make_async_copy(src, dst, sems.at[k]) for k, (src, dst) in enumerate(copies)]
    for copy in copies:
        copy.start()
    for copy in copies:
        copy.wait()

    for hi in range(s.his):
        begin = starts_ref[2 * hi] // UNROLL
        middle = starts_ref[2 * hi + 1] // UNROLL
        end = starts_ref[2 * hi + 2] // UNROLL

        def near(group, carry):
            for u in range(UNROLL):
                n = group * UNROLL + u
                entry = jnp.maximum(plan_ref[n], 0)
                slots_ref[n] = jnp.dot(
                    a_buf[field(s, entry, 0)],
                    panel[field(s, entry, 1)],
                    preferred_element_type=jnp.float32,
                ).astype(jnp.bfloat16)
            return carry

        def far(group, carry):
            for u in range(UNROLL):
                n = group * UNROLL + u
                slots_ref[n] = a_buf[field(s, jnp.maximum(plan_ref[n], 0), 0)]
            return carry

        lax.fori_loop(begin, middle, near, 0)
        lax.fori_loop(middle, end, far, 0)


def make_products(s, plan, starts, a_pair, near):
    smem, vmem, hbm = (
        pl.BlockSpec(memory_space=space) for space in (pltpu.SMEM, pltpu.VMEM, pltpu.HBM)
    )
    anywhere = pl.BlockSpec(memory_space=pl.ANY)
    shapes = [((count, s.side, s.side), jnp.bfloat16) for count in (s.slots, s.near)]
    own = pltpu.with_memory_space_constraint(near[0], pltpu.HBM)
    return pl.pallas_call(
        functools.partial(product_kernel, s),
        in_specs=[smem, smem, vmem, hbm] + [anywhere] * (len(near) - 1),
        out_specs=vmem,
        out_shape=jax.ShapeDtypeStruct(*shapes[0]),
        scratch_shapes=[pltpu.VMEM(*shapes[1]), pltpu.SemaphoreType.DMA((len(near),))],
        compiler_params=pltpu.CompilerParams(vmem_limit_bytes=room(*shapes)),
        cost_estimate=pl.CostEstimate(
            flops=s.pairs * s.side**3, bytes_accessed=1 << 20, transcendentals=0
        ),
    )(plan, starts, a_pair, own, *near[1:])


def add_term(s, rows_ref, total, entry, product):
    known = jnp.maximum(entry, 0)
    term = jnp.dot(rows_ref[known & (s.slab - 1)], product, preferred_element_type=jnp.float32)
    cell = field(s, known, 2)
    at = pl.ds(pl.multiple_of((cell & (s.per - 1)) * s.side, s.side), s.side)
    total[cell >> log2(s.per), at, :] += jnp.where(entry >= 0, term, 0.0)


def sum_near(s, hi, plan_ref, starts_ref, slots_ref, rows_ref, total):
    def clear(k, carry):
        total[k] = jnp.zeros(total.shape[1:], jnp.float32)
        return carry

    def near(group, carry):
        for u in range(UNROLL):
            n = group * UNROLL + u
            add_term(s, rows_ref, total, plan_ref[n], slots_ref[n])
        return carry

    lax.fori_loop(0, s.blocks, clear, 0)
    lax.fori_loop(starts_ref[2 * hi] // UNROLL, starts_ref[2 * hi + 1] // UNROLL, near, 0)


def sum_kernel(s, plan_ref, starts_ref, slots_ref, rows_ref, far0, far1, *refs):
    if s.his == 1:
        hi, (total, *outs), (far_buf, sems) = 0, refs[1:-2], refs[-2:]
    else:
        hi, outs, (total, far_buf, sems) = pl.program_id(0), refs[:-3], refs[-3:]
    copies = [
        pltpu.make_async_copy(ref, far_buf.at[pl.ds(k * s.tiles, s.tiles)], sems.at[k])
        for k, ref in enumerate((far0, far1))
    ]

    @pl.when(hi == 0)
    def _():
        for copy in copies:
            copy.start()

    if s.his > 1:
        sum_near(s, hi, plan_ref, starts_ref, slots_ref, rows_ref, total)

    @pl.when(hi == 0)
    def _():
        for copy in copies:
            copy.wait()

    def far(group, carry):
        for u in range(UNROLL):
            n = group * UNROLL + u
            entry = plan_ref[n]
            piece = far_buf[field(s, jnp.maximum(entry, 0), 1)]
            product = jnp.dot(slots_ref[n], piece, preferred_element_type=jnp.float32)
            add_term(s, rows_ref, total, entry, product.astype(jnp.bfloat16))
        return carry

    middle = starts_ref[2 * hi + 1] // UNROLL
    lax.fori_loop(middle, starts_ref[2 * hi + 2] // UNROLL, far, 0)

    half = s.cols // 2
    weight = {"x": 1, "y": half, "1": 2 * half, "2": 4 * half}
    core = lax.axis_index("col") & 1
    for k, (send, keep) in enumerate(zip(outs[0::2], outs[1::2])):
        for bits in itertools.product(range(2), repeat=4):
            base = [
                sum(weight[link] * bit for link, bit in zip(order, bits)) for order in ORDERS[k]
            ]
            base = jnp.where(core == 0, *base)
            for x in range(half // 2):
                part = total[base + 2 * x, s.splits[k]:s.splits[k + 1], :]
                if bits[0]:
                    send[(*bits[1:], 0, x)] = part.astype(jnp.bfloat16)
                else:
                    keep[(*bits[1:], 0, x)] = part


def total_shape(s):
    return (s.blocks, s.tall, s.side), jnp.float32


def make_near_sums(s, plan, starts, slots, rows_t):
    smem = pl.BlockSpec(memory_space=pltpu.SMEM)
    vmem = pl.BlockSpec(memory_space=pltpu.VMEM)
    return pl.pallas_call(
        functools.partial(sum_near, s, 0),
        in_specs=[smem, smem, vmem, vmem],
        out_specs=vmem,
        out_shape=jax.ShapeDtypeStruct(*total_shape(s)),
        compiler_params=pltpu.CompilerParams(vmem_limit_bytes=room(total_shape(s))),
        cost_estimate=pl.CostEstimate(
            flops=s.pairs * s.side**3, bytes_accessed=1 << 20, transcendentals=0
        ),
    )(plan, starts, slots, rows_t)


def make_sums(s, plan, starts, slots, rows_t, far, total):
    smem = pl.BlockSpec(memory_space=pltpu.SMEM)
    vmem = pl.BlockSpec(memory_space=pltpu.VMEM)
    anywhere = pl.BlockSpec(memory_space=pl.ANY)
    shapes = [
        ((s.slots + s.slab + 2 * s.tiles, s.side, s.side), jnp.bfloat16),
        total_shape(s),
    ]
    in_specs = [smem, smem, vmem, vmem, anywhere, anywhere]
    out_shape, out_specs = [], []
    for k in range(len(ORDERS)):
        last = (s.cols // 4, s.splits[k + 1] - s.splits[k], s.side)
        for dtype in (jnp.bfloat16, jnp.float32):
            out_shape.append(jax.ShapeDtypeStruct((2, 2, 2, s.his) + last, dtype))
            out_specs.append(
                pl.BlockSpec((2, 2, 2, 1) + last, lambda h: (0, 0, 0, h, 0, 0, 0))
            )
            shapes.append(((2 if s.his > 1 else 1, 8) + last, dtype))
    scratch = [
        pltpu.VMEM((2 * s.tiles, s.side, s.side), jnp.bfloat16),
        pltpu.SemaphoreType.DMA((2,)),
    ]
    operands = [plan, starts, slots, rows_t, *far]
    aliases = {}
    if s.his == 1:
        aliases = {len(operands): 0}
        operands.append(total)
        in_specs.append(vmem)
        out_shape.insert(0, jax.ShapeDtypeStruct(*total_shape(s)))
        out_specs = [vmem] * len(out_shape)
    else:
        scratch.insert(0, pltpu.VMEM(*total_shape(s)))
    parts = pl.pallas_call(
        functools.partial(sum_kernel, s),
        grid=() if s.his == 1 else (s.his,),
        in_specs=in_specs,
        out_specs=out_specs,
        out_shape=out_shape,
        scratch_shapes=scratch,
        input_output_aliases=aliases,
        compiler_params=pltpu.CompilerParams(vmem_limit_bytes=room(*shapes)),
        cost_estimate=pl.CostEstimate(
            flops=s.pairs * s.side**3, bytes_accessed=16 << 20, transcendentals=0
        ),
    )(*operands)
    return parts[len(aliases):]


def shards(a_blocks, p_tiles, owner, agg_local, a_cols):
    s = Sizes(
        lax.axis_size("row"), lax.axis_size("col"), p_tiles.shape[0], p_tiles.shape[1]
    )
    order = ring_order(s.rows)
    barrier = lax.optimization_barrier

    def ring(value, stream):
        moves = []
        for k in range(s.rows):
            for c in range(s.cols):
                step = 1 if (stream + c) % 2 == 0 else -1
                to = order[(k + step) % s.rows]
                moves.append((order[k] * s.cols + c, to * s.cols + c))
        return lax.ppermute(value, ("row", "col"), moves)

    first = ring(p_tiles, 0)
    cols = a_cols[:, 0]
    cols_other = swap(cols, "col", 1)
    cols_other, mine = barrier((cols_other, p_tiles))
    second = ring(mine, 1)
    a_other, p_other = swap(a_blocks[:, 0], "col", 1), swap(p_tiles, "col", 1)

    aggs = owner[:, 0] * OWN + agg_local
    came, aggs, a_other, p_other = barrier((first, aggs, a_other, p_other))
    first = ring(first, 0)
    aggs = [aggs] + [swap(aggs, "row", mask) for mask in (1, 2, 3)]
    own_near, other_near = {0: p_tiles, s.rows - 1: came, 1: second}, {0: p_other}
    second = ring(second, 1)
    aggs, mine = barrier((jnp.concatenate(aggs, 0), p_tiles))
    bit = 4
    while bit < s.rows:
        aggs = jnp.concatenate([aggs, swap(aggs, "row", bit)], 0)
        bit *= 2
    rows = [mine]
    bit = 2
    while bit < s.cols:
        rows += [swap(piece, "col", bit) for piece in rows]
        bit *= 2
    plan, starts, a_pair = make_plan(
        s, jnp.concatenate([cols, cols_other], 0), aggs, a_blocks[:, 0], a_other
    )

    held = [1, s.rows - 1]
    for step in range(2, s.half - 1):
        came, *rest = barrier((second, *(own_near[away] for away in held), *rows[1:]))
        for away, piece in zip(held, rest):
            other_near[away] = swap(piece, "col", 1)
        if step == 2:
            rows += [p_other] + [swap(piece, "col", 1) for piece in rest[len(held):]]
        own_near[s.rows - step], own_near[step] = first, came
        first, second = ring(first, 0), ring(second, 1)
        held = [step, s.rows - step]

    others = sorted(set(other_near) - {0})
    rows_t = turn_rows(s, rows)
    tie = (first, second, plan, starts, rows_t, a_pair)
    tie += (*(own_near[away] for away in held), *(other_near[away] for away in others))
    first, second, plan, starts, rows_t, a_pair, *rest = barrier(tie)
    for away, piece in zip(others, rest[len(held):]):
        other_near[away] = piece
    far = ring(first, 0)
    own_near[s.half + 1], own_near[s.half - 1] = first, second
    for away, piece in zip(held, rest):
        other_near[away] = swap(piece, "col", 1)
    for away in (s.half + 1, s.half - 1):
        other_near[away] = swap(own_near[away], "col", 1)
    near = [own_near[k] for k in sorted(own_near)]
    near += [other_near[k] for k in sorted(other_near)]
    slots = make_products(s, plan, starts, a_pair, near)
    total = None
    if s.his == 1:
        total = make_near_sums(s, plan, starts, slots, rows_t)
        far, total = barrier((far, total))
    else:
        far, slots = barrier((far, slots))
    far_other = swap(far, "col", 1)
    parts = make_sums(s, plan, starts, slots, rows_t, [far, far_other], total)

    sends, keeps = list(parts[0::2]), list(parts[1::2])
    groups = range(len(ORDERS))
    moving = [exchange(sends[k], [order[0] for order in ORDERS[k]]) for k in groups]
    for step in range(1, 5):
        for k in groups:
            got = moving[k]
            if step < 4:
                send = (keeps[k][1] + got[1].astype(jnp.float32)).astype(jnp.bfloat16)
                moving[k] = exchange(send, [order[step] for order in ORDERS[k]])
                keeps[k] = keeps[k][0] + got[0].astype(jnp.float32)
            else:
                keeps[k] = keeps[k] + got.astype(jnp.float32)
    total = jnp.concatenate(keeps, -2)
    tail = [("row", 1 << k) for k in range(3, log2(s.rows))][::-1]
    tail += [("col", 1 << k) for k in range(2, log2(s.cols))][::-1]
    total = total.reshape((2,) * len(tail) + total.shape[-2:])
    for axis in tail:
        got = swap(total[1].astype(jnp.bfloat16), *axis)
        total = total[0] + got.astype(jnp.float32)
    return total.reshape(OWN, s.width, s.side, s.side)


def solution(mesh):
    in_specs = (
        P("row", "col", None, None),
        P(("row", "col"), None, None),
        P("row", None),
        P("row"),
        P("row", "col"),
    )
    out_specs = P("row", "col", None, None)
    return jax.shard_map(shards, mesh=mesh, in_specs=in_specs, out_specs=out_specs, check_vma=False)
```
